128 devices in a mesh: inner: 16 (over x_hi, y, core), outer: 8 (over x_lo, z).
Axes of the slice: x: 4 (x_hi: 2, x_lo: 2; x = x_hi * 2 + x_lo), y: 4, z: 4, core: 2. Of those that a mesh axis runs over, the one named last changes fastest.
Arguments:
- hidden_in: bfloat16 [16384, 4096], P(('inner', 'outer')), may hold values from -6 to 6
- queries: bfloat16 [16384, 2048], P(('inner', 'outer')), may hold values from -6 to 6
- keys: bfloat16 [16384, 512], P(('inner', 'outer')), may hold values from -6 to 6
- values: bfloat16 [16384, 512], P(('inner', 'outer')), may hold values from -6 to 6
- attention_output: bfloat16 [16384, 2048], P(('inner', 'outer')), may hold values from -6 to 6
- output_gradient: bfloat16 [16384, 2048], P(('inner', 'outer')), may hold values from -6 to 6
- log_softmax_total: float32 [16384, 16], P(('inner', 'outer')), may hold values from 0 to 20
- positions: int32 [16384], P(('inner', 'outer')), may hold values from 0 to 16383, as said below
Outputs:
- grad_queries: bfloat16 [16384, 2048], P(('inner', 'outer'))
- grad_wk: float32 [4096, 512], replicated
- grad_wv: float32 [4096, 512], replicated
The draws below stay inside these ranges and needn't reach their ends.
Inputs may be any that keep to these rules, and one draw needn't show every extreme that they name: Each device's 128 rows form two runs of 64 consecutive positions, each starting at a multiple of 64; every position occurs once.
All inputs are finite; a program needn't handle non-finite values.
Results may differ from the reference program's by a relative error of at most 0.0052.
Values may be sent and summed in bfloat16 or wider, within the bound.
A program may use at most 320 MiB of HBM per device.

```python
import jax
import jax.numpy as jnp
from jax import lax

D = 4096
QUERY_HEADS = 16
KEY_VALUE_HEADS = 4
HEAD_SIZE = 128
SEQUENCE_TOKENS = 16384
BLK = 64


def block_positions(key):
    block_count = SEQUENCE_TOKENS // BLK
    order = jax.random.permutation(key, block_count)
    token_rows = jnp.arange(SEQUENCE_TOKENS)
    return (order[token_rows // BLK] * BLK + token_rows % BLK).astype(jnp.int32)


def draw_positions(key, part):
    return block_positions(key)


def draw_log_softmax_total(key, part):
    where = block_positions(key).astype(jnp.float32)
    key = jax.random.fold_in(key, 7)
    offset = jax.random.uniform(key, (SEQUENCE_TOKENS, QUERY_HEADS), jnp.float32, 0.5, 1.5)
    return jnp.log(where + 1.0)[:, None] + offset


def levels(stream_key, extent, pieces, smallest, largest):
    def one(dim, blocks):
        steps = jax.random.uniform(jax.random.fold_in(jax.random.fold_in(stream_key, 6), dim), (blocks,), jnp.float32, smallest / len(pieces), largest / len(pieces))
        return jnp.repeat(jnp.exp(steps), extent[dim] // blocks).reshape((-1,) + (1,) * (len(extent) - dim - 1))

    loudness = one(*pieces[0])
    for cut in pieces[1:]:
        loudness = loudness * one(*cut)
    return loudness


def bell_draw(key, shape, spread, bound, cuts=(), kind=jnp.bfloat16):
    result = spread * jax.random.normal(key, shape, jnp.float32)
    if cuts:
        result = result * levels(key, shape, cuts, -0.22, 0.18)
    return jnp.clip(result, -bound, bound).astype(kind)


def setup_inputs(seed: int = 0) -> dict:
    streams_of = jax.random.split(jax.random.key(seed), 9)
    return {
        "hidden_in": bell_draw(streams_of[0], (SEQUENCE_TOKENS, D), 1.0, 6.0, ((0, 128),)),
        "queries": bell_draw(streams_of[1], (SEQUENCE_TOKENS, QUERY_HEADS * HEAD_SIZE), 1.0, 6.0, ((0, 128),)),
        "keys": bell_draw(streams_of[2], (SEQUENCE_TOKENS, KEY_VALUE_HEADS * HEAD_SIZE), 1.0, 6.0, ((0, 128),)),
        "values": bell_draw(streams_of[3], (SEQUENCE_TOKENS, KEY_VALUE_HEADS * HEAD_SIZE), 1.0, 6.0, ((0, 128),)),
        "attention_output": bell_draw(streams_of[4], (SEQUENCE_TOKENS, QUERY_HEADS * HEAD_SIZE), 1.0, 6.0, ((0, 128),)),
        "output_gradient": bell_draw(streams_of[5], (SEQUENCE_TOKENS, QUERY_HEADS * HEAD_SIZE), 1.0, 6.0, ((0, 128),)),
        "log_softmax_total": draw_log_softmax_total(jax.random.fold_in(streams_of[8], 71), 0),
        "positions": draw_positions(jax.random.fold_in(streams_of[8], 71), 0),
    }


def reference(hidden_in, queries, keys, values, attention_output, output_gradient, log_softmax_total, positions):
    query_group = QUERY_HEADS // KEY_VALUE_HEADS
    scale = HEAD_SIZE ** -0.5
    query_block = min(512, SEQUENCE_TOKENS)
    keys_wide = keys.astype(jnp.float32).reshape(SEQUENCE_TOKENS, KEY_VALUE_HEADS, HEAD_SIZE)
    values_wide = values.astype(jnp.float32).reshape(SEQUENCE_TOKENS, KEY_VALUE_HEADS, HEAD_SIZE)

    def step(carry, index):
        key_gradient, value_gradient = carry
        start_offset = (index * query_block).astype(jnp.int32)
        query_rows = lax.dynamic_slice_in_dim(queries, start_offset, query_block, 0).astype(jnp.float32).reshape(query_block, KEY_VALUE_HEADS, query_group, HEAD_SIZE)
        output_rows = lax.dynamic_slice_in_dim(attention_output, start_offset, query_block, 0).astype(jnp.float32).reshape(query_block, KEY_VALUE_HEADS, query_group, HEAD_SIZE)
        gradient_rows = lax.dynamic_slice_in_dim(output_gradient, start_offset, query_block, 0).astype(jnp.float32).reshape(query_block, KEY_VALUE_HEADS, query_group, HEAD_SIZE)
        logsumexp_rows = lax.dynamic_slice_in_dim(log_softmax_total, start_offset, query_block, 0).reshape(query_block, KEY_VALUE_HEADS, query_group).transpose(1, 2, 0)[..., None]
        pos_rows = lax.dynamic_slice_in_dim(positions, start_offset, query_block, 0)
        delta = jnp.sum(gradient_rows * output_rows, axis=-1).transpose(1, 2, 0)[..., None]
        scores = jnp.einsum('qgrd,kgd->grqk', query_rows, keys_wide) * scale
        allowed = positions[None, :] <= pos_rows[:, None]
        probs = jnp.where(allowed, jnp.exp(scores - logsumexp_rows), 0.0)
        dprobs = jnp.einsum('qgrd,kgd->grqk', gradient_rows, values_wide)
        dscores = lax.optimization_barrier((probs * (dprobs - delta)).astype(jnp.bfloat16)).astype(jnp.float32)
        probs_r = lax.optimization_barrier(probs.astype(jnp.bfloat16)).astype(jnp.float32)
        grad_q = (jnp.einsum('grqk,kgd->qgrd', dscores, keys_wide) * scale).astype(jnp.bfloat16).reshape(query_block, QUERY_HEADS * HEAD_SIZE)
        key_gradient = key_gradient + jnp.einsum('grqk,qgrd->kgd', dscores, query_rows) * scale
        value_gradient = value_gradient + jnp.einsum('grqk,qgrd->kgd', probs_r, gradient_rows)
        return (key_gradient, value_gradient), grad_q

    zero_buffer = jnp.zeros((SEQUENCE_TOKENS, KEY_VALUE_HEADS, HEAD_SIZE), jnp.float32)
    (key_gradient, value_gradient), grad_q = lax.scan(step, (zero_buffer, zero_buffer), jnp.arange(SEQUENCE_TOKENS // query_block))
    grad_queries = grad_q.reshape(SEQUENCE_TOKENS, QUERY_HEADS * HEAD_SIZE)
    key_gradient = key_gradient.astype(jnp.bfloat16).reshape(SEQUENCE_TOKENS, KEY_VALUE_HEADS * HEAD_SIZE)
    value_gradient = value_gradient.astype(jnp.bfloat16).reshape(SEQUENCE_TOKENS, KEY_VALUE_HEADS * HEAD_SIZE)
    grad_wk = jnp.dot(hidden_in.T, key_gradient, preferred_element_type=jnp.float32)
    grad_wv = jnp.dot(hidden_in.T, value_gradient, preferred_element_type=jnp.float32)
    return (grad_queries, grad_wk, grad_wv)
```

```python
import functools
import math

import jax
import jax.numpy as jnp
from jax import lax
from jax.experimental import pallas as pl
from jax.experimental.pallas import tpu as pltpu
from jax.sharding import PartitionSpec as P

HEAD = 128
GROUPS = 2
SHARE = 4
RUN = 64
KEYS = 4096
KEY_RUNS = KEYS // RUN
QUERY_ROWS = 1024
QUERY_RUNS = QUERY_ROWS // RUN
UNIT = 2
CHUNK = 512
SCALE = HEAD**-0.5
LOG2E = math.log2(math.e)
F32 = jnp.float32
BF16 = jnp.bfloat16
MESH = pl.DeviceIdType.MESH
NT = (((1,), (1,)), ((), ()))
NN = (((1,), (0,)), ((), ()))
VMEM = pl.BlockSpec(memory_space=pltpu.VMEM)
SMEM = pl.BlockSpec(memory_space=pltpu.SMEM)
HBM = pl.BlockSpec(memory_space=pltpu.HBM)
PARTS = (6, 5, 5)
ORDERS = ("zxy", "xyz", "yzx")


def dot(a, b, dims):
    return lax.dot_general(a, b, dims, preferred_element_type=F32)


def wrap(value):
    return lax.rem(value + 4, 4)


class Place:
    def __init__(self):
        inner, outer = lax.axis_index("inner"), lax.axis_index("outer")
        c = lax.rem(inner, 2)
        x = lax.div(inner, 8) * 2 + lax.div(outer, 4)
        y = lax.rem(lax.div(inner, 2), 4)
        z = lax.rem(outer, 4)
        self.c = c
        self.at = {"x": x, "y": y, "z": z, "L": z + c * (x - z), "M": x + c * (z - x)}
        self.step = {"x": (1, 0, 0), "y": (0, 1, 0), "z": (0, 0, 1), "L": (c, 0, 1 - c), "M": (1 - c, 0, c)}

    def device(self, axis=None, by=0, other=False):
        step = (0, 0, 0) if axis is None else self.step[axis]
        x, y, z = (wrap(self.at[name] + by * d) for name, d in zip("xyz", step))
        c = 1 - self.c if other else self.c
        return ((lax.div(x, 2) * 4 + y) * 2 + c, lax.rem(x, 2) * 4 + z)

    def beside(self):
        near = [self.device(axis, by) for axis in "xyz" for by in (1, -1, 2)]
        return near + [self.device(other=True)]


class Net:
    def __init__(self, place, send_sems, recv_sems):
        self.place, self.send_sems, self.recv_sems = place, send_sems, recv_sems
        self.sent = []

    def greet(self):
        barrier = pltpu.get_barrier_semaphore()
        near = self.place.beside()
        for device in near:
            pl.semaphore_signal(barrier, inc=1, device_id=device, device_id_type=MESH)
        pl.semaphore_wait(barrier, len(near))

    def send(self, src, dst, device):
        k = len(self.sent)
        assert k < self.send_sems.shape[0]
        copy = pltpu.make_async_remote_copy(
            src_ref=src,
            dst_ref=dst,
            send_sem=self.send_sems.at[k],
            recv_sem=self.recv_sems.at[k],
            device_id=device,
            device_id_type=MESH,
        )
        copy.start()
        self.sent.append(copy)
        return copy

    def finish(self):
        for copy in self.sent:
            copy.wait_send()

    def pair(self, axis, src, dst):
        return [self.send(src, dst, self.place.device(axis, by)) for by in (1, -1)]

    def relay(self, axis, pair, ref, n):
        s = self.place.at[axis]
        low, high = pl.ds(0, n // 2), pl.ds(n // 2, n - n // 2)
        pair[0].wait_recv()
        block = ref(wrap(s - 1), low)
        up = self.send(block, block, self.place.device(axis, 1))
        pair[1].wait_recv()
        block = ref(wrap(s + 1), high)
        return [up, self.send(block, block, self.place.device(axis, -1))]

    def cast(self, axis, block):
        return [self.send(block, block, self.place.device(axis, by)) for by in (1, -1, 2)]

    def scatter(self, axis, hbm, buf, relay, from_behind, from_ahead, out):
        s = self.place.at[axis]
        ahead, behind = self.place.device(axis, 1), self.place.device(axis, -1)
        n = buf.shape[1]
        h = n // 2
        low, high = pl.ds(0, h), pl.ds(h, n - h)
        far, left, right = wrap(s + 2), wrap(s - 1), wrap(s + 1)
        relay_up = self.send(hbm.at[far, low], relay.at[low], ahead)
        relay_down = self.send(hbm.at[far, high], relay.at[high], behind)
        up_high = self.send(hbm.at[right, high], from_behind.at[high], ahead)
        down_low = self.send(hbm.at[left, low], from_ahead.at[low], behind)
        yield
        relay_up.wait_recv()
        buf[right, low] = (buf[right, low].astype(F32) + relay[low].astype(F32)).astype(BF16)
        up_low = self.send(buf.at[right, low], from_behind.at[low], ahead)
        relay_down.wait_recv()
        buf[left, high] = (buf[left, high].astype(F32) + relay[high].astype(F32)).astype(BF16)
        down_high = self.send(buf.at[left, high], from_ahead.at[high], behind)
        yield
        for copy in (up_high, down_low, up_low, down_high):
            copy.wait_recv()
        out[...] = (
            buf[s].astype(F32) + from_behind[...].astype(F32) + from_ahead[...].astype(F32)
        ).astype(out.dtype)

    def scatter_direct(self, axis, buf, inbox, out):
        s = self.place.at[axis]
        copies = [
            self.send(buf.at[wrap(s + by)], inbox.at[i], self.place.device(axis, by))
            for i, by in enumerate((1, -1, 2))
        ]
        yield
        for copy in copies:
            copy.wait_recv()
        out[...] = (
            buf[s].astype(F32)
            + inbox[0].astype(F32)
            + inbox[1].astype(F32)
            + inbox[2].astype(F32)
        ).astype(out.dtype)


def together(*chains):
    chains = list(chains)
    while chains:
        for chain in list(chains):
            try:
                next(chain)
            except StopIteration:
                chains.remove(chain)


def gather_kernel(
    q, do, k, v, do_v, ao, lse, pos, qg, dog, kg, vg, sg, pg, stats, mine, spots, send_sems, recv_sems, own_sems
):
    place = Place()
    net = Net(place, send_sems, recv_sems)
    y, c, l, m = place.at["y"], place.c, place.at["L"], place.at["M"]
    twin = place.device(other=True)
    net.greet()
    first, second = (pl.multiple_of(i * 128, 128) for i in (c, 1 - c))

    def cut(columns):
        return [pl.ds(pl.multiple_of(i * columns, columns), columns) for i in (c, 1 - c)]

    wide, thin = cut(1024), cut(256)
    owns = []

    def keep(src, dst):
        copy = pltpu.make_async_copy(src, dst, own_sems.at[len(owns)])
        copy.start()
        owns.append(copy)
        return copy

    def queries_chain(src, buf):
        def block(start):
            return lambda slot, rows: buf.at[slot, pl.ds(start + rows.start, rows.size)]

        whole = pl.ds(0, 128)
        mine_at, twin_at = block(first), block(second)
        from_twin = net.send(src.at[:, wide[1]], buf.at[m, pl.ds(first, 128)], twin)
        pair = net.pair("L", src.at[:, wide[0]], mine_at(l, whole))
        own = keep(src.at[:, wide[0]], mine_at(l, whole))
        yield
        from_twin.wait_recv()
        pair2 = net.pair("L", twin_at(l, whole), twin_at(l, whole))
        yield
        relays = net.relay("L", pair, mine_at, 128)
        yield
        relays += net.relay("L", pair2, twin_at, 128)
        yield
        for copy in relays:
            copy.wait_recv()
        own.wait()

    def keys_chain(src, buf, a, b):
        i, j = place.at[a], place.at[b]
        whole = pl.ds(0, 128)

        def block(start):
            return lambda slot, rows: buf.at[j, slot, pl.ds(start + rows.start, rows.size)]

        def chip(slot):
            return lambda other, rows: buf.at[other, slot, rows]

        def pair_b(slot):
            return (slot, net.pair(b, buf.at[j, slot], buf.at[j, slot]))

        mine_at, twin_at = block(first), block(second)
        there = buf.at[y, l] if a == "M" else buf.at[l, y]
        from_twin = net.send(src.at[:, thin[1]], there.at[pl.ds(first, 128)], twin)
        pair = net.pair(a, src.at[:, thin[0]], mine_at(i, whole))
        own = keep(src.at[:, thin[0]], mine_at(i, whole))
        yield
        from_twin.wait_recv()
        pair2 = net.pair(a, twin_at(i, whole), twin_at(i, whole))
        own.wait()
        pairs = [pair_b(i)]
        yield
        relays = net.relay(a, pair, mine_at, 128)
        yield
        relays += net.relay(a, pair2, twin_at, 128)
        pairs += [pair_b(wrap(i - 1)), pair_b(wrap(i + 1))]
        yield
        for copy in relays:
            copy.wait_recv()
        pairs.append(pair_b(wrap(i + 2)))
        yield
        relays = []
        for slot, both in pairs:
            relays += net.relay(b, both, chip(slot), 256)
        yield
        for copy in relays:
            copy.wait_recv()

    def stats_chain():
        spots[...] = jnp.broadcast_to(pos[...], (8, 128)).astype(F32)
        place_own = keep(spots, pg.at[y, m, c])
        place_twin = net.send(spots, pg.at[y, l, c], twin)
        stats[...] = jnp.zeros_like(stats)
        stats[:, 0:16] = lse[...] * LOG2E
        for h in range(16):
            columns = slice(h * HEAD, (h + 1) * HEAD)
            product = do_v[:, columns].astype(F32) * ao[:, columns].astype(F32)
            stats[:, 16 + h : 17 + h] = jnp.sum(product, axis=1, keepdims=True)
        turned = stats[...].T
        for i in range(2):
            mine[i, 0:8, :] = turned[i * 8 : i * 8 + 8]
            mine[i, 8:16, :] = turned[16 + i * 8 : 24 + i * 8]
            mine[i, 16:24, :] = spots[...]
        stats_twin = net.send(mine.at[1 - c], sg.at[m, c], twin)
        stats_own = keep(mine.at[c], sg.at[l, c])
        yield
        place_own.wait()
        place_twin.wait_recv()
        places = net.cast("M", pg.at[y, m])
        stats_own.wait()
        stats_twin.wait_recv()
        rest = net.cast("L", sg.at[l])
        yield
        for copy in places:
            copy.wait_recv()
        rest += net.cast("y", pg.at[y])
        yield
        yield
        for copy in rest:
            copy.wait_recv()

    together(
        keys_chain(k, kg, "M", "y"),
        keys_chain(v, vg, "y", "M"),
        queries_chain(q, qg),
        queries_chain(do, dog),
        stats_chain(),
    )
    net.finish()


def gather_all(q, do, k, v, ao, lse, pos):
    shape = jax.ShapeDtypeStruct
    return pl.pallas_call(
        gather_kernel,
        out_shape=[
            shape((4, 256, 1024), BF16),
            shape((4, 256, 1024), BF16),
            shape((4, 4, 256, 256), BF16),
            shape((4, 4, 256, 256), BF16),
            shape((4, 2, 24, 128), F32),
            shape((4, 4, 2, 8, 128), F32),
        ],
        in_specs=[HBM] * 4 + [VMEM] * 4,
        out_specs=[HBM] * 6,
        scratch_shapes=[
            pltpu.VMEM((128, 128), F32),
            pltpu.VMEM((2, 24, 128), F32),
            pltpu.VMEM((8, 128), F32),
            pltpu.SemaphoreType.DMA((96,)),
            pltpu.SemaphoreType.DMA((96,)),
            pltpu.SemaphoreType.DMA((6,)),
        ],
        compiler_params=pltpu.CompilerParams(
            collective_id=0, has_side_effects=True, vmem_limit_bytes=60 * 2**20
        ),
    )(q, do, k, v, do, ao, lse, pos)


def attend_kernel(
    rank, order, reach, qplace, kplace, qg, dog, kg, vg, sg, dqp, dkp, dvp,
    q_all, do_all, k_all, v_all, columns, dq_all, dk_all, dv_all,
    qs, dos, qt, dot_, lse_s, delta_s, dq_sum, dk_sum, dv_sum, in_sems, out_sems,
):
    rows = UNIT * SHARE * RUN

    def at_run(ref, j, first):
        a, b, r = lax.div(j, 16), lax.rem(lax.div(j, 4), 4), lax.rem(j, 4)
        part = pl.ds(pl.multiple_of(r * RUN, RUN), RUN)
        return ref.at[a, b, part] if first else ref.at[b, a, part]

    def key_copies(j):
        spot = pl.ds(pl.multiple_of(rank[j] * RUN, RUN), RUN)
        return (
            pltpu.make_async_copy(at_run(kg, j, True), k_all.at[spot], in_sems.at[0]),
            pltpu.make_async_copy(at_run(vg, j, False), v_all.at[spot], in_sems.at[1]),
        )

    def query_copies(r):
        i = order[r]
        part = pl.ds(pl.multiple_of(lax.rem(i, 4) * RUN, RUN), RUN)
        spot = pl.ds(pl.multiple_of(r * RUN, RUN), RUN)
        return (
            pltpu.make_async_copy(qg.at[lax.div(i, 4), part], q_all.at[spot], in_sems.at[2]),
            pltpu.make_async_copy(dog.at[lax.div(i, 4), part], do_all.at[spot], in_sems.at[3]),
        )

    def start(make):
        def body(i, _):
            for copy in make(i):
                copy.start()
            return 0

        return body

    lax.fori_loop(0, QUERY_RUNS, start(query_copies), 0)
    lax.fori_loop(0, KEY_RUNS, start(key_copies), 0)
    for z in range(4):
        for c in range(2):
            spot = (z * 2 + c) * 128
            columns[spot : spot + 128, 0:24] = sg[z, c].T
    dk_sum[...] = jnp.zeros_like(dk_sum)
    dv_sum[...] = jnp.zeros_like(dv_sum)
    pltpu.make_async_copy(q_all, q_all, in_sems.at[2]).wait()
    pltpu.make_async_copy(do_all, do_all, in_sems.at[3]).wait()
    pltpu.make_async_copy(k_all, k_all, in_sems.at[0]).wait()
    pltpu.make_async_copy(v_all, v_all, in_sems.at[1]).wait()

    per = CHUNK // RUN

    def unit(i, _):
        for u in range(UNIT):
            r = i * UNIT + u
            r0 = pl.multiple_of(r * RUN, RUN)
            s0 = pl.multiple_of(order[r] * RUN, RUN)
            for g in range(GROUPS):
                for h in range(SHARE):
                    head = g * SHARE + h
                    o = (u * SHARE + h) * RUN
                    spot = pl.ds(o, RUN)
                    qs[g, spot, :] = q_all[pl.ds(r0, RUN), head * HEAD : (head + 1) * HEAD]
                    dos[g, spot, :] = do_all[pl.ds(r0, RUN), head * HEAD : (head + 1) * HEAD]
                    lse_s[g, spot, :] = columns[pl.ds(s0, RUN), head : head + 1]
                    delta_s[g, spot, :] = columns[pl.ds(s0, RUN), 8 + head : 9 + head]
        for g in range(GROUPS):
            qt[g] = qs[g].T
            dot_[g] = dos[g].T
        dq_sum[...] = jnp.zeros_like(dq_sum)
        first, last = reach[i * UNIT], reach[i * UNIT + UNIT - 1]
        whole, chunks = lax.div(first - 1, per), lax.div(last + per - 1, per)

        def step(masked, chunk, _):
            k0 = pl.multiple_of(chunk * CHUNK, CHUNK)
            keys = pl.ds(k0, CHUNK)
            if masked:
                row = lax.broadcasted_iota(jnp.int32, (rows, 1), 0)
                qpos = lax.rem(row, RUN)
                for u in range(UNIT):
                    inside = lax.div(row, SHARE * RUN) == u
                    qpos = qpos + jnp.where(inside, qplace[i * UNIT + u], 0)
                column = lax.broadcasted_iota(jnp.int32, (1, CHUNK), 1)
                kpos = lax.rem(column, RUN)
                for u in range(per):
                    kpos = kpos + jnp.where(lax.div(column, RUN) == u, kplace[chunk * per + u], 0)
                allowed = kpos <= qpos
            for g in range(GROUPS):
                kk = k_all[keys, g * HEAD : (g + 1) * HEAD]
                vv = v_all[keys, g * HEAD : (g + 1) * HEAD]
                probs = jnp.exp2(dot(qs[g], kk, NT) * (SCALE * LOG2E) - lse_s[g])
                if masked:
                    probs = jnp.where(allowed, probs, 0.0)
                dprobs = dot(dos[g], vv, NT)
                dscores = (probs * (dprobs - delta_s[g])).astype(BF16)
                dq_sum[g] += dot(dscores, kk, NN)
                dv_sum[g, :, keys] += dot(dot_[g], probs.astype(BF16), NN)
                dk_sum[g, :, keys] += dot(qt[g], dscores, NN)
            return 0

        lax.fori_loop(0, whole, functools.partial(step, False), 0)
        lax.fori_loop(whole, chunks, functools.partial(step, True), 0)
        for u in range(UNIT):
            r0 = pl.multiple_of((i * UNIT + u) * RUN, RUN)
            for g in range(GROUPS):
                for h in range(SHARE):
                    head = g * SHARE + h
                    o = (u * SHARE + h) * RUN
                    dq_all[pl.ds(r0, RUN), head * HEAD : (head + 1) * HEAD] = (
                        dq_sum[g, o : o + RUN, :] * SCALE
                    ).astype(BF16)
        return 0

    lax.fori_loop(0, QUERY_RUNS // UNIT, unit, 0)

    def query_back(r):
        i = order[r]
        part = pl.ds(pl.multiple_of(lax.rem(i, 4) * RUN, RUN), RUN)
        spot = pl.ds(pl.multiple_of(r * RUN, RUN), RUN)
        return (pltpu.make_async_copy(dq_all.at[spot], dqp.at[lax.div(i, 4), part], out_sems.at[0]),)

    def key_back(j):
        spot = pl.ds(pl.multiple_of(rank[j] * RUN, RUN), RUN)
        return (
            pltpu.make_async_copy(dk_all.at[spot], at_run(dkp, j, True), out_sems.at[1]),
            pltpu.make_async_copy(dv_all.at[spot], at_run(dvp, j, False), out_sems.at[2]),
        )

    lax.fori_loop(0, QUERY_RUNS, start(query_back), 0)

    def turn(chunk, _):
        keys = pl.ds(pl.multiple_of(chunk * CHUNK, CHUNK), CHUNK)
        for g in range(GROUPS):
            columns_g = slice(g * HEAD, (g + 1) * HEAD)
            dk_all[keys, columns_g] = (dk_sum[g, :, keys] * SCALE).astype(BF16).T
            dv_all[keys, columns_g] = dv_sum[g, :, keys].astype(BF16).T
        return 0

    lax.fori_loop(0, KEYS // CHUNK, turn, 0)
    lax.fori_loop(0, KEY_RUNS, start(key_back), 0)
    pltpu.make_async_copy(dq_all, dq_all, out_sems.at[0]).wait()
    pltpu.make_async_copy(dk_all, dk_all, out_sems.at[1]).wait()
    pltpu.make_async_copy(dv_all, dv_all, out_sems.at[2]).wait()


def attend(rank, order, reach, qplace, kplace, qg, dog, kg, vg, sg):
    shape = jax.ShapeDtypeStruct
    rows = UNIT * SHARE * RUN
    return pl.pallas_call(
        attend_kernel,
        out_shape=[
            shape((4, 256, 1024), BF16),
            shape((4, 4, 256, 256), BF16),
            shape((4, 4, 256, 256), BF16),
        ],
        in_specs=[SMEM] * 5 + [HBM] * 4 + [VMEM],
        out_specs=[HBM] * 3,
        scratch_shapes=[
            pltpu.VMEM((QUERY_ROWS, 1024), BF16),
            pltpu.VMEM((QUERY_ROWS, 1024), BF16),
            pltpu.VMEM((KEYS, 256), BF16),
            pltpu.VMEM((KEYS, 256), BF16),
            pltpu.VMEM((QUERY_ROWS, 24), F32),
            pltpu.VMEM((QUERY_ROWS, 1024), BF16),
            pltpu.VMEM((KEYS, 256), BF16),
            pltpu.VMEM((KEYS, 256), BF16),
            pltpu.VMEM((GROUPS, rows, HEAD), BF16),
            pltpu.VMEM((GROUPS, rows, HEAD), BF16),
            pltpu.VMEM((GROUPS, HEAD, rows), BF16),
            pltpu.VMEM((GROUPS, HEAD, rows), BF16),
            pltpu.VMEM((GROUPS, rows, 1), F32),
            pltpu.VMEM((GROUPS, rows, 1), F32),
            pltpu.VMEM((GROUPS, rows, HEAD), F32),
            pltpu.VMEM((GROUPS, HEAD, KEYS), F32),
            pltpu.VMEM((GROUPS, HEAD, KEYS), F32),
            pltpu.SemaphoreType.DMA((4,)),
            pltpu.SemaphoreType.DMA((3,)),
        ],
        compiler_params=pltpu.CompilerParams(vmem_limit_bytes=60 * 2**20),
    )(rank, order, reach, qplace, kplace, qg, dog, kg, vg, sg)


def reduce_kernel(hidden, dqp, dkp, dvp, dq, *rest):
    wg = rest[0:3]
    (h_twin, ht, dkv, dq_sums, dk_sums, dv_sums) = rest[3:9]
    (dq_relay, dq_up, dq_down, dq_own) = rest[9:13]
    (dk_relay, dk_up, dk_down, dk_mid, dk_inbox) = rest[13:18]
    (dv_relay, dv_up, dv_down, dv_mid, dv_inbox) = rest[18:23]
    spare = rest[23:-3]
    send_sems, recv_sems, own_sems = rest[-3:]
    place = Place()
    net = Net(place, send_sems, recv_sems)
    c = place.c
    twin = place.device(other=True)
    loads = []
    for src, dst in ((dkp, dk_sums), (dvp, dv_sums), (dqp, dq_sums)):
        loads.append(pltpu.make_async_copy(src, dst, own_sems.at[len(loads)]))
        loads[-1].start()
    net.greet()
    rows = pl.ds(pl.multiple_of(c * 128, 128), 128)
    theirs = pl.ds(pl.multiple_of((1 - c) * 128, 128), 128)

    def queries_chain():
        first = net.scatter("L", dqp, dq_sums, dq_relay, dq_up, dq_down, dq_own)
        next(first)
        yield
        loads[2].wait()
        yield from first
        columns = pl.ds(pl.multiple_of(c * 1024, 1024), 1024)
        copy = net.send(dq_own.at[theirs], dq.at[:, columns], twin)
        own = pltpu.make_async_copy(dq_own.at[rows], dq.at[:, columns], own_sems.at[3])
        own.start()
        yield
        own.wait()
        copy.wait_recv()

    def keys_chain(load, hbm, sums, relay, up, down, mid, inbox, a, b, out):
        first = net.scatter(a, hbm, sums, relay, up, down, mid)
        next(first)
        yield
        load.wait()
        yield from first
        yield from net.scatter_direct(b, mid, inbox, out)

    def hidden_chain():
        copy = net.send(hidden, h_twin, twin)
        yield
        copy.wait_recv()
        ht[:, 0:128] = jnp.where(c == 0, hidden[...], h_twin[...]).T
        ht[:, 128:256] = jnp.where(c == 0, h_twin[...], hidden[...]).T

    together(
        keys_chain(
            loads[0], dkp, dk_sums, dk_relay, dk_up, dk_down, dk_mid, dk_inbox, "y", "M", dkv.at[:, 0:256]
        ),
        keys_chain(
            loads[1], dvp, dv_sums, dv_relay, dv_up, dv_down, dv_mid, dv_inbox, "M", "y", dkv.at[:, 256:512]
        ),
        queries_chain(),
        hidden_chain(),
    )

    parts = [spare[i * 10 : (i + 1) * 10] for i in range(3)]
    where = []
    for tile in range(16):
        row, column = tile // 4, tile % 4
        if row < 3:
            where.append((row, column))
        else:
            where.append({0: (1, 4), 1: (2, 4), 2: (0, 4), 3: (0, 5)}[column])

    def project(i, _):
        xi, yi = lax.div(i, 4), lax.rem(i, 4)
        block = pl.ds(pl.multiple_of(i * 256, 256), 256)
        term = dot(ht[block, :], dkv[...], NN).astype(BF16)
        for zi in range(4):
            at = {"x": xi, "y": yi, "z": zi}
            for tile in range(16):
                part, u = where[tile]
                r0, c0 = zi * 64 + (tile // 4) * 16, (tile % 4) * 128
                o = [at[axis] for axis in ORDERS[part]]
                parts[part][0][o[0], o[1], o[2], u] = term[r0 : r0 + 16, c0 : c0 + 128]
        return 0

    lax.fori_loop(0, 16, project, 0)

    def part_chain(p):
        order, whole = ORDERS[p], wg[p]
        terms, relay, up, down, mid, inbox, mid2, inbox2, total = parts[p][:9]
        at = [place.at[axis] for axis in order]
        yield from net.scatter(order[0], terms, terms, relay, up, down, mid)
        yield from net.scatter_direct(order[1], mid, inbox, mid2)
        yield from net.scatter_direct(order[2], mid2, inbox2, total)
        mine = whole.at[c]
        own = pltpu.make_async_copy(total, mine.at[at[0], at[1], at[2]], own_sems.at[4 + p])
        own.start()
        own.wait()
        for copy in net.cast(order[2], mine.at[at[0], at[1], at[2]]):
            yield
            copy.wait_recv()
        for copy in net.cast(order[1], mine.at[at[0], at[1]]):
            yield
            copy.wait_recv()

        def ref(slot, part):
            return mine.at[slot, part]

        def share(slot):
            return net.send(mine.at[slot], mine.at[slot], twin)

        pair = net.pair(order[0], mine.at[at[0]], mine.at[at[0]])
        shares = [share(at[0])]
        yield
        relays = net.relay(order[0], pair, ref, 4)
        shares += [share(wrap(at[0] - 1)), share(wrap(at[0] + 1))]
        yield
        for copy in relays:
            copy.wait_recv()
        shares.append(share(wrap(at[0] + 2)))
        yield
        for copy in shares:
            copy.wait_recv()

    together(*[part_chain(p) for p in range(3)])
    net.finish()


def reduce_all(hidden, dqp, dkp, dvp):
    shape = jax.ShapeDtypeStruct

    def buf(*dims, dtype=BF16):
        return pltpu.VMEM(dims, dtype)

    scratch = [buf(128, 4096), buf(4096, 256), buf(256, 512)]
    scratch += [buf(4, 256, 1024), buf(4, 4, 256, 256), buf(4, 4, 256, 256)]
    scratch += [buf(256, 1024)] * 4
    for _ in range(2):
        scratch += [buf(4, 256, 256)] * 4 + [buf(3, 256, 256)]
    for n in PARTS:
        scratch += [buf(4, 4, 4, n, 16, 128)]
        scratch += [buf(4, 4, n, 16, 128)] * 4 + [buf(3, 4, n, 16, 128)]
        scratch += [buf(4, n, 16, 128, dtype=F32), buf(3, n, 16, 128, dtype=F32)]
        scratch += [buf(n, 16, 128)] * 2
    return pl.pallas_call(
        reduce_kernel,
        out_shape=[shape((128, 2048), BF16)]
        + [shape((2, 4, 4, 4, n, 16, 128), BF16) for n in PARTS],
        in_specs=[VMEM] + [HBM] * 3,
        out_specs=[VMEM] + [HBM] * 3,
        scratch_shapes=scratch
        + [
            pltpu.SemaphoreType.DMA((128,)),
            pltpu.SemaphoreType.DMA((128,)),
            pltpu.SemaphoreType.DMA((8,)),
        ],
        compiler_params=pltpu.CompilerParams(
            collective_id=1, has_side_effects=True, vmem_limit_bytes=60 * 2**20
        ),
    )(hidden, dqp, dkp, dvp)


def widen_kernel(a, b, c, wk, wv):
    for zi in range(4):
        for core in range(2):
            for tile in range(16):
                row, column = tile // 4, tile % 4
                if row == 0:
                    value = a[core, zi, 0, 0, column]
                elif row == 1:
                    value = b[core, 0, 0, zi, column]
                elif row == 2:
                    value = c[core, 0, zi, 0, column]
                elif column == 0:
                    value = b[core, 0, 0, zi, 4]
                elif column == 1:
                    value = c[core, 0, zi, 0, 4]
                else:
                    value = a[core, zi, 0, 0, column + 2]
                r0 = zi * 64 + row * 16
                c0 = core * 256 + (column % 2) * 128
                out = wk if column < 2 else wv
                out[r0 : r0 + 16, c0 : c0 + 128] = value.astype(F32)


def widen(a, b, c):
    shape = jax.ShapeDtypeStruct
    return pl.pallas_call(
        widen_kernel,
        grid=(16,),
        out_shape=[shape((4096, 512), F32)] * 2,
        in_specs=[
            pl.BlockSpec((2, 4, 1, 1, 6, 16, 128), lambda i: (0, 0, i // 4, i % 4, 0, 0, 0)),
            pl.BlockSpec((2, 1, 1, 4, 5, 16, 128), lambda i: (0, i // 4, i % 4, 0, 0, 0, 0)),
            pl.BlockSpec((2, 1, 4, 1, 5, 16, 128), lambda i: (0, i % 4, 0, i // 4, 0, 0, 0)),
        ],
        out_specs=[pl.BlockSpec((256, 512), lambda i: (i, 0))] * 2,
        compiler_params=pltpu.CompilerParams(vmem_limit_bytes=60 * 2**20),
    )(a, b, c)


def local(hidden, q, k, v, ao, do, lse, pos):
    qg, dog, kg, vg, sg, pg = gather_all(q, do, k, v, ao, lse, pos[None, :])
    kp = pg[:, :, :, 0, ::RUN].reshape(KEY_RUNS).astype(jnp.int32)
    qp = sg[:, :, 16, ::RUN].reshape(QUERY_RUNS).astype(jnp.int32)
    rank = jnp.sum(kp[None, :] < kp[:, None], axis=1, dtype=jnp.int32)
    kplace = jnp.sum(
        jnp.where(rank[None, :] == jnp.arange(KEY_RUNS)[:, None], kp[None, :], 0), axis=1, dtype=jnp.int32
    )
    qrank = jnp.sum(qp[None, :] < qp[:, None], axis=1, dtype=jnp.int32)
    here = qrank[None, :] == jnp.arange(QUERY_RUNS)[:, None]
    order = jnp.sum(jnp.where(here, jnp.arange(QUERY_RUNS)[None, :], 0), axis=1, dtype=jnp.int32)
    qplace = jnp.sum(jnp.where(here, qp[None, :], 0), axis=1, dtype=jnp.int32)
    reach = jnp.sum(kp[None, :] <= qplace[:, None], axis=1, dtype=jnp.int32)
    dqp, dkp, dvp = attend(rank, order, reach, qplace, kplace, qg, dog, kg, vg, sg)
    dq, a, b, c = reduce_all(hidden, dqp, dkp, dvp)
    wk, wv = widen(a, b, c)
    return dq, wk, wv


def solution(mesh):
    rows = P(("inner", "outer"), None)
    return jax.shard_map(
        local,
        mesh=mesh,
        in_specs=(rows,) * 7 + (P(("inner", "outer")),),
        out_specs=(rows, P(), P()),
        check_vma=False,
    )
```

```python
import functools
import math

import jax
import jax.numpy as jnp
from jax import lax
from jax.experimental import pallas as pl
from jax.experimental.pallas import tpu as pltpu
from jax.sharding import PartitionSpec as P

HEAD = 128
GROUPS = 2
SHARE = 4
RUN = 64
KEYS = 4096
KEY_RUNS = KEYS // RUN
QUERY_ROWS = 1024
QUERY_RUNS = QUERY_ROWS // RUN
UNIT = 2
CHUNK = 512
SCALE = HEAD**-0.5
LOG2E = math.log2(math.e)
F32 = jnp.float32
BF16 = jnp.bfloat16
MESH = pl.DeviceIdType.MESH
NT = (((1,), (1,)), ((), ()))
NN = (((1,), (0,)), ((), ()))
VMEM = pl.BlockSpec(memory_space=pltpu.VMEM)
SMEM = pl.BlockSpec(memory_space=pltpu.SMEM)
HBM = pl.BlockSpec(memory_space=pltpu.HBM)
ORDERS = ("zxy", "xyz", "yzx")
PARTS = (
    (((0, 0), (0, 1), (3, 0)), ((1, 0), (1, 1), (3, 1)), ((2, 0), (2, 1))),
    (((0, 0), (0, 1), (3, 0)), ((1, 0), (1, 1)), ((2, 0), (2, 1), (3, 1))),
)
SIZES = [len(tiles) for batch in PARTS for tiles in batch]


def dot(a, b, dims):
    return lax.dot_general(a, b, dims, preferred_element_type=F32)


def wrap(value):
    return lax.rem(value + 4, 4)


class Place:
    def __init__(self):
        inner, outer = lax.axis_index("inner"), lax.axis_index("outer")
        c = lax.rem(inner, 2)
        x = lax.div(inner, 8) * 2 + lax.div(outer, 4)
        y = lax.rem(lax.div(inner, 2), 4)
        z = lax.rem(outer, 4)
        self.c = c
        self.at = {"x": x, "y": y, "z": z, "L": z + c * (x - z), "M": x + c * (z - x)}
        self.step = {"x": (1, 0, 0), "y": (0, 1, 0), "z": (0, 0, 1), "L": (c, 0, 1 - c), "M": (1 - c, 0, c)}

    def device(self, axis=None, by=0, other=False):
        step = (0, 0, 0) if axis is None else self.step[axis]
        x, y, z = (wrap(self.at[name] + by * d) for name, d in zip("xyz", step))
        c = 1 - self.c if other else self.c
        return ((lax.div(x, 2) * 4 + y) * 2 + c, lax.rem(x, 2) * 4 + z)

    def beside(self):
        near = [self.device(axis, by) for axis in "xyz" for by in (1, -1, 2)]
        return near + [self.device(other=True)]


class Net:
    def __init__(self, place, send_sems, recv_sems):
        self.place, self.send_sems, self.recv_sems = place, send_sems, recv_sems
        self.sent = []

    def greet(self):
        barrier = pltpu.get_barrier_semaphore()
        near = self.place.beside()
        for device in near:
            pl.semaphore_signal(barrier, inc=1, device_id=device, device_id_type=MESH)
        pl.semaphore_wait(barrier, len(near))

    def send(self, src, dst, device):
        k = len(self.sent)
        assert k < self.send_sems.shape[0]
        copy = pltpu.make_async_remote_copy(
            src_ref=src,
            dst_ref=dst,
            send_sem=self.send_sems.at[k],
            recv_sem=self.recv_sems.at[k],
            device_id=device,
            device_id_type=MESH,
        )
        copy.start()
        self.sent.append(copy)
        return copy

    def finish(self):
        for copy in self.sent:
            copy.wait_send()

    def pair(self, axis, src, dst):
        return [self.send(src, dst, self.place.device(axis, by)) for by in (1, -1)]

    def relay(self, axis, pair, ref, n):
        s = self.place.at[axis]
        low, high = pl.ds(0, n // 2), pl.ds(n // 2, n - n // 2)
        pair[0].wait_recv()
        block = ref(wrap(s - 1), low)
        up = self.send(block, block, self.place.device(axis, 1))
        pair[1].wait_recv()
        block = ref(wrap(s + 1), high)
        return [up, self.send(block, block, self.place.device(axis, -1))]

    def cast(self, axis, block):
        return [self.send(block, block, self.place.device(axis, by)) for by in (1, -1, 2)]

    def scatter(self, axis, hbm, buf, at, n, relay, from_behind, from_ahead, out):
        s = self.place.at[axis]
        ahead, behind = self.place.device(axis, 1), self.place.device(axis, -1)
        h = n // 2
        low, high, whole = pl.ds(0, h), pl.ds(h, n - h), pl.ds(0, n)
        far, left, right = wrap(s + 2), wrap(s - 1), wrap(s + 1)
        relay_up = self.send(hbm.at[at(far, low)], relay.at[low], ahead)
        relay_down = self.send(hbm.at[at(far, high)], relay.at[high], behind)
        up_high = self.send(hbm.at[at(right, high)], from_behind.at[high], ahead)
        down_low = self.send(hbm.at[at(left, low)], from_ahead.at[low], behind)
        yield
        relay_up.wait_recv()
        spot = at(right, low)
        buf[spot] = (buf[spot].astype(F32) + relay[low].astype(F32)).astype(BF16)
        up_low = self.send(buf.at[spot], from_behind.at[low], ahead)
        relay_down.wait_recv()
        spot = at(left, high)
        buf[spot] = (buf[spot].astype(F32) + relay[high].astype(F32)).astype(BF16)
        down_high = self.send(buf.at[spot], from_ahead.at[high], behind)
        yield
        for copy in (up_high, down_low, up_low, down_high):
            copy.wait_recv()
        out[...] = (
            buf[at(s, whole)].astype(F32) + from_behind[...].astype(F32) + from_ahead[...].astype(F32)
        ).astype(out.dtype)

    def scatter_direct(self, axis, buf, inbox, out):
        s = self.place.at[axis]
        copies = [
            self.send(buf.at[wrap(s + by)], inbox.at[i], self.place.device(axis, by))
            for i, by in enumerate((1, -1, 2))
        ]
        yield
        for copy in copies:
            copy.wait_recv()
        out[...] = (
            buf[s].astype(F32)
            + inbox[0].astype(F32)
            + inbox[1].astype(F32)
            + inbox[2].astype(F32)
        ).astype(out.dtype)


def together(*chains):
    chains = list(chains)
    while chains:
        for chain in list(chains):
            try:
                next(chain)
            except StopIteration:
                chains.remove(chain)


def gather_kernel(
    q, do, k, v, do_v, ao, lse, pos, qg, dog, kg, vg, sg, pq, pk, stats, mine, send_sems, recv_sems, own_sems
):
    place = Place()
    net = Net(place, send_sems, recv_sems)
    y, c, l, m = place.at["y"], place.c, place.at["L"], place.at["M"]
    twin = place.device(other=True)
    net.greet()
    first, second = (pl.multiple_of(i * 128, 128) for i in (c, 1 - c))

    def cut(columns):
        return [pl.ds(pl.multiple_of(i * columns, columns), columns) for i in (c, 1 - c)]

    wide, thin = cut(1024), cut(256)
    owns = []

    def keep(src, dst):
        copy = pltpu.make_async_copy(src, dst, own_sems.at[len(owns)])
        copy.start()
        owns.append(copy)
        return copy

    def queries_chain(src, buf):
        def block(start):
            return lambda slot, rows: buf.at[slot, pl.ds(start + rows.start, rows.size)]

        whole = pl.ds(0, 128)
        mine_at, twin_at = block(first), block(second)
        from_twin = net.send(src.at[:, wide[1]], buf.at[m, pl.ds(first, 128)], twin)
        pair = net.pair("L", src.at[:, wide[0]], mine_at(l, whole))
        own = keep(src.at[:, wide[0]], mine_at(l, whole))
        yield
        from_twin.wait_recv()
        pair2 = net.pair("L", twin_at(l, whole), twin_at(l, whole))
        yield
        relays = net.relay("L", pair, mine_at, 128)
        yield
        relays += net.relay("L", pair2, twin_at, 128)
        yield
        for copy in relays:
            copy.wait_recv()
        own.wait()

    def keys_chain(src, buf, a, b):
        i, j = place.at[a], place.at[b]
        whole = pl.ds(0, 128)

        def block(start):
            return lambda slot, rows: buf.at[j, slot, pl.ds(start + rows.start, rows.size)]

        def chip(slot):
            return lambda other, rows: buf.at[other, slot, rows]

        def pair_b(slot):
            return (slot, net.pair(b, buf.at[j, slot], buf.at[j, slot]))

        mine_at, twin_at = block(first), block(second)
        there = buf.at[y, l] if a == "M" else buf.at[l, y]
        from_twin = net.send(src.at[:, thin[1]], there.at[pl.ds(first, 128)], twin)
        pair = net.pair(a, src.at[:, thin[0]], mine_at(i, whole))
        own = keep(src.at[:, thin[0]], mine_at(i, whole))
        yield
        from_twin.wait_recv()
        pair2 = net.pair(a, twin_at(i, whole), twin_at(i, whole))
        own.wait()
        pairs = [pair_b(i)]
        yield
        relays = net.relay(a, pair, mine_at, 128)
        yield
        relays += net.relay(a, pair2, twin_at, 128)
        pairs += [pair_b(wrap(i - 1)), pair_b(wrap(i + 1))]
        yield
        for copy in relays:
            copy.wait_recv()
        pairs.append(pair_b(wrap(i + 2)))
        yield
        relays = []
        for slot, both in pairs:
            relays += net.relay(b, both, chip(slot), 256)
        yield
        for copy in relays:
            copy.wait_recv()

    def stats_chain():
        kept = [keep(pos, pk.at[y, m, c]), keep(pos, pq.at[l, c])]
        from_twin = [net.send(pos, pk.at[y, l, c], twin), net.send(pos, pq.at[m, c], twin)]
        for h in range(16):
            columns = slice(h * HEAD, (h + 1) * HEAD)
            product = do_v[:, columns].astype(F32) * ao[:, columns].astype(F32)
            stats[:, h : h + 1] = jnp.sum(product, axis=1, keepdims=True)
        turned = stats[...].T
        for i in range(2):
            mine[i, 0:8, :] = lse[i * 8 : i * 8 + 8] * LOG2E
            mine[i, 8:16, :] = turned[i * 8 : i * 8 + 8]
        from_twin.append(net.send(mine.at[1 - c], sg.at[m, c], twin))
        kept.append(keep(mine.at[c], sg.at[l, c]))
        yield
        for copy in kept:
            copy.wait()
        for copy in from_twin:
            copy.wait_recv()
        places = net.cast("M", pk.at[y, m])
        rest = net.cast("L", sg.at[l]) + net.cast("L", pq.at[l])
        yield
        for copy in places:
            copy.wait_recv()
        rest += net.cast("y", pk.at[y])
        yield
        yield
        for copy in rest:
            copy.wait_recv()

    together(
        keys_chain(k, kg, "M", "y"),
        keys_chain(v, vg, "y", "M"),
        queries_chain(q, qg),
        queries_chain(do, dog),
        stats_chain(),
    )
    net.finish()


def gather_all(q, do, k, v, ao, lse, pos):
    shape = jax.ShapeDtypeStruct
    return pl.pallas_call(
        gather_kernel,
        out_shape=[
            shape((4, 256, 1024), BF16),
            shape((4, 256, 1024), BF16),
            shape((4, 4, 256, 256), BF16),
            shape((4, 4, 256, 256), BF16),
            shape((4, 2, 16, 128), F32),
            shape((4, 2, 1, 128), jnp.int32),
            shape((4, 4, 2, 1, 128), jnp.int32),
        ],
        in_specs=[HBM] * 4 + [VMEM] * 4,
        out_specs=[HBM] * 7,
        scratch_shapes=[
            pltpu.VMEM((128, 128), F32),
            pltpu.VMEM((2, 16, 128), F32),
            pltpu.SemaphoreType.DMA((96,)),
            pltpu.SemaphoreType.DMA((96,)),
            pltpu.SemaphoreType.DMA((8,)),
        ],
        compiler_params=pltpu.CompilerParams(
            collective_id=0, has_side_effects=True, vmem_limit_bytes=60 * 2**20
        ),
    )(q, do, k, v, do, ao, lse, pos)


def attend_kernel(
    pq, pk, qg, dog, kg, vg, sg, dqp, dkp, dvp, order, reach, qplace, rank, kplace, found, found_s,
    q_all, do_all, k_all, v_all, columns, dq_all, dk_all, dv_all,
    qs, dos, qt, dot_, lse_s, delta_s, dq_sum, dk_sum, dv_sum, in_sems, out_sems,
):
    rows = UNIT * SHARE * RUN

    def at_run(ref, j, first):
        a, b, r = lax.div(j, 16), lax.rem(lax.div(j, 4), 4), lax.rem(j, 4)
        part = pl.ds(pl.multiple_of(r * RUN, RUN), RUN)
        return ref.at[a, b, part] if first else ref.at[b, a, part]

    def key_copies(j):
        spot = pl.ds(pl.multiple_of(rank[j] * RUN, RUN), RUN)
        return (
            pltpu.make_async_copy(at_run(kg, j, True), k_all.at[spot], in_sems.at[0]),
            pltpu.make_async_copy(at_run(vg, j, False), v_all.at[spot], in_sems.at[1]),
        )

    def query_copies(r):
        i = order[r]
        part = pl.ds(pl.multiple_of(lax.rem(i, 4) * RUN, RUN), RUN)
        spot = pl.ds(pl.multiple_of(r * RUN, RUN), RUN)
        return (
            pltpu.make_async_copy(qg.at[lax.div(i, 4), part], q_all.at[spot], in_sems.at[2]),
            pltpu.make_async_copy(dog.at[lax.div(i, 4), part], do_all.at[spot], in_sems.at[3]),
        )

    def start(make):
        def body(i, _):
            for copy in make(i):
                copy.start()
            return 0

        return body

    def query_place(i):
        return pq[lax.div(i, 4), lax.rem(lax.div(i, 2), 2), 0, lax.rem(i, 2) * RUN]

    def key_place(j):
        c = lax.rem(lax.div(j, 2), 2)
        return pk[lax.div(j, 16), lax.rem(lax.div(j, 4), 4), c, 0, lax.rem(j, 2) * RUN]

    lane = lax.broadcasted_iota(jnp.int32, (1, 128), 1)
    blank = jnp.zeros((1, 128), jnp.int32)
    query_row = lax.fori_loop(
        0, QUERY_RUNS, lambda i, row: jnp.where(lane == i, query_place(i), row), blank, unroll=True
    )
    key_row = lax.fori_loop(
        0, KEY_RUNS, lambda j, row: jnp.where(lane == j, key_place(j), row), blank, unroll=True
    )

    def count_queries(i, total):
        return total + jnp.where(query_place(i) < query_row, 1, 0)

    def count_keys(j, totals):
        place = key_place(j)
        return (
            totals[0] + jnp.where(place < key_row, 1, 0),
            totals[1] + jnp.where(place <= query_row, 1, 0),
        )

    found[0:1, :] = lax.fori_loop(0, QUERY_RUNS, count_queries, blank, unroll=True)
    key_rank, query_reach = lax.fori_loop(0, KEY_RUNS, count_keys, (blank, blank), unroll=True)
    found[1:2, :] = query_reach
    found[2:3, :] = key_rank
    copy = pltpu.make_async_copy(found, found_s, in_sems.at[4])
    copy.start()
    for z in range(4):
        for c in range(2):
            spot = (z * 2 + c) * 128
            columns[spot : spot + 128, 0:16] = sg[z, c].T
    copy.wait()

    def place_query(i, _):
        r = found_s[0, i]
        order[r] = i
        reach[r] = found_s[1, i]
        qplace[r] = query_place(i)
        return 0

    def place_key(j, _):
        rank[j] = found_s[2, j]
        kplace[found_s[2, j]] = key_place(j)
        return 0

    lax.fori_loop(0, QUERY_RUNS, place_query, 0)
    lax.fori_loop(0, QUERY_RUNS, start(query_copies), 0)
    lax.fori_loop(0, KEY_RUNS, place_key, 0)
    lax.fori_loop(0, KEY_RUNS, start(key_copies), 0)
    dk_sum[...] = jnp.zeros_like(dk_sum)
    dv_sum[...] = jnp.zeros_like(dv_sum)
    pltpu.make_async_copy(q_all, q_all, in_sems.at[2]).wait()
    pltpu.make_async_copy(do_all, do_all, in_sems.at[3]).wait()
    pltpu.make_async_copy(k_all, k_all, in_sems.at[0]).wait()
    pltpu.make_async_copy(v_all, v_all, in_sems.at[1]).wait()

    per = CHUNK // RUN

    def unit(i, _):
        for u in range(UNIT):
            r = i * UNIT + u
            r0 = pl.multiple_of(r * RUN, RUN)
            s0 = pl.multiple_of(order[r] * RUN, RUN)
            for g in range(GROUPS):
                for h in range(SHARE):
                    head = g * SHARE + h
                    o = (u * SHARE + h) * RUN
                    spot = pl.ds(o, RUN)
                    qs[g, spot, :] = q_all[pl.ds(r0, RUN), head * HEAD : (head + 1) * HEAD]
                    dos[g, spot, :] = do_all[pl.ds(r0, RUN), head * HEAD : (head + 1) * HEAD]
                    lse_s[g, spot, :] = columns[pl.ds(s0, RUN), head : head + 1]
                    delta_s[g, spot, :] = columns[pl.ds(s0, RUN), 8 + head : 9 + head]
        for g in range(GROUPS):
            qt[g] = qs[g].T
            dot_[g] = dos[g].T
        dq_sum[...] = jnp.zeros_like(dq_sum)
        first, last = reach[i * UNIT], reach[i * UNIT + UNIT - 1]
        whole, chunks = lax.div(first - 1, per), lax.div(last + per - 1, per)

        def step(masked, chunk, _):
            k0 = pl.multiple_of(chunk * CHUNK, CHUNK)
            keys = pl.ds(k0, CHUNK)
            if masked:
                row = lax.broadcasted_iota(jnp.int32, (rows, 1), 0)
                qpos = lax.rem(row, RUN)
                for u in range(UNIT):
                    inside = lax.div(row, SHARE * RUN) == u
                    qpos = qpos + jnp.where(inside, qplace[i * UNIT + u], 0)
                column = lax.broadcasted_iota(jnp.int32, (1, CHUNK), 1)
                kpos = lax.rem(column, RUN)
                for u in range(per):
                    kpos = kpos + jnp.where(lax.div(column, RUN) == u, kplace[chunk * per + u], 0)
                allowed = kpos <= qpos
            for g in range(GROUPS):
                kk = k_all[keys, g * HEAD : (g + 1) * HEAD]
                vv = v_all[keys, g * HEAD : (g + 1) * HEAD]
                probs = jnp.exp2(dot(qs[g], kk, NT) * (SCALE * LOG2E) - lse_s[g])
                if masked:
                    probs = jnp.where(allowed, probs, 0.0)
                dprobs = dot(dos[g], vv, NT)
                dscores = (probs * (dprobs - delta_s[g])).astype(BF16)
                dq_sum[g] += dot(dscores, kk, NN)
                dv_sum[g, :, keys] += dot(dot_[g], probs.astype(BF16), NN)
                dk_sum[g, :, keys] += dot(qt[g], dscores, NN)
            return 0

        lax.fori_loop(0, whole, functools.partial(step, False), 0)
        lax.fori_loop(whole, chunks, functools.partial(step, True), 0)
        for u in range(UNIT):
            r0 = pl.multiple_of((i * UNIT + u) * RUN, RUN)
            for g in range(GROUPS):
                for h in range(SHARE):
                    head = g * SHARE + h
                    o = (u * SHARE + h) * RUN
                    dq_all[pl.ds(r0, RUN), head * HEAD : (head + 1) * HEAD] = (
                        dq_sum[g, o : o + RUN, :] * SCALE
                    ).astype(BF16)
        return 0

    lax.fori_loop(0, QUERY_RUNS // UNIT, unit, 0)

    def query_back(r):
        i = order[r]
        part = pl.ds(pl.multiple_of(lax.rem(i, 4) * RUN, RUN), RUN)
        spot = pl.ds(pl.multiple_of(r * RUN, RUN), RUN)
        return (pltpu.make_async_copy(dq_all.at[spot], dqp.at[lax.div(i, 4), part], out_sems.at[0]),)

    def key_back(j):
        spot = pl.ds(pl.multiple_of(rank[j] * RUN, RUN), RUN)
        return (
            pltpu.make_async_copy(dk_all.at[spot], at_run(dkp, j, True), out_sems.at[1]),
            pltpu.make_async_copy(dv_all.at[spot], at_run(dvp, j, False), out_sems.at[2]),
        )

    lax.fori_loop(0, QUERY_RUNS, start(query_back), 0)

    def turn(chunk, _):
        keys = pl.ds(pl.multiple_of(chunk * CHUNK, CHUNK), CHUNK)
        for g in range(GROUPS):
            columns_g = slice(g * HEAD, (g + 1) * HEAD)
            dk_all[keys, columns_g] = (dk_sum[g, :, keys] * SCALE).astype(BF16).T
            dv_all[keys, columns_g] = dv_sum[g, :, keys].astype(BF16).T
        return 0

    lax.fori_loop(0, KEYS // CHUNK, turn, 0)
    lax.fori_loop(0, KEY_RUNS, start(key_back), 0)
    pltpu.make_async_copy(dq_all, dq_all, out_sems.at[0]).wait()
    pltpu.make_async_copy(dk_all, dk_all, out_sems.at[1]).wait()
    pltpu.make_async_copy(dv_all, dv_all, out_sems.at[2]).wait()


def attend(pq, pk, qg, dog, kg, vg, sg):
    shape = jax.ShapeDtypeStruct
    rows = UNIT * SHARE * RUN
    return pl.pallas_call(
        attend_kernel,
        out_shape=[
            shape((4, 256, 1024), BF16),
            shape((4, 4, 256, 256), BF16),
            shape((4, 4, 256, 256), BF16),
        ],
        in_specs=[SMEM] * 2 + [HBM] * 4 + [VMEM],
        out_specs=[HBM] * 3,
        scratch_shapes=[
            pltpu.SMEM((QUERY_RUNS,), jnp.int32),
            pltpu.SMEM((QUERY_RUNS,), jnp.int32),
            pltpu.SMEM((QUERY_RUNS,), jnp.int32),
            pltpu.SMEM((KEY_RUNS,), jnp.int32),
            pltpu.SMEM((KEY_RUNS,), jnp.int32),
            pltpu.VMEM((8, 128), jnp.int32),
            pltpu.SMEM((8, 128), jnp.int32),
            pltpu.VMEM((QUERY_ROWS, 1024), BF16),
            pltpu.VMEM((QUERY_ROWS, 1024), BF16),
            pltpu.VMEM((KEYS, 256), BF16),
            pltpu.VMEM((KEYS, 256), BF16),
            pltpu.VMEM((QUERY_ROWS, 16), F32),
            pltpu.VMEM((QUERY_ROWS, 1024), BF16),
            pltpu.VMEM((KEYS, 256), BF16),
            pltpu.VMEM((KEYS, 256), BF16),
            pltpu.VMEM((GROUPS, rows, HEAD), BF16),
            pltpu.VMEM((GROUPS, rows, HEAD), BF16),
            pltpu.VMEM((GROUPS, HEAD, rows), BF16),
            pltpu.VMEM((GROUPS, HEAD, rows), BF16),
            pltpu.VMEM((GROUPS, rows, 1), F32),
            pltpu.VMEM((GROUPS, rows, 1), F32),
            pltpu.VMEM((GROUPS, rows, HEAD), F32),
            pltpu.VMEM((GROUPS, HEAD, KEYS), F32),
            pltpu.VMEM((GROUPS, HEAD, KEYS), F32),
            pltpu.SemaphoreType.DMA((5,)),
            pltpu.SemaphoreType.DMA((3,)),
        ],
        compiler_params=pltpu.CompilerParams(vmem_limit_bytes=60 * 2**20),
    )(pq, pk, qg, dog, kg, vg, sg)


def reduce_kernel(hidden, dqp, dkp, dvp, dq, *rest):
    rest = list(rest)

    def take(n):
        taken, rest[:n] = rest[:n], []
        return taken

    wg = take(6)
    h_twin, ht, dkv, dq_sums, dk_sums, dv_sums = take(6)
    dq_bufs, dq_own = take(3), take(1)[0]
    term_bufs = [take(5) for _ in range(4)]
    part_bufs = [take(9) for _ in range(6)]
    send_sems, recv_sems, own_sems = rest
    place = Place()
    net = Net(place, send_sems, recv_sems)
    c = place.c
    twin = place.device(other=True)
    loads = []
    for src, dst in ((dkp, dk_sums), (dvp, dv_sums), (dqp, dq_sums)):
        loads.append(pltpu.make_async_copy(src, dst, own_sems.at[len(loads)]))
        loads[-1].start()
    net.greet()
    rows = pl.ds(pl.multiple_of(c * 128, 128), 128)
    theirs = pl.ds(pl.multiple_of((1 - c) * 128, 128), 128)
    done = set()

    def loaded(i):
        if i not in done:
            loads[i].wait()
            done.add(i)

    def queries_chain():
        for _ in range(3):
            yield
        first = net.scatter("L", dqp, dq_sums, lambda slot, part: (slot, part), 256, *dq_bufs, dq_own)
        next(first)
        yield
        loaded(2)
        yield from first
        columns = pl.ds(pl.multiple_of(c * 1024, 1024), 1024)
        copy = net.send(dq_own.at[theirs], dq.at[:, columns], twin)
        own = pltpu.make_async_copy(dq_own.at[rows], dq.at[:, columns], own_sems.at[3])
        own.start()
        yield
        own.wait()
        copy.wait_recv()

    def terms_chain(batch, g):
        for _ in range(batch):
            yield
        hbm, sums = ((dkp, dk_sums), (dvp, dv_sums))[batch]
        relay, up, down, mid, inbox = term_bufs[batch * 2 + g]
        axes = ("y", "M") if g == 0 else ("M", "y")
        columns = pl.ds(g * HEAD, HEAD)

        def at(slot, part):
            return (slot, part) + (slice(None), columns) if batch == g else (part, slot) + (slice(None), columns)

        first = net.scatter(axes[0], hbm, sums, at, 4, relay, up, down, mid)
        next(first)
        yield
        loaded(batch)
        yield from first
        out = dkv.at[:, pl.ds(batch * 256 + g * HEAD, HEAD)]
        yield from net.scatter_direct(axes[1], mid, inbox, out)
        done.add(("terms", batch, g))

    def hidden_chain():
        copy = net.send(hidden, h_twin, twin)
        yield
        copy.wait_recv()
        ht[:, 0:128] = jnp.where(c == 0, hidden[...], h_twin[...]).T
        ht[:, 128:256] = jnp.where(c == 0, h_twin[...], hidden[...]).T
        done.add("hidden")

    def project_chain(batch):
        while not {("terms", batch, 0), ("terms", batch, 1), "hidden"} <= done:
            yield

        def project(i, _):
            xi, yi = lax.div(i, 4), lax.rem(i, 4)
            block = pl.ds(pl.multiple_of(i * 256, 256), 256)
            term = dot(ht[block, :], dkv[:, batch * 256 : batch * 256 + 256], NN).astype(BF16)
            for zi in range(4):
                at = {"x": xi, "y": yi, "z": zi}
                for p, tiles in enumerate(PARTS[batch]):
                    o = [at[axis] for axis in ORDERS[p]]
                    for u, (row, column) in enumerate(tiles):
                        r0, c0 = zi * 64 + row * 16, column * 128
                        part_bufs[batch * 3 + p][0][o[0], o[1], o[2], u] = term[r0 : r0 + 16, c0 : c0 + 128]
            return 0

        lax.fori_loop(0, 16, project, 0)
        done.add(("project", batch))

    def part_chain(batch, p):
        while ("project", batch) not in done:
            yield
        order, whole = ORDERS[p], wg[batch * 3 + p]
        terms, relay, up, down, mid, inbox, mid2, inbox2, total = part_bufs[batch * 3 + p]
        at = [place.at[axis] for axis in order]
        yield from net.scatter(
            order[0], terms, terms, lambda slot, part: (slot, part), 4, relay, up, down, mid
        )
        yield from net.scatter_direct(order[1], mid, inbox, mid2)
        yield from net.scatter_direct(order[2], mid2, inbox2, total)
        mine = whole.at[c]
        own = pltpu.make_async_copy(total, mine.at[at[0], at[1], at[2]], own_sems.at[4 + batch * 3 + p])
        own.start()
        own.wait()
        copies = net.cast(order[2], mine.at[at[0], at[1], at[2]])
        yield
        for copy in copies:
            copy.wait_recv()
        copies = net.cast(order[1], mine.at[at[0], at[1]])
        yield
        for copy in copies:
            copy.wait_recv()

        def ref(slot, part):
            return mine.at[slot, part]

        def share(slot):
            return net.send(mine.at[slot], mine.at[slot], twin)

        pair = net.pair(order[0], mine.at[at[0]], mine.at[at[0]])
        shares = [share(at[0])]
        yield
        relays = net.relay(order[0], pair, ref, 4)
        shares += [share(wrap(at[0] - 1)), share(wrap(at[0] + 1))]
        yield
        for copy in relays:
            copy.wait_recv()
        shares.append(share(wrap(at[0] + 2)))
        yield
        for copy in shares:
            copy.wait_recv()

    chains = []
    for batch in range(2):
        chains += [terms_chain(batch, 0), terms_chain(batch, 1)]
        chains += [hidden_chain()] if batch == 0 else []
        chains += [project_chain(batch)] + [part_chain(batch, p) for p in range(3)]
    together(*chains, queries_chain())
    net.finish()


def reduce_all(hidden, dqp, dkp, dvp):
    shape = jax.ShapeDtypeStruct

    def buf(*dims, dtype=BF16):
        return pltpu.VMEM(dims, dtype)

    scratch = [buf(128, 4096), buf(4096, 256), buf(256, 512)]
    scratch += [buf(4, 256, 1024), buf(4, 4, 256, 256), buf(4, 4, 256, 256)]
    scratch += [buf(256, 1024)] * 4
    for _ in range(4):
        scratch += [buf(4, 256, HEAD)] * 4 + [buf(3, 256, HEAD)]
    for n in SIZES:
        scratch += [buf(4, 4, 4, n, 16, 128)]
        scratch += [buf(4, 4, n, 16, 128)] * 4 + [buf(3, 4, n, 16, 128)]
        scratch += [buf(4, n, 16, 128, dtype=F32), buf(3, n, 16, 128, dtype=F32)]
        scratch += [buf(n, 16, 128)]
    return pl.pallas_call(
        reduce_kernel,
        out_shape=[shape((128, 2048), BF16)]
        + [shape((2, 4, 4, 4, n, 16, 128), BF16) for n in SIZES],
        in_specs=[VMEM] + [HBM] * 3,
        out_specs=[VMEM] + [HBM] * 6,
        scratch_shapes=scratch
        + [
            pltpu.SemaphoreType.DMA((204,)),
            pltpu.SemaphoreType.DMA((204,)),
            pltpu.SemaphoreType.DMA((10,)),
        ],
        compiler_params=pltpu.CompilerParams(
            collective_id=1, has_side_effects=True, vmem_limit_bytes=60 * 2**20
        ),
    )(hidden, dqp, dkp, dvp)


def widen_kernel(*refs):
    parts, (wk, wv), held, (wk_v, wv_v), (in_sems, out_sems) = (
        refs[0:6], refs[6:8], refs[8:14], refs[14:16], refs[16:18]
    )

    def at(p, x, y, z):
        places = {"x": x, "y": y, "z": z}
        return tuple(places[axis] for axis in ORDERS[p % 3])

    def loads(i):
        x, y = lax.div(i, 4), lax.rem(i, 4)
        spots = [(slice(None),) + at(p, x, y, slice(None)) for p in range(6)]
        return [
            pltpu.make_async_copy(parts[p].at[spot], held[p].at[spot], in_sems.at[p, i])
            for p, spot in enumerate(spots)
        ]

    def stores(i):
        rows = pl.ds(pl.multiple_of(i * 256, 256), 256)
        return [
            pltpu.make_async_copy(src.at[rows], dst.at[rows], out_sems.at[n, i])
            for n, (src, dst) in enumerate(((wk_v, wk), (wv_v, wv)))
        ]

    def begin(i, _):
        for copy in loads(i):
            copy.start()
        return 0

    def block(i, _):
        x, y = lax.div(i, 4), lax.rem(i, 4)
        for copy in loads(i):
            copy.wait()
        for z in range(4):
            r0 = pl.multiple_of(i * 256 + z * 64, 64)
            for core in range(2):
                for p in range(6):
                    out = wk_v if p < 3 else wv_v
                    for u, (row, column) in enumerate(PARTS[p // 3][p % 3]):
                        value = held[p][(core,) + at(p, x, y, z) + (u,)]
                        c0 = core * 256 + column * 128
                        out[pl.ds(r0 + row * 16, 16), c0 : c0 + 128] = value.astype(F32)
        for copy in stores(i):
            copy.start()
        return 0

    def end(i, _):
        for copy in stores(i):
            copy.wait()
        return 0

    lax.fori_loop(0, 16, begin, 0)
    lax.fori_loop(0, 16, block, 0)
    lax.fori_loop(0, 16, end, 0)


def widen(*parts):
    shape = jax.ShapeDtypeStruct
    return pl.pallas_call(
        widen_kernel,
        out_shape=[shape((4096, 512), F32)] * 2,
        in_specs=[HBM] * 6,
        out_specs=[HBM] * 2,
        scratch_shapes=[pltpu.VMEM((2, 4, 4, 4, n, 16, 128), BF16) for n in SIZES]
        + [
            pltpu.VMEM((4096, 512), F32),
            pltpu.VMEM((4096, 512), F32),
            pltpu.SemaphoreType.DMA((6, 16)),
            pltpu.SemaphoreType.DMA((2, 16)),
        ],
        compiler_params=pltpu.CompilerParams(vmem_limit_bytes=60 * 2**20),
    )(*parts)


def local(hidden, q, k, v, ao, do, lse, pos):
    qg, dog, kg, vg, sg, pq, pk = gather_all(q, do, k, v, ao, lse.T, pos[None, :])
    dqp, dkp, dvp = attend(pq, pk, qg, dog, kg, vg, sg)
    dq, *parts = reduce_all(hidden, dqp, dkp, dvp)
    wk, wv = widen(*parts)
    return dq, wk, wv


def solution(mesh):
    rows = P(("inner", "outer"), None)
    return jax.shard_map(
        local,
        mesh=mesh,
        in_specs=(rows,) * 7 + (P(("inner", "outer")),),
        out_specs=(rows, P(), P()),
        check_vma=False,
    )
```

```python
import functools
import math

import jax
import jax.numpy as jnp
from jax import lax
from jax.experimental import pallas as pl
from jax.experimental.pallas import tpu as pltpu
from jax.sharding import PartitionSpec as P

HEAD = 128
GROUPS = 2
SHARE = 4
RUN = 64
KEYS = 4096
KEY_RUNS = KEYS // RUN
QUERY_ROWS = 1024
QUERY_RUNS = QUERY_ROWS // RUN
UNIT = 2
CHUNK = 512
SCALE = HEAD**-0.5
LOG2E = math.log2(math.e)
F32 = jnp.float32
BF16 = jnp.bfloat16
MESH = pl.DeviceIdType.MESH
NT = (((1,), (1,)), ((), ()))
NN = (((1,), (0,)), ((), ()))
VMEM = pl.BlockSpec(memory_space=pltpu.VMEM)
SMEM = pl.BlockSpec(memory_space=pltpu.SMEM)
HBM = pl.BlockSpec(memory_space=pltpu.HBM)
ORDERS = ("zxy", "xyz", "yzx")
PARTS = (
    (((0, 0), (0, 1), (3, 0)), ((1, 0), (1, 1), (3, 1)), ((2, 0), (2, 1))),
    (((0, 0), (0, 1), (3, 0)), ((1, 0), (1, 1)), ((2, 0), (2, 1), (3, 1))),
)
AXES = ((("y", "M"), ("M", "y")), (("M", "y"), ("M", "y")))
SIZES = [len(tiles) for batch in PARTS for tiles in batch]


def dot(a, b, dims):
    return lax.dot_general(a, b, dims, preferred_element_type=F32)


def wrap(value):
    return lax.rem(value + 4, 4)


class Place:
    def __init__(self):
        inner, outer = lax.axis_index("inner"), lax.axis_index("outer")
        c = lax.rem(inner, 2)
        x = lax.div(inner, 8) * 2 + lax.div(outer, 4)
        y = lax.rem(lax.div(inner, 2), 4)
        z = lax.rem(outer, 4)
        self.c = c
        self.at = {"x": x, "y": y, "z": z, "L": z + c * (x - z), "M": x + c * (z - x)}
        self.step = {"x": (1, 0, 0), "y": (0, 1, 0), "z": (0, 0, 1), "L": (c, 0, 1 - c), "M": (1 - c, 0, c)}

    def device(self, axis=None, by=0, other=False):
        step = (0, 0, 0) if axis is None else self.step[axis]
        x, y, z = (wrap(self.at[name] + by * d) for name, d in zip("xyz", step))
        c = 1 - self.c if other else self.c
        return ((lax.div(x, 2) * 4 + y) * 2 + c, lax.rem(x, 2) * 4 + z)

    def beside(self):
        near = [self.device(axis, by) for axis in "xyz" for by in (1, -1, 2)]
        return near + [self.device(other=True)]


class Net:
    def __init__(self, place, send_sems, recv_sems):
        self.place, self.send_sems, self.recv_sems = place, send_sems, recv_sems
        self.sent = []

    def greet(self):
        barrier = pltpu.get_barrier_semaphore()
        near = self.place.beside()
        for device in near:
            pl.semaphore_signal(barrier, inc=1, device_id=device, device_id_type=MESH)
        pl.semaphore_wait(barrier, len(near))

    def send(self, src, dst, device):
        k = len(self.sent)
        assert k < self.send_sems.shape[0]
        copy = pltpu.make_async_remote_copy(
            src_ref=src,
            dst_ref=dst,
            send_sem=self.send_sems.at[k],
            recv_sem=self.recv_sems.at[k],
            device_id=device,
            device_id_type=MESH,
        )
        copy.start()
        self.sent.append(copy)
        return copy

    def finish(self):
        for copy in self.sent:
            copy.wait_send()

    def pair(self, axis, src, dst):
        return [self.send(src, dst, self.place.device(axis, by)) for by in (1, -1)]

    def relay(self, axis, pair, ref, n):
        s = self.place.at[axis]
        low, high = pl.ds(0, n // 2), pl.ds(n // 2, n - n // 2)
        pair[0].wait_recv()
        block = ref(wrap(s - 1), low)
        up = self.send(block, block, self.place.device(axis, 1))
        pair[1].wait_recv()
        block = ref(wrap(s + 1), high)
        return [up, self.send(block, block, self.place.device(axis, -1))]

    def cast(self, axis, block):
        return [self.send(block, block, self.place.device(axis, by)) for by in (1, -1, 2)]

    def scatter(self, axis, hbm, buf, at, n, relay, from_behind, from_ahead, out):
        s = self.place.at[axis]
        ahead, behind = self.place.device(axis, 1), self.place.device(axis, -1)
        h = n // 2
        low, high, whole = pl.ds(0, h), pl.ds(h, n - h), pl.ds(0, n)
        far, left, right = wrap(s + 2), wrap(s - 1), wrap(s + 1)
        relay_up = self.send(hbm.at[at(far, low)], relay.at[low], ahead)
        relay_down = self.send(hbm.at[at(far, high)], relay.at[high], behind)
        up_high = self.send(hbm.at[at(right, high)], from_behind.at[high], ahead)
        down_low = self.send(hbm.at[at(left, low)], from_ahead.at[low], behind)
        yield
        relay_up.wait_recv()
        spot = at(right, low)
        buf[spot] = (buf[spot].astype(F32) + relay[low].astype(F32)).astype(BF16)
        up_low = self.send(buf.at[spot], from_behind.at[low], ahead)
        relay_down.wait_recv()
        spot = at(left, high)
        buf[spot] = (buf[spot].astype(F32) + relay[high].astype(F32)).astype(BF16)
        down_high = self.send(buf.at[spot], from_ahead.at[high], behind)
        yield
        for copy in (up_high, down_low, up_low, down_high):
            copy.wait_recv()
        out[...] = (
            buf[at(s, whole)].astype(F32) + from_behind[...].astype(F32) + from_ahead[...].astype(F32)
        ).astype(out.dtype)

    def scatter_direct(self, axis, buf, inbox, out):
        s = self.place.at[axis]
        copies = [
            self.send(buf.at[wrap(s + by)], inbox.at[i], self.place.device(axis, by))
            for i, by in enumerate((1, -1, 2))
        ]
        yield
        for copy in copies:
            copy.wait_recv()
        out[...] = (
            buf[s].astype(F32)
            + inbox[0].astype(F32)
            + inbox[1].astype(F32)
            + inbox[2].astype(F32)
        ).astype(out.dtype)


def late(rounds, chain):
    for _ in range(rounds):
        yield
    yield from chain


def together(*chains):
    chains = list(chains)
    while chains:
        for chain in list(chains):
            try:
                next(chain)
            except StopIteration:
                chains.remove(chain)


def gather_kernel(
    q, do, k, v, do_v, ao, lse, pos, qg, dog, kg, vg, sg, pq, pk, stats, mine, send_sems, recv_sems, own_sems
):
    place = Place()
    net = Net(place, send_sems, recv_sems)
    y, c, l, m = place.at["y"], place.c, place.at["L"], place.at["M"]
    twin = place.device(other=True)
    net.greet()
    first, second = (pl.multiple_of(i * 128, 128) for i in (c, 1 - c))

    def cut(columns):
        return [pl.ds(pl.multiple_of(i * columns, columns), columns) for i in (c, 1 - c)]

    wide, thin = cut(1024), cut(256)
    owns = []

    def keep(src, dst):
        copy = pltpu.make_async_copy(src, dst, own_sems.at[len(owns)])
        copy.start()
        owns.append(copy)
        return copy

    def queries_chain(src, buf):
        def block(start):
            return lambda slot, rows: buf.at[slot, pl.ds(start + rows.start, rows.size)]

        whole = pl.ds(0, 128)
        mine_at, twin_at = block(first), block(second)
        from_twin = net.send(src.at[:, wide[1]], buf.at[m, pl.ds(first, 128)], twin)
        pair = net.pair("L", src.at[:, wide[0]], mine_at(l, whole))
        own = keep(src.at[:, wide[0]], mine_at(l, whole))
        yield
        from_twin.wait_recv()
        pair2 = net.pair("L", twin_at(l, whole), twin_at(l, whole))
        yield
        relays = net.relay("L", pair, mine_at, 128)
        yield
        relays += net.relay("L", pair2, twin_at, 128)
        yield
        for copy in relays:
            copy.wait_recv()
        own.wait()

    def keys_chain(src, buf, a, b):
        i, j = place.at[a], place.at[b]
        whole = pl.ds(0, 128)

        def block(start):
            return lambda slot, rows: buf.at[j, slot, pl.ds(start + rows.start, rows.size)]

        def chip(slot):
            return lambda other, rows: buf.at[other, slot, rows]

        def pair_b(slot):
            return (slot, net.pair(b, buf.at[j, slot], buf.at[j, slot]))

        mine_at, twin_at = block(first), block(second)
        there = buf.at[y, l] if a == "M" else buf.at[l, y]
        from_twin = net.send(src.at[:, thin[1]], there.at[pl.ds(first, 128)], twin)
        pair = net.pair(a, src.at[:, thin[0]], mine_at(i, whole))
        own = keep(src.at[:, thin[0]], mine_at(i, whole))
        yield
        from_twin.wait_recv()
        pair2 = net.pair(a, twin_at(i, whole), twin_at(i, whole))
        own.wait()
        pairs = [pair_b(i)]
        yield
        relays = net.relay(a, pair, mine_at, 128)
        yield
        relays += net.relay(a, pair2, twin_at, 128)
        pairs += [pair_b(wrap(i - 1)), pair_b(wrap(i + 1))]
        yield
        for copy in relays:
            copy.wait_recv()
        pairs.append(pair_b(wrap(i + 2)))
        yield
        relays = []
        for slot, both in pairs:
            relays += net.relay(b, both, chip(slot), 256)
        yield
        for copy in relays:
            copy.wait_recv()

    def stats_chain():
        kept = [keep(pos, pk.at[y, m, c]), keep(pos, pq.at[l, c])]
        from_twin = [net.send(pos, pk.at[y, l, c], twin), net.send(pos, pq.at[m, c], twin)]
        for h in range(16):
            columns = slice(h * HEAD, (h + 1) * HEAD)
            product = do_v[:, columns].astype(F32) * ao[:, columns].astype(F32)
            stats[:, h : h + 1] = jnp.sum(product, axis=1, keepdims=True)
        turned = stats[...].T
        for i in range(2):
            mine[i, 0:8, :] = lse[i * 8 : i * 8 + 8] * LOG2E
            mine[i, 8:16, :] = turned[i * 8 : i * 8 + 8]
        from_twin.append(net.send(mine.at[1 - c], sg.at[m, c], twin))
        kept.append(keep(mine.at[c], sg.at[l, c]))
        yield
        for copy in kept:
            copy.wait()
        for copy in from_twin:
            copy.wait_recv()
        places = net.cast("M", pk.at[y, m])
        rest = net.cast("L", sg.at[l]) + net.cast("L", pq.at[l])
        yield
        for copy in places:
            copy.wait_recv()
        rest += net.cast("y", pk.at[y])
        yield
        yield
        for copy in rest:
            copy.wait_recv()

    together(
        keys_chain(k, kg, "M", "y"),
        keys_chain(v, vg, "y", "M"),
        queries_chain(q, qg),
        late(2, queries_chain(do, dog)),
        stats_chain(),
    )
    net.finish()


def gather_all(q, do, k, v, ao, lse, pos):
    shape = jax.ShapeDtypeStruct
    return pl.pallas_call(
        gather_kernel,
        out_shape=[
            shape((4, 256, 1024), BF16),
            shape((4, 256, 1024), BF16),
            shape((4, 4, 256, 256), BF16),
            shape((4, 4, 256, 256), BF16),
            shape((4, 2, 16, 128), F32),
            shape((4, 2, 1, 128), jnp.int32),
            shape((4, 4, 2, 1, 128), jnp.int32),
        ],
        in_specs=[HBM] * 4 + [VMEM] * 4,
        out_specs=[HBM] * 7,
        scratch_shapes=[
            pltpu.VMEM((128, 128), F32),
            pltpu.VMEM((2, 16, 128), F32),
            pltpu.SemaphoreType.DMA((83,)),
            pltpu.SemaphoreType.DMA((83,)),
            pltpu.SemaphoreType.DMA((8,)),
        ],
        compiler_params=pltpu.CompilerParams(
            collective_id=0, has_side_effects=True, vmem_limit_bytes=60 * 2**20
        ),
    )(q, do, k, v, do, ao, lse, pos)


def attend_kernel(
    pq, pk, qg, dog, kg, vg, sg, dqp, dkp, dvp, order, reach, qplace, rank, origin, kplace, found, found_s,
    q_all, do_all, k_all, v_all, columns, dq_all, dk_all, dv_all,
    qs, dos, qt, dot_, lse_s, delta_s, dq_sum, dk_sum, dv_sum, in_sems, out_sems,
):
    rows = UNIT * SHARE * RUN

    def at_run(ref, j, first):
        a, b, r = lax.div(j, 16), lax.rem(lax.div(j, 4), 4), lax.rem(j, 4)
        part = pl.ds(pl.multiple_of(r * RUN, RUN), RUN)
        return ref.at[a, b, part] if first else ref.at[b, a, part]

    def key_copies(j):
        spot = pl.ds(pl.multiple_of(rank[j] * RUN, RUN), RUN)
        return (
            pltpu.make_async_copy(at_run(kg, j, True), k_all.at[spot], in_sems.at[0]),
            pltpu.make_async_copy(at_run(vg, j, False), v_all.at[spot], in_sems.at[1]),
        )

    def query_copies(r):
        i = order[r]
        part = pl.ds(pl.multiple_of(lax.rem(i, 4) * RUN, RUN), RUN)
        spot = pl.ds(pl.multiple_of(r * RUN, RUN), RUN)
        return (
            pltpu.make_async_copy(qg.at[lax.div(i, 4), part], q_all.at[spot], in_sems.at[2]),
            pltpu.make_async_copy(dog.at[lax.div(i, 4), part], do_all.at[spot], in_sems.at[3]),
        )

    def start(make):
        def body(i, _):
            for copy in make(i):
                copy.start()
            return 0

        return body

    def query_place(i):
        return pq[lax.div(i, 4), lax.rem(lax.div(i, 2), 2), 0, lax.rem(i, 2) * RUN]

    def key_place(j):
        c = lax.rem(lax.div(j, 2), 2)
        return pk[lax.div(j, 16), lax.rem(lax.div(j, 4), 4), c, 0, lax.rem(j, 2) * RUN]

    lane = lax.broadcasted_iota(jnp.int32, (1, 128), 1)
    blank = jnp.zeros((1, 128), jnp.int32)
    query_row = lax.fori_loop(
        0, QUERY_RUNS, lambda i, row: jnp.where(lane == i, query_place(i), row), blank, unroll=True
    )
    key_row = lax.fori_loop(
        0, KEY_RUNS, lambda j, row: jnp.where(lane == j, key_place(j), row), blank, unroll=True
    )

    def count_queries(i, total):
        return total + jnp.where(query_place(i) < query_row, 1, 0)

    def count_keys(j, totals):
        place = key_place(j)
        return (
            totals[0] + jnp.where(place < key_row, 1, 0),
            totals[1] + jnp.where(place <= query_row, 1, 0),
        )

    found[0:1, :] = lax.fori_loop(0, QUERY_RUNS, count_queries, blank, unroll=True)
    key_rank, query_reach = lax.fori_loop(0, KEY_RUNS, count_keys, (blank, blank), unroll=True)
    found[1:2, :] = query_reach
    found[2:3, :] = key_rank
    copy = pltpu.make_async_copy(found, found_s, in_sems.at[4])
    copy.start()
    for z in range(4):
        for c in range(2):
            spot = (z * 2 + c) * 128
            columns[spot : spot + 128, 0:16] = sg[z, c].T
    copy.wait()

    def place_query(i, _):
        r = found_s[0, i]
        order[r] = i
        reach[r] = found_s[1, i]
        qplace[r] = query_place(i)
        return 0

    def place_key(j, _):
        rank[j] = found_s[2, j]
        origin[found_s[2, j]] = j
        kplace[found_s[2, j]] = key_place(j)
        return 0

    lax.fori_loop(0, QUERY_RUNS, place_query, 0)
    lax.fori_loop(0, QUERY_RUNS, start(query_copies), 0)
    lax.fori_loop(0, KEY_RUNS, place_key, 0)
    lax.fori_loop(0, KEY_RUNS, start(key_copies), 0)
    dk_sum[...] = jnp.zeros_like(dk_sum)
    dv_sum[...] = jnp.zeros_like(dv_sum)
    pltpu.make_async_copy(q_all, q_all, in_sems.at[2]).wait()
    pltpu.make_async_copy(do_all, do_all, in_sems.at[3]).wait()
    pltpu.make_async_copy(k_all, k_all, in_sems.at[0]).wait()
    pltpu.make_async_copy(v_all, v_all, in_sems.at[1]).wait()

    per = CHUNK // RUN

    def query_back(r):
        i = order[r]
        part = pl.ds(pl.multiple_of(lax.rem(i, 4) * RUN, RUN), RUN)
        spot = pl.ds(pl.multiple_of(r * RUN, RUN), RUN)
        return (pltpu.make_async_copy(dq_all.at[spot], dqp.at[lax.div(i, 4), part], out_sems.at[0]),)

    def key_back(r):
        j = origin[r]
        spot = pl.ds(pl.multiple_of(r * RUN, RUN), RUN)
        return (
            pltpu.make_async_copy(dk_all.at[spot], at_run(dkp, j, True), out_sems.at[1]),
            pltpu.make_async_copy(dv_all.at[spot], at_run(dvp, j, False), out_sems.at[2]),
        )

    def unit(i, _):
        for u in range(UNIT):
            r = i * UNIT + u
            r0 = pl.multiple_of(r * RUN, RUN)
            s0 = pl.multiple_of(order[r] * RUN, RUN)
            for g in range(GROUPS):
                for h in range(SHARE):
                    head = g * SHARE + h
                    o = (u * SHARE + h) * RUN
                    spot = pl.ds(o, RUN)
                    qs[g, spot, :] = q_all[pl.ds(r0, RUN), head * HEAD : (head + 1) * HEAD]
                    dos[g, spot, :] = do_all[pl.ds(r0, RUN), head * HEAD : (head + 1) * HEAD]
                    lse_s[g, spot, :] = columns[pl.ds(s0, RUN), head : head + 1]
                    delta_s[g, spot, :] = columns[pl.ds(s0, RUN), 8 + head : 9 + head]
        for g in range(GROUPS):
            qt[g] = qs[g].T
            dot_[g] = dos[g].T
        dq_sum[...] = jnp.zeros_like(dq_sum)
        first, last = reach[i * UNIT], reach[i * UNIT + UNIT - 1]
        whole = lax.div(first - 1, per)
        rest = lax.rem(last, per)
        chunks = lax.div(last, per) + jnp.where(rest > per // 2, 1, 0)
        halves = jnp.where((rest > 0) & (rest <= per // 2), 1, 0)

        def step(masked, size, base, chunk, _):
            r0 = base + chunk * (size // RUN)
            keys = pl.ds(pl.multiple_of(r0 * RUN, size), size)
            if masked:
                row = lax.broadcasted_iota(jnp.int32, (rows, 1), 0)
                qpos = lax.rem(row, RUN)
                for u in range(UNIT):
                    inside = lax.div(row, SHARE * RUN) == u
                    qpos = qpos + jnp.where(inside, qplace[i * UNIT + u], 0)
                column = lax.broadcasted_iota(jnp.int32, (1, size), 1)
                kpos = lax.rem(column, RUN)
                for u in range(size // RUN):
                    kpos = kpos + jnp.where(lax.div(column, RUN) == u, kplace[r0 + u], 0)
                allowed = kpos <= qpos
            for g in range(GROUPS):
                kk = k_all[keys, g * HEAD : (g + 1) * HEAD]
                vv = v_all[keys, g * HEAD : (g + 1) * HEAD]
                probs = jnp.exp2(dot(qs[g], kk, NT) * (SCALE * LOG2E) - lse_s[g])
                if masked:
                    probs = jnp.where(allowed, probs, 0.0)
                dprobs = dot(dos[g], vv, NT)
                dscores = (probs * (dprobs - delta_s[g])).astype(BF16)
                dq_sum[g] += dot(dscores, kk, NN)
                dv_sum[g, :, keys] += dot(dot_[g], probs.astype(BF16), NN)
                dk_sum[g, :, keys] += dot(qt[g], dscores, NN)
            return 0

        lax.fori_loop(0, whole, functools.partial(step, False, CHUNK, 0), 0)
        lax.fori_loop(whole, chunks, functools.partial(step, True, CHUNK, 0), 0)
        lax.fori_loop(0, halves, functools.partial(step, True, CHUNK // 2, chunks * per), 0)
        for u in range(UNIT):
            r0 = pl.multiple_of((i * UNIT + u) * RUN, RUN)
            for g in range(GROUPS):
                for h in range(SHARE):
                    head = g * SHARE + h
                    o = (u * SHARE + h) * RUN
                    dq_all[pl.ds(r0, RUN), head * HEAD : (head + 1) * HEAD] = (
                        dq_sum[g, o : o + RUN, :] * SCALE
                    ).astype(BF16)
            for copy in query_back(i * UNIT + u):
                copy.start()
        return 0

    lax.fori_loop(0, QUERY_RUNS // UNIT, unit, 0)

    def turn(chunk, _):
        keys = pl.ds(pl.multiple_of(chunk * CHUNK, CHUNK), CHUNK)
        for g in range(GROUPS):
            columns_g = slice(g * HEAD, (g + 1) * HEAD)
            dk_all[keys, columns_g] = (dk_sum[g, :, keys] * SCALE).astype(BF16).T
            dv_all[keys, columns_g] = dv_sum[g, :, keys].astype(BF16).T
        for u in range(per):
            for copy in key_back(chunk * per + u):
                copy.start()
        return 0

    lax.fori_loop(0, KEYS // CHUNK, turn, 0)
    pltpu.make_async_copy(dq_all, dq_all, out_sems.at[0]).wait()
    pltpu.make_async_copy(dk_all, dk_all, out_sems.at[1]).wait()
    pltpu.make_async_copy(dv_all, dv_all, out_sems.at[2]).wait()


def attend(pq, pk, qg, dog, kg, vg, sg):
    shape = jax.ShapeDtypeStruct
    rows = UNIT * SHARE * RUN
    return pl.pallas_call(
        attend_kernel,
        out_shape=[
            shape((4, 256, 1024), BF16),
            shape((4, 4, 256, 256), BF16),
            shape((4, 4, 256, 256), BF16),
        ],
        in_specs=[SMEM] * 2 + [HBM] * 4 + [VMEM],
        out_specs=[HBM] * 3,
        scratch_shapes=[
            pltpu.SMEM((QUERY_RUNS,), jnp.int32),
            pltpu.SMEM((QUERY_RUNS,), jnp.int32),
            pltpu.SMEM((QUERY_RUNS,), jnp.int32),
            pltpu.SMEM((KEY_RUNS,), jnp.int32),
            pltpu.SMEM((KEY_RUNS,), jnp.int32),
            pltpu.SMEM((KEY_RUNS,), jnp.int32),
            pltpu.VMEM((8, 128), jnp.int32),
            pltpu.SMEM((8, 128), jnp.int32),
            pltpu.VMEM((QUERY_ROWS, 1024), BF16),
            pltpu.VMEM((QUERY_ROWS, 1024), BF16),
            pltpu.VMEM((KEYS, 256), BF16),
            pltpu.VMEM((KEYS, 256), BF16),
            pltpu.VMEM((QUERY_ROWS, 16), F32),
            pltpu.VMEM((QUERY_ROWS, 1024), BF16),
            pltpu.VMEM((KEYS, 256), BF16),
            pltpu.VMEM((KEYS, 256), BF16),
            pltpu.VMEM((GROUPS, rows, HEAD), BF16),
            pltpu.VMEM((GROUPS, rows, HEAD), BF16),
            pltpu.VMEM((GROUPS, HEAD, rows), BF16),
            pltpu.VMEM((GROUPS, HEAD, rows), BF16),
            pltpu.VMEM((GROUPS, rows, 1), F32),
            pltpu.VMEM((GROUPS, rows, 1), F32),
            pltpu.VMEM((GROUPS, rows, HEAD), F32),
            pltpu.VMEM((GROUPS, HEAD, KEYS), F32),
            pltpu.VMEM((GROUPS, HEAD, KEYS), F32),
            pltpu.SemaphoreType.DMA((5,)),
            pltpu.SemaphoreType.DMA((3,)),
        ],
        compiler_params=pltpu.CompilerParams(vmem_limit_bytes=60 * 2**20),
    )(pq, pk, qg, dog, kg, vg, sg)


def reduce_kernel(hidden, dqp, dkp, dvp, dq, *rest):
    rest = list(rest)

    def take(n):
        taken, rest[:n] = rest[:n], []
        return taken

    wg = take(6)
    h_twin, ht, dkv, dq_sums, dk_sums, dv_sums = take(6)
    dq_bufs, dq_own = take(3), take(1)[0]
    term_bufs = [take(5) for _ in range(4)]
    part_bufs = [take(9) for _ in range(6)]
    send_sems, recv_sems, own_sems = rest
    place = Place()
    net = Net(place, send_sems, recv_sems)
    c = place.c
    twin = place.device(other=True)
    loads = []
    for src, dst in ((dkp, dk_sums), (dvp, dv_sums), (dqp, dq_sums)):
        loads.append(pltpu.make_async_copy(src, dst, own_sems.at[len(loads)]))
        loads[-1].start()
    net.greet()
    rows = pl.ds(pl.multiple_of(c * 128, 128), 128)
    theirs = pl.ds(pl.multiple_of((1 - c) * 128, 128), 128)
    done = set()

    def loaded(i):
        if i not in done:
            loads[i].wait()
            done.add(i)

    def queries_chain():
        first = net.scatter("L", dqp, dq_sums, lambda slot, part: (slot, part), 256, *dq_bufs, dq_own)
        next(first)
        yield
        loaded(2)
        yield from first
        columns = pl.ds(pl.multiple_of(c * 1024, 1024), 1024)
        copy = net.send(dq_own.at[theirs], dq.at[:, columns], twin)
        own = pltpu.make_async_copy(dq_own.at[rows], dq.at[:, columns], own_sems.at[3])
        own.start()
        yield
        own.wait()
        copy.wait_recv()

    def terms_chain(batch, g):
        hbm, sums = ((dkp, dk_sums), (dvp, dv_sums))[batch]
        relay, up, down, mid, inbox = term_bufs[batch * 2 + g]
        axes = AXES[batch][g]
        columns = pl.ds(g * HEAD, HEAD)

        def at(slot, part):
            outer = axes[0] == ("y", "M")[batch]
            return ((slot, part) if outer else (part, slot)) + (slice(None), columns)

        first = net.scatter(axes[0], hbm, sums, at, 4, relay, up, down, mid)
        next(first)
        yield
        loaded(batch)
        yield from first
        out = dkv.at[:, pl.ds(batch * 256 + g * HEAD, HEAD)]
        yield from net.scatter_direct(axes[1], mid, inbox, out)
        done.add(("terms", batch, g))

    def hidden_chain():
        copy = net.send(hidden, h_twin, twin)
        yield
        copy.wait_recv()
        ht[:, 0:128] = jnp.where(c == 0, hidden[...], h_twin[...]).T
        ht[:, 128:256] = jnp.where(c == 0, h_twin[...], hidden[...]).T
        done.add("hidden")

    def project_chain(batch):
        while not {("terms", batch, 0), ("terms", batch, 1), "hidden"} <= done:
            yield

        def project(i, _):
            xi, yi = lax.div(i, 4), lax.rem(i, 4)
            block = pl.ds(pl.multiple_of(i * 256, 256), 256)
            term = dot(ht[block, :], dkv[:, batch * 256 : batch * 256 + 256], NN).astype(BF16)
            for zi in range(4):
                at = {"x": xi, "y": yi, "z": zi}
                for p, tiles in enumerate(PARTS[batch]):
                    o = [at[axis] for axis in ORDERS[p]]
                    for u, (row, column) in enumerate(tiles):
                        r0, c0 = zi * 64 + row * 16, column * 128
                        part_bufs[batch * 3 + p][0][o[0], o[1], o[2], u] = term[r0 : r0 + 16, c0 : c0 + 128]
            return 0

        lax.fori_loop(0, 16, project, 0)
        done.add(("project", batch))

    def part_chain(batch, p):
        while ("project", batch) not in done:
            yield
        order, whole = ORDERS[p], wg[batch * 3 + p]
        terms, relay, up, down, mid, inbox, mid2, inbox2, total = part_bufs[batch * 3 + p]
        at = [place.at[axis] for axis in order]
        yield from net.scatter(
            order[0], terms, terms, lambda slot, part: (slot, part), 4, relay, up, down, mid
        )
        yield from net.scatter_direct(order[1], mid, inbox, mid2)
        yield from net.scatter_direct(order[2], mid2, inbox2, total)
        mine = whole.at[c]
        own = pltpu.make_async_copy(total, mine.at[at[0], at[1], at[2]], own_sems.at[4 + batch * 3 + p])
        own.start()
        own.wait()
        copies = net.cast(order[2], mine.at[at[0], at[1], at[2]])
        yield
        for copy in copies:
            copy.wait_recv()
        copies = net.cast(order[1], mine.at[at[0], at[1]])
        yield
        for copy in copies:
            copy.wait_recv()

        def ref(slot, part):
            return mine.at[slot, part]

        def share(slot):
            return net.send(mine.at[slot], mine.at[slot], twin)

        pair = net.pair(order[0], mine.at[at[0]], mine.at[at[0]])
        shares = [share(at[0])]
        yield
        relays = net.relay(order[0], pair, ref, 4)
        shares += [share(wrap(at[0] - 1)), share(wrap(at[0] + 1))]
        yield
        for copy in relays:
            copy.wait_recv()
        shares.append(share(wrap(at[0] + 2)))
        yield
        for copy in shares:
            copy.wait_recv()

    chains = []
    for batch in range(2):
        chains += [terms_chain(batch, g) for g in range(GROUPS)]
        chains += [hidden_chain()] if batch == 0 else []
        chains += [project_chain(batch)] + [part_chain(batch, p) for p in range(3)]
    together(*chains, late(1, queries_chain()))
    net.finish()


def reduce_all(hidden, dqp, dkp, dvp):
    shape = jax.ShapeDtypeStruct

    def buf(*dims, dtype=BF16):
        return pltpu.VMEM(dims, dtype)

    scratch = [buf(128, 4096), buf(4096, 256), buf(256, 512)]
    scratch += [buf(4, 256, 1024), buf(4, 4, 256, 256), buf(4, 4, 256, 256)]
    scratch += [buf(256, 1024)] * 4
    for _ in range(4):
        scratch += [buf(4, 256, HEAD)] * 4 + [buf(3, 256, HEAD)]
    for n in SIZES:
        scratch += [buf(4, 4, 4, n, 16, 128)]
        scratch += [buf(4, 4, n, 16, 128)] * 4 + [buf(3, 4, n, 16, 128)]
        scratch += [buf(4, n, 16, 128, dtype=F32), buf(3, n, 16, 128, dtype=F32)]
        scratch += [buf(n, 16, 128)]
    return pl.pallas_call(
        reduce_kernel,
        out_shape=[shape((128, 2048), BF16)]
        + [shape((2, 4, 4, 4, n, 16, 128), BF16) for n in SIZES],
        in_specs=[VMEM] + [HBM] * 3,
        out_specs=[VMEM] + [HBM] * 6,
        scratch_shapes=scratch
        + [
            pltpu.SemaphoreType.DMA((200,)),
            pltpu.SemaphoreType.DMA((200,)),
            pltpu.SemaphoreType.DMA((10,)),
        ],
        compiler_params=pltpu.CompilerParams(
            collective_id=1, has_side_effects=True, vmem_limit_bytes=60 * 2**20
        ),
    )(hidden, dqp, dkp, dvp)


def widen_kernel(*refs):
    parts, (wk, wv), held, (wk_v, wv_v), (in_sems, out_sems) = (
        refs[0:6], refs[6:8], refs[8:14], refs[14:16], refs[16:18]
    )

    def at(p, x, y, z):
        places = {"x": x, "y": y, "z": z}
        return tuple(places[axis] for axis in ORDERS[p % 3])

    def loads(i):
        x, y = lax.div(i, 4), lax.rem(i, 4)
        spots = [(slice(None),) + at(p, x, y, slice(None)) for p in range(6)]
        return [
            pltpu.make_async_copy(parts[p].at[spot], held[p].at[spot], in_sems.at[p, i])
            for p, spot in enumerate(spots)
        ]

    def stores(i):
        rows = pl.ds(pl.multiple_of(i * 256, 256), 256)
        return [
            pltpu.make_async_copy(src.at[rows], dst.at[rows], out_sems.at[n, i])
            for n, (src, dst) in enumerate(((wk_v, wk), (wv_v, wv)))
        ]

    def begin(i, _):
        for copy in loads(i):
            copy.start()
        return 0

    def block(i, _):
        x, y = lax.div(i, 4), lax.rem(i, 4)
        for copy in loads(i):
            copy.wait()
        for z in range(4):
            r0 = pl.multiple_of(i * 256 + z * 64, 64)
            for core in range(2):
                for p in range(6):
                    out = wk_v if p < 3 else wv_v
                    for u, (row, column) in enumerate(PARTS[p // 3][p % 3]):
                        value = held[p][(core,) + at(p, x, y, z) + (u,)]
                        c0 = core * 256 + column * 128
                        out[pl.ds(r0 + row * 16, 16), c0 : c0 + 128] = value.astype(F32)
        for copy in stores(i):
            copy.start()
        return 0

    def end(i, _):
        for copy in stores(i):
            copy.wait()
        return 0

    lax.fori_loop(0, 16, begin, 0)
    lax.fori_loop(0, 16, block, 0)
    lax.fori_loop(0, 16, end, 0)


def widen(*parts):
    shape = jax.ShapeDtypeStruct
    return pl.pallas_call(
        widen_kernel,
        out_shape=[shape((4096, 512), F32)] * 2,
        in_specs=[HBM] * 6,
        out_specs=[HBM] * 2,
        scratch_shapes=[pltpu.VMEM((2, 4, 4, 4, n, 16, 128), BF16) for n in SIZES]
        + [
            pltpu.VMEM((4096, 512), F32),
            pltpu.VMEM((4096, 512), F32),
            pltpu.SemaphoreType.DMA((6, 16)),
            pltpu.SemaphoreType.DMA((2, 16)),
        ],
        compiler_params=pltpu.CompilerParams(vmem_limit_bytes=60 * 2**20),
    )(*parts)


def local(hidden, q, k, v, ao, do, lse, pos):
    qg, dog, kg, vg, sg, pq, pk = gather_all(q, do, k, v, ao, lse.T, pos[None, :])
    dqp, dkp, dvp = attend(pq, pk, qg, dog, kg, vg, sg)
    dq, *parts = reduce_all(hidden, dqp, dkp, dvp)
    wk, wv = widen(*parts)
    return dq, wk, wv


def solution(mesh):
    rows = P(("inner", "outer"), None)
    return jax.shard_map(
        local,
        mesh=mesh,
        in_specs=(rows,) * 7 + (P(("inner", "outer")),),
        out_specs=(rows, P(), P()),
        check_vma=False,
    )
```

```python
import functools
import math

import jax
import jax.numpy as jnp
from jax import lax
from jax.experimental import pallas as pl
from jax.experimental.pallas import tpu as pltpu
from jax.sharding import PartitionSpec as P

HEAD = 128
GROUPS = 2
SHARE = 4
RUN = 64
KEYS = 4096
KEY_RUNS = KEYS // RUN
QUERY_ROWS = 1024
QUERY_RUNS = QUERY_ROWS // RUN
UNIT = 2
CHUNK = 512
SCALE = HEAD**-0.5
LOG2E = math.log2(math.e)
F32 = jnp.float32
BF16 = jnp.bfloat16
MESH = pl.DeviceIdType.MESH
NT = (((1,), (1,)), ((), ()))
NN = (((1,), (0,)), ((), ()))
VMEM = pl.BlockSpec(memory_space=pltpu.VMEM)
SMEM = pl.BlockSpec(memory_space=pltpu.SMEM)
HBM = pl.BlockSpec(memory_space=pltpu.HBM)
ORDERS = ("zxy", "xyz", "yzx")
PARTS = (
    (((0, 0), (0, 1), (3, 0)), ((1, 0), (1, 1), (3, 1)), ((2, 0), (2, 1))),
    (((0, 0), (0, 1), (3, 0)), ((1, 0), (1, 1)), ((2, 0), (2, 1), (3, 1))),
)
AXES = ((("y", "M"), ("M", "y")), (("M", "y"), ("M", "y")))
SIZES = [len(tiles) for batch in PARTS for tiles in batch]


def dot(a, b, dims):
    return lax.dot_general(a, b, dims, preferred_element_type=F32)


def wrap(value):
    return lax.rem(value + 4, 4)


class Place:
    def __init__(self):
        inner, outer = lax.axis_index("inner"), lax.axis_index("outer")
        c = lax.rem(inner, 2)
        x = lax.div(inner, 8) * 2 + lax.div(outer, 4)
        y = lax.rem(lax.div(inner, 2), 4)
        z = lax.rem(outer, 4)
        self.c = c
        self.at = {"x": x, "y": y, "z": z, "L": z + c * (x - z), "M": x + c * (z - x)}
        self.step = {"x": (1, 0, 0), "y": (0, 1, 0), "z": (0, 0, 1), "L": (c, 0, 1 - c), "M": (1 - c, 0, c)}

    def device(self, axis=None, by=0, other=False):
        step = (0, 0, 0) if axis is None else self.step[axis]
        x, y, z = (wrap(self.at[name] + by * d) for name, d in zip("xyz", step))
        c = 1 - self.c if other else self.c
        return ((lax.div(x, 2) * 4 + y) * 2 + c, lax.rem(x, 2) * 4 + z)

    def beside(self):
        near = [self.device(axis, by) for axis in "xyz" for by in (1, -1, 2)]
        return near + [self.device(other=True)]


class Net:
    def __init__(self, place, send_sems, recv_sems):
        self.place, self.send_sems, self.recv_sems = place, send_sems, recv_sems
        self.sent = []

    def greet(self):
        barrier = pltpu.get_barrier_semaphore()
        near = self.place.beside()
        for device in near:
            pl.semaphore_signal(barrier, inc=1, device_id=device, device_id_type=MESH)
        pl.semaphore_wait(barrier, len(near))

    def send(self, src, dst, device):
        k = len(self.sent)
        assert k < self.send_sems.shape[0]
        copy = pltpu.make_async_remote_copy(
            src_ref=src,
            dst_ref=dst,
            send_sem=self.send_sems.at[k],
            recv_sem=self.recv_sems.at[k],
            device_id=device,
            device_id_type=MESH,
        )
        copy.start()
        self.sent.append(copy)
        return copy

    def finish(self):
        for copy in self.sent:
            copy.wait_send()

    def pair(self, axis, src, dst):
        return [self.send(src, dst, self.place.device(axis, by)) for by in (1, -1)]

    def relay(self, axis, pair, ref, n):
        s = self.place.at[axis]
        low, high = pl.ds(0, n // 2), pl.ds(n // 2, n - n // 2)
        pair[0].wait_recv()
        block = ref(wrap(s - 1), low)
        up = self.send(block, block, self.place.device(axis, 1))
        pair[1].wait_recv()
        block = ref(wrap(s + 1), high)
        return [up, self.send(block, block, self.place.device(axis, -1))]

    def cast(self, axis, block):
        return [self.send(block, block, self.place.device(axis, by)) for by in (1, -1, 2)]

    def scatter(self, axis, hbm, buf, at, n, relay, from_behind, from_ahead, out):
        s = self.place.at[axis]
        ahead, behind = self.place.device(axis, 1), self.place.device(axis, -1)
        h = n // 2
        low, high, whole = pl.ds(0, h), pl.ds(h, n - h), pl.ds(0, n)
        far, left, right = wrap(s + 2), wrap(s - 1), wrap(s + 1)
        relay_up = self.send(hbm.at[at(far, low)], relay.at[low], ahead)
        relay_down = self.send(hbm.at[at(far, high)], relay.at[high], behind)
        up_high = self.send(hbm.at[at(right, high)], from_behind.at[high], ahead)
        down_low = self.send(hbm.at[at(left, low)], from_ahead.at[low], behind)
        yield
        relay_up.wait_recv()
        spot = at(right, low)
        buf[spot] = (buf[spot].astype(F32) + relay[low].astype(F32)).astype(BF16)
        up_low = self.send(buf.at[spot], from_behind.at[low], ahead)
        relay_down.wait_recv()
        spot = at(left, high)
        buf[spot] = (buf[spot].astype(F32) + relay[high].astype(F32)).astype(BF16)
        down_high = self.send(buf.at[spot], from_ahead.at[high], behind)
        yield
        for copy in (up_high, down_low, up_low, down_high):
            copy.wait_recv()
        out[...] = (
            buf[at(s, whole)].astype(F32) + from_behind[...].astype(F32) + from_ahead[...].astype(F32)
        ).astype(out.dtype)

    def scatter_direct(self, axis, buf, inbox, out):
        s = self.place.at[axis]
        copies = [
            self.send(buf.at[wrap(s + by)], inbox.at[i], self.place.device(axis, by))
            for i, by in enumerate((1, -1, 2))
        ]
        yield
        for copy in copies:
            copy.wait_recv()
        out[...] = (
            buf[s].astype(F32)
            + inbox[0].astype(F32)
            + inbox[1].astype(F32)
            + inbox[2].astype(F32)
        ).astype(out.dtype)


def late(rounds, chain):
    for _ in range(rounds):
        yield
    yield from chain


def together(*chains):
    chains = list(chains)
    while chains:
        for chain in list(chains):
            try:
                next(chain)
            except StopIteration:
                chains.remove(chain)


def gather_kernel(
    q, do, k, v, ao, lse, pos, qg, dog, kg, vg, sg, pq, pk, do_v, ao_v, stats, mine, send_sems, recv_sems, own_sems
):
    place = Place()
    net = Net(place, send_sems, recv_sems)
    y, c, l, m = place.at["y"], place.c, place.at["L"], place.at["M"]
    twin = place.device(other=True)
    loads = [
        pltpu.make_async_copy(src, dst, own_sems.at[7 + n]) for n, (src, dst) in enumerate(((do, do_v), (ao, ao_v)))
    ]
    for copy in loads:
        copy.start()
    net.greet()
    first, second = (pl.multiple_of(i * 128, 128) for i in (c, 1 - c))

    def cut(columns):
        return [pl.ds(pl.multiple_of(i * columns, columns), columns) for i in (c, 1 - c)]

    wide, thin = cut(1024), cut(256)
    owns = []

    def keep(src, dst):
        copy = pltpu.make_async_copy(src, dst, own_sems.at[len(owns)])
        copy.start()
        owns.append(copy)
        return copy

    def queries_chain(src, buf):
        def block(start):
            return lambda slot, rows: buf.at[slot, pl.ds(start + rows.start, rows.size)]

        whole = pl.ds(0, 128)
        mine_at, twin_at = block(first), block(second)
        from_twin = net.send(src.at[:, wide[1]], buf.at[m, pl.ds(first, 128)], twin)
        pair = net.pair("L", src.at[:, wide[0]], mine_at(l, whole))
        own = keep(src.at[:, wide[0]], mine_at(l, whole))
        yield
        from_twin.wait_recv()
        pair2 = net.pair("L", twin_at(l, whole), twin_at(l, whole))
        yield
        relays = net.relay("L", pair, mine_at, 128)
        yield
        relays += net.relay("L", pair2, twin_at, 128)
        yield
        for copy in relays:
            copy.wait_recv()
        own.wait()

    def keys_chain(src, buf, a, b):
        i, j = place.at[a], place.at[b]
        whole = pl.ds(0, 128)

        def block(start):
            return lambda slot, rows: buf.at[j, slot, pl.ds(start + rows.start, rows.size)]

        def chip(slot):
            return lambda other, rows: buf.at[other, slot, rows]

        def pair_b(slot):
            return (slot, net.pair(b, buf.at[j, slot], buf.at[j, slot]))

        mine_at, twin_at = block(first), block(second)
        there = buf.at[y, l] if a == "M" else buf.at[l, y]
        from_twin = net.send(src.at[:, thin[1]], there.at[pl.ds(first, 128)], twin)
        pair = net.pair(a, src.at[:, thin[0]], mine_at(i, whole))
        own = keep(src.at[:, thin[0]], mine_at(i, whole))
        yield
        from_twin.wait_recv()
        pair2 = net.pair(a, twin_at(i, whole), twin_at(i, whole))
        own.wait()
        pairs = [pair_b(i)]
        yield
        relays = net.relay(a, pair, mine_at, 128)
        yield
        relays += net.relay(a, pair2, twin_at, 128)
        pairs += [pair_b(wrap(i - 1)), pair_b(wrap(i + 1))]
        yield
        for copy in relays:
            copy.wait_recv()
        pairs.append(pair_b(wrap(i + 2)))
        yield
        relays = []
        for slot, both in pairs:
            relays += net.relay(b, both, chip(slot), 256)
        yield
        for copy in relays:
            copy.wait_recv()

    def stats_chain():
        kept = [keep(pos, pk.at[y, m, c]), keep(pos, pq.at[l, c])]
        from_twin = [net.send(pos, pk.at[y, l, c], twin), net.send(pos, pq.at[m, c], twin)]
        for copy in loads:
            copy.wait()
        for h in range(16):
            columns = slice(h * HEAD, (h + 1) * HEAD)
            product = do_v[:, columns].astype(F32) * ao_v[:, columns].astype(F32)
            stats[:, h : h + 1] = jnp.sum(product, axis=1, keepdims=True)
        turned = stats[...].T
        for i in range(2):
            mine[i, 0:8, :] = lse[i * 8 : i * 8 + 8] * LOG2E
            mine[i, 8:16, :] = turned[i * 8 : i * 8 + 8]
        from_twin.append(net.send(mine.at[1 - c], sg.at[m, c], twin))
        kept.append(keep(mine.at[c], sg.at[l, c]))
        yield
        for copy in kept:
            copy.wait()
        for copy in from_twin:
            copy.wait_recv()
        places = net.cast("M", pk.at[y, m])
        rest = net.cast("L", sg.at[l]) + net.cast("L", pq.at[l])
        yield
        for copy in places:
            copy.wait_recv()
        rest += net.cast("y", pk.at[y])
        yield
        yield
        for copy in rest:
            copy.wait_recv()

    together(
        keys_chain(k, kg, "M", "y"),
        keys_chain(v, vg, "y", "M"),
        queries_chain(q, qg),
        late(2, queries_chain(do, dog)),
        stats_chain(),
    )
    net.finish()


def gather_all(q, do, k, v, ao, lse, pos):
    shape = jax.ShapeDtypeStruct
    return pl.pallas_call(
        gather_kernel,
        out_shape=[
            shape((4, 256, 1024), BF16),
            shape((4, 256, 1024), BF16),
            shape((4, 4, 256, 256), BF16),
            shape((4, 4, 256, 256), BF16),
            shape((4, 2, 16, 128), F32),
            shape((4, 2, 1, 128), jnp.int32),
            shape((4, 4, 2, 1, 128), jnp.int32),
        ],
        in_specs=[HBM] * 5 + [VMEM] * 2,
        out_specs=[HBM] * 7,
        scratch_shapes=[
            pltpu.VMEM((128, 2048), BF16),
            pltpu.VMEM((128, 2048), BF16),
            pltpu.VMEM((128, 128), F32),
            pltpu.VMEM((2, 16, 128), F32),
            pltpu.SemaphoreType.DMA((83,)),
            pltpu.SemaphoreType.DMA((83,)),
            pltpu.SemaphoreType.DMA((9,)),
        ],
        compiler_params=pltpu.CompilerParams(
            collective_id=0, has_side_effects=True, vmem_limit_bytes=60 * 2**20
        ),
    )(q, do, k, v, ao, lse, pos)


def attend_kernel(
    pq, pk, qg, dog, kg, vg, sg, dqp, dkp, dvp, order, reach, qplace, rank, origin, kplace, found, found_s,
    q_all, do_all, k_all, v_all, columns, dq_all, dk_all, dv_all,
    qs, dos, qt, dot_, lse_s, delta_s, dq_sum, dk_sum, dv_sum, in_sems, out_sems,
):
    rows = UNIT * SHARE * RUN

    def at_run(ref, j, first):
        a, b, r = lax.div(j, 16), lax.rem(lax.div(j, 4), 4), lax.rem(j, 4)
        part = pl.ds(pl.multiple_of(r * RUN, RUN), RUN)
        return ref.at[a, b, part] if first else ref.at[b, a, part]

    def key_copies(j):
        spot = pl.ds(pl.multiple_of(rank[j] * RUN, RUN), RUN)
        return (
            pltpu.make_async_copy(at_run(kg, j, True), k_all.at[spot], in_sems.at[0]),
            pltpu.make_async_copy(at_run(vg, j, False), v_all.at[spot], in_sems.at[1]),
        )

    def query_copies(r):
        i = order[r]
        part = pl.ds(pl.multiple_of(lax.rem(i, 4) * RUN, RUN), RUN)
        spot = pl.ds(pl.multiple_of(r * RUN, RUN), RUN)
        return (
            pltpu.make_async_copy(qg.at[lax.div(i, 4), part], q_all.at[spot], in_sems.at[2]),
            pltpu.make_async_copy(dog.at[lax.div(i, 4), part], do_all.at[spot], in_sems.at[3]),
        )

    def start(make):
        def body(i, _):
            for copy in make(i):
                copy.start()
            return 0

        return body

    def query_place(i):
        return pq[lax.div(i, 4), lax.rem(lax.div(i, 2), 2), 0, lax.rem(i, 2) * RUN]

    def key_place(j):
        c = lax.rem(lax.div(j, 2), 2)
        return pk[lax.div(j, 16), lax.rem(lax.div(j, 4), 4), c, 0, lax.rem(j, 2) * RUN]

    lane = lax.broadcasted_iota(jnp.int32, (1, 128), 1)
    blank = jnp.zeros((1, 128), jnp.int32)
    query_row = lax.fori_loop(
        0, QUERY_RUNS, lambda i, row: jnp.where(lane == i, query_place(i), row), blank, unroll=True
    )
    key_row = lax.fori_loop(
        0, KEY_RUNS, lambda j, row: jnp.where(lane == j, key_place(j), row), blank, unroll=True
    )

    def count_queries(i, total):
        return total + jnp.where(query_place(i) < query_row, 1, 0)

    def count_keys(j, totals):
        place = key_place(j)
        return (
            totals[0] + jnp.where(place < key_row, 1, 0),
            totals[1] + jnp.where(place <= query_row, 1, 0),
        )

    found[0:1, :] = lax.fori_loop(0, QUERY_RUNS, count_queries, blank, unroll=True)
    key_rank, query_reach = lax.fori_loop(0, KEY_RUNS, count_keys, (blank, blank), unroll=True)
    found[1:2, :] = query_reach
    found[2:3, :] = key_rank
    copy = pltpu.make_async_copy(found, found_s, in_sems.at[4])
    copy.start()
    for z in range(4):
        for c in range(2):
            spot = (z * 2 + c) * 128
            columns[spot : spot + 128, 0:16] = sg[z, c].T
    copy.wait()

    def place_query(i, _):
        r = found_s[0, i]
        order[r] = i
        reach[r] = found_s[1, i]
        qplace[r] = query_place(i)
        return 0

    def place_key(j, _):
        rank[j] = found_s[2, j]
        origin[found_s[2, j]] = j
        kplace[found_s[2, j]] = key_place(j)
        return 0

    lax.fori_loop(0, QUERY_RUNS, place_query, 0)
    lax.fori_loop(0, QUERY_RUNS, start(query_copies), 0)
    lax.fori_loop(0, KEY_RUNS, place_key, 0)
    lax.fori_loop(0, KEY_RUNS, start(key_copies), 0)
    dk_sum[...] = jnp.zeros_like(dk_sum)
    dv_sum[...] = jnp.zeros_like(dv_sum)
    pltpu.make_async_copy(q_all, q_all, in_sems.at[2]).wait()
    pltpu.make_async_copy(do_all, do_all, in_sems.at[3]).wait()
    pltpu.make_async_copy(k_all, k_all, in_sems.at[0]).wait()
    pltpu.make_async_copy(v_all, v_all, in_sems.at[1]).wait()

    per = CHUNK // RUN

    def query_back(r):
        i = order[r]
        part = pl.ds(pl.multiple_of(lax.rem(i, 4) * RUN, RUN), RUN)
        spot = pl.ds(pl.multiple_of(r * RUN, RUN), RUN)
        return (pltpu.make_async_copy(dq_all.at[spot], dqp.at[lax.div(i, 4), part], out_sems.at[0]),)

    def key_back(r):
        j = origin[r]
        spot = pl.ds(pl.multiple_of(r * RUN, RUN), RUN)
        return (
            pltpu.make_async_copy(dk_all.at[spot], at_run(dkp, j, True), out_sems.at[1]),
            pltpu.make_async_copy(dv_all.at[spot], at_run(dvp, j, False), out_sems.at[2]),
        )

    def unit(i, _):
        for u in range(UNIT):
            r = i * UNIT + u
            r0 = pl.multiple_of(r * RUN, RUN)
            s0 = pl.multiple_of(order[r] * RUN, RUN)
            for g in range(GROUPS):
                for h in range(SHARE):
                    head = g * SHARE + h
                    o = (u * SHARE + h) * RUN
                    spot = pl.ds(o, RUN)
                    qs[g, spot, :] = q_all[pl.ds(r0, RUN), head * HEAD : (head + 1) * HEAD]
                    dos[g, spot, :] = do_all[pl.ds(r0, RUN), head * HEAD : (head + 1) * HEAD]
                    lse_s[g, spot, :] = columns[pl.ds(s0, RUN), head : head + 1]
                    delta_s[g, spot, :] = columns[pl.ds(s0, RUN), 8 + head : 9 + head]
        for g in range(GROUPS):
            qt[g] = qs[g].T
            dot_[g] = dos[g].T
        dq_sum[...] = jnp.zeros_like(dq_sum)
        first, last = reach[i * UNIT], reach[i * UNIT + UNIT - 1]
        whole = lax.div(first - 1, per)
        rest = lax.rem(last, per)
        chunks = lax.div(last, per) + jnp.where(rest > per // 2, 1, 0)
        halves = jnp.where((rest > 0) & (rest <= per // 2), 1, 0)

        def step(masked, size, base, chunk, _):
            r0 = base + chunk * (size // RUN)
            keys = pl.ds(pl.multiple_of(r0 * RUN, size), size)
            if masked:
                row = lax.broadcasted_iota(jnp.int32, (rows, 1), 0)
                qpos = lax.rem(row, RUN)
                for u in range(UNIT):
                    inside = lax.div(row, SHARE * RUN) == u
                    qpos = qpos + jnp.where(inside, qplace[i * UNIT + u], 0)
                column = lax.broadcasted_iota(jnp.int32, (1, size), 1)
                kpos = lax.rem(column, RUN)
                for u in range(size // RUN):
                    kpos = kpos + jnp.where(lax.div(column, RUN) == u, kplace[r0 + u], 0)
                allowed = kpos <= qpos
            for g in range(GROUPS):
                kk = k_all[keys, g * HEAD : (g + 1) * HEAD]
                vv = v_all[keys, g * HEAD : (g + 1) * HEAD]
                probs = jnp.exp2(dot(qs[g], kk, NT) * (SCALE * LOG2E) - lse_s[g])
                if masked:
                    probs = jnp.where(allowed, probs, 0.0)
                dprobs = dot(dos[g], vv, NT)
                dscores = (probs * (dprobs - delta_s[g])).astype(BF16)
                dq_sum[g] += dot(dscores, kk, NN)
                dv_sum[g, :, keys] += dot(dot_[g], probs.astype(BF16), NN)
                dk_sum[g, :, keys] += dot(qt[g], dscores, NN)
            return 0

        lax.fori_loop(0, whole, functools.partial(step, False, CHUNK, 0), 0)
        lax.fori_loop(whole, chunks, functools.partial(step, True, CHUNK, 0), 0)
        lax.fori_loop(0, halves, functools.partial(step, True, CHUNK // 2, chunks * per), 0)
        for u in range(UNIT):
            r0 = pl.multiple_of((i * UNIT + u) * RUN, RUN)
            for g in range(GROUPS):
                for h in range(SHARE):
                    head = g * SHARE + h
                    o = (u * SHARE + h) * RUN
                    dq_all[pl.ds(r0, RUN), head * HEAD : (head + 1) * HEAD] = (
                        dq_sum[g, o : o + RUN, :] * SCALE
                    ).astype(BF16)
            for copy in query_back(i * UNIT + u):
                copy.start()
        return 0

    lax.fori_loop(0, QUERY_RUNS // UNIT, unit, 0)

    def turn(chunk, _):
        keys = pl.ds(pl.multiple_of(chunk * CHUNK, CHUNK), CHUNK)
        for g in range(GROUPS):
            columns_g = slice(g * HEAD, (g + 1) * HEAD)
            dk_all[keys, columns_g] = (dk_sum[g, :, keys] * SCALE).astype(BF16).T
            dv_all[keys, columns_g] = dv_sum[g, :, keys].astype(BF16).T
        for u in range(per):
            for copy in key_back(chunk * per + u):
                copy.start()
        return 0

    lax.fori_loop(0, KEYS // CHUNK, turn, 0)
    pltpu.make_async_copy(dq_all, dq_all, out_sems.at[0]).wait()
    pltpu.make_async_copy(dk_all, dk_all, out_sems.at[1]).wait()
    pltpu.make_async_copy(dv_all, dv_all, out_sems.at[2]).wait()


def attend(pq, pk, qg, dog, kg, vg, sg):
    shape = jax.ShapeDtypeStruct
    rows = UNIT * SHARE * RUN
    return pl.pallas_call(
        attend_kernel,
        out_shape=[
            shape((4, 256, 1024), BF16),
            shape((4, 4, 256, 256), BF16),
            shape((4, 4, 256, 256), BF16),
        ],
        in_specs=[SMEM] * 2 + [HBM] * 4 + [VMEM],
        out_specs=[HBM] * 3,
        scratch_shapes=[
            pltpu.SMEM((QUERY_RUNS,), jnp.int32),
            pltpu.SMEM((QUERY_RUNS,), jnp.int32),
            pltpu.SMEM((QUERY_RUNS,), jnp.int32),
            pltpu.SMEM((KEY_RUNS,), jnp.int32),
            pltpu.SMEM((KEY_RUNS,), jnp.int32),
            pltpu.SMEM((KEY_RUNS,), jnp.int32),
            pltpu.VMEM((8, 128), jnp.int32),
            pltpu.SMEM((8, 128), jnp.int32),
            pltpu.VMEM((QUERY_ROWS, 1024), BF16),
            pltpu.VMEM((QUERY_ROWS, 1024), BF16),
            pltpu.VMEM((KEYS, 256), BF16),
            pltpu.VMEM((KEYS, 256), BF16),
            pltpu.VMEM((QUERY_ROWS, 16), F32),
            pltpu.VMEM((QUERY_ROWS, 1024), BF16),
            pltpu.VMEM((KEYS, 256), BF16),
            pltpu.VMEM((KEYS, 256), BF16),
            pltpu.VMEM((GROUPS, rows, HEAD), BF16),
            pltpu.VMEM((GROUPS, rows, HEAD), BF16),
            pltpu.VMEM((GROUPS, HEAD, rows), BF16),
            pltpu.VMEM((GROUPS, HEAD, rows), BF16),
            pltpu.VMEM((GROUPS, rows, 1), F32),
            pltpu.VMEM((GROUPS, rows, 1), F32),
            pltpu.VMEM((GROUPS, rows, HEAD), F32),
            pltpu.VMEM((GROUPS, HEAD, KEYS), F32),
            pltpu.VMEM((GROUPS, HEAD, KEYS), F32),
            pltpu.SemaphoreType.DMA((5,)),
            pltpu.SemaphoreType.DMA((3,)),
        ],
        compiler_params=pltpu.CompilerParams(vmem_limit_bytes=60 * 2**20),
    )(pq, pk, qg, dog, kg, vg, sg)


def reduce_kernel(hidden, dqp, dkp, dvp, dq, *rest):
    rest = list(rest)

    def take(n):
        taken, rest[:n] = rest[:n], []
        return taken

    wg = take(6)
    h_own, h_twin, ht, dkv, dq_sums, dk_sums, dv_sums = take(7)
    dq_bufs, dq_own = take(3), take(1)[0]
    term_bufs = [take(5) for _ in range(4)]
    part_bufs = [take(8) for _ in range(6)]
    held = take(6)
    send_sems, recv_sems, own_sems = rest
    place = Place()
    net = Net(place, send_sems, recv_sems)
    c = place.c
    twin = place.device(other=True)
    loads = []
    for src, dst in ((dkp, dk_sums), (dvp, dv_sums), (dqp, dq_sums), (hidden, h_own)):
        loads.append(pltpu.make_async_copy(src, dst, own_sems.at[len(loads)]))
        loads[-1].start()
    net.greet()
    rows = pl.ds(pl.multiple_of(c * 128, 128), 128)
    theirs = pl.ds(pl.multiple_of((1 - c) * 128, 128), 128)
    done = set()

    def loaded(i):
        if i not in done:
            loads[i].wait()
            done.add(i)

    def queries_chain():
        first = net.scatter("L", dqp, dq_sums, lambda slot, part: (slot, part), 256, *dq_bufs, dq_own)
        next(first)
        yield
        loaded(2)
        yield from first
        columns = pl.ds(pl.multiple_of(c * 1024, 1024), 1024)
        copy = net.send(dq_own.at[theirs], dq.at[:, columns], twin)
        own = pltpu.make_async_copy(dq_own.at[rows], dq.at[:, columns], own_sems.at[16])
        own.start()
        yield
        own.wait()
        copy.wait_recv()

    def terms_chain(batch, g):
        hbm, sums = ((dkp, dk_sums), (dvp, dv_sums))[batch]
        relay, up, down, mid, inbox = term_bufs[batch * 2 + g]
        axes = AXES[batch][g]
        columns = pl.ds(g * HEAD, HEAD)

        def at(slot, part):
            outer = axes[0] == ("y", "M")[batch]
            return ((slot, part) if outer else (part, slot)) + (slice(None), columns)

        first = net.scatter(axes[0], hbm, sums, at, 4, relay, up, down, mid)
        next(first)
        yield
        loaded(batch)
        yield from first
        out = dkv.at[:, pl.ds(batch * 256 + g * HEAD, HEAD)]
        yield from net.scatter_direct(axes[1], mid, inbox, out)
        done.add(("terms", batch, g))

    def hidden_chain():
        copy = net.send(hidden, h_twin, twin)
        yield
        loaded(3)
        copy.wait_recv()
        ht[:, 0:128] = jnp.where(c == 0, h_own[...], h_twin[...]).T
        ht[:, 128:256] = jnp.where(c == 0, h_twin[...], h_own[...]).T
        done.add("hidden")

    def project_chain(batch):
        while not {("terms", batch, 0), ("terms", batch, 1), "hidden"} <= done:
            yield

        def project(i, _):
            xi, yi = lax.div(i, 4), lax.rem(i, 4)
            block = pl.ds(pl.multiple_of(i * 256, 256), 256)
            term = dot(ht[block, :], dkv[:, batch * 256 : batch * 256 + 256], NN).astype(BF16)
            for zi in range(4):
                at = {"x": xi, "y": yi, "z": zi}
                for p, tiles in enumerate(PARTS[batch]):
                    o = [at[axis] for axis in ORDERS[p]]
                    for u, (row, column) in enumerate(tiles):
                        r0, c0 = zi * 64 + row * 16, column * 128
                        part_bufs[batch * 3 + p][0][o[0], o[1], o[2], u] = term[r0 : r0 + 16, c0 : c0 + 128]
            return 0

        lax.fori_loop(0, 16, project, 0)
        done.add(("project", batch))

    def part_chain(batch, p):
        while ("project", batch) not in done:
            yield
        n = batch * 3 + p
        order, whole, out = ORDERS[p], held[n], wg[n]
        terms, relay, up, down, mid, inbox, mid2, inbox2 = part_bufs[n]
        at = [place.at[axis] for axis in order]
        mine = whole.at[c]
        yield from net.scatter(
            order[0], terms, terms, lambda slot, part: (slot, part), 4, relay, up, down, mid
        )
        yield from net.scatter_direct(order[1], mid, inbox, mid2)
        yield from net.scatter_direct(order[2], mid2, inbox2, mine.at[at[0], at[1], at[2]])
        copies = net.cast(order[2], mine.at[at[0], at[1], at[2]])
        yield
        for copy in copies:
            copy.wait_recv()
        copies = net.cast(order[1], mine.at[at[0], at[1]])
        yield
        for copy in copies:
            copy.wait_recv()

        def ref(slot, part):
            return mine.at[slot, part]

        def keep(core, which, slot):
            pltpu.make_async_copy(whole.at[core, slot], out.at[core, slot], own_sems.at[4 + 2 * n + which]).start()

        def share(slot):
            keep(c, 0, slot)
            return slot, net.send(mine.at[slot], mine.at[slot], twin)

        pair = net.pair(order[0], mine.at[at[0]], mine.at[at[0]])
        shares = [share(at[0])]
        yield
        relays = net.relay(order[0], pair, ref, 4)
        shares += [share(wrap(at[0] - 1)), share(wrap(at[0] + 1))]
        yield
        for copy in relays:
            copy.wait_recv()
        shares.append(share(wrap(at[0] + 2)))
        yield
        for slot, copy in shares:
            copy.wait_recv()
            keep(1 - c, 1, slot)
        yield
        for which, core in enumerate((c, 1 - c)):
            pltpu.make_async_copy(whole.at[core], out.at[core], own_sems.at[4 + 2 * n + which]).wait()

    chains = []
    for batch in range(2):
        chains += [terms_chain(batch, g) for g in range(GROUPS)]
        chains += [hidden_chain()] if batch == 0 else []
        chains += [project_chain(batch)] + [part_chain(batch, p) for p in range(3)]
    together(*chains, late(1, queries_chain()))
    net.finish()


def reduce_all(hidden, dqp, dkp, dvp):
    shape = jax.ShapeDtypeStruct

    def buf(*dims, dtype=BF16):
        return pltpu.VMEM(dims, dtype)

    scratch = [buf(128, 4096), buf(128, 4096), buf(4096, 256), buf(256, 512)]
    scratch += [buf(4, 256, 1024), buf(4, 4, 256, 256), buf(4, 4, 256, 256)]
    scratch += [buf(256, 1024)] * 4
    for _ in range(4):
        scratch += [buf(4, 256, HEAD)] * 4 + [buf(3, 256, HEAD)]
    for n in SIZES:
        scratch += [buf(4, 4, 4, n, 16, 128)]
        scratch += [buf(4, 4, n, 16, 128)] * 4 + [buf(3, 4, n, 16, 128)]
        scratch += [buf(4, n, 16, 128, dtype=F32), buf(3, n, 16, 128, dtype=F32)]
    scratch += [buf(2, 4, 4, 4, n, 16, 128) for n in SIZES]
    return pl.pallas_call(
        reduce_kernel,
        out_shape=[shape((128, 2048), BF16)]
        + [shape((2, 4, 4, 4, n, 16, 128), BF16) for n in SIZES],
        in_specs=[HBM] * 4,
        out_specs=[HBM] * 7,
        scratch_shapes=scratch
        + [
            pltpu.SemaphoreType.DMA((200,)),
            pltpu.SemaphoreType.DMA((200,)),
            pltpu.SemaphoreType.DMA((17,)),
        ],
        compiler_params=pltpu.CompilerParams(
            collective_id=1, has_side_effects=True, vmem_limit_bytes=60 * 2**20
        ),
    )(hidden, dqp, dkp, dvp)


def widen_kernel(*refs):
    parts, (wk, wv), held, (wk_v, wv_v), (in_sems, out_sems) = (
        refs[0:6], refs[6:8], refs[8:14], refs[14:16], refs[16:18]
    )

    def at(p, x, y, z):
        places = {"x": x, "y": y, "z": z}
        return tuple(places[axis] for axis in ORDERS[p % 3])

    def loads(i):
        x, y = lax.div(i, 4), lax.rem(i, 4)
        spots = [(slice(None),) + at(p, x, y, slice(None)) for p in range(6)]
        return [
            pltpu.make_async_copy(parts[p].at[spot], held[p].at[spot], in_sems.at[p, i])
            for p, spot in enumerate(spots)
        ]

    def stores(i):
        rows = pl.ds(pl.multiple_of(i * 256, 256), 256)
        return [
            pltpu.make_async_copy(src.at[rows], dst.at[rows], out_sems.at[n, i])
            for n, (src, dst) in enumerate(((wk_v, wk), (wv_v, wv)))
        ]

    def begin(i, _):
        for copy in loads(i):
            copy.start()
        return 0

    def block(i, _):
        x, y = lax.div(i, 4), lax.rem(i, 4)
        for copy in loads(i):
            copy.wait()
        for z in range(4):
            r0 = pl.multiple_of(i * 256 + z * 64, 64)
            for core in range(2):
                for p in range(6):
                    out = wk_v if p < 3 else wv_v
                    for u, (row, column) in enumerate(PARTS[p // 3][p % 3]):
                        value = held[p][(core,) + at(p, x, y, z) + (u,)]
                        c0 = core * 256 + column * 128
                        out[pl.ds(r0 + row * 16, 16), c0 : c0 + 128] = value.astype(F32)
        for copy in stores(i):
            copy.start()
        return 0

    def end(i, _):
        for copy in stores(i):
            copy.wait()
        return 0

    lax.fori_loop(0, 16, begin, 0)
    lax.fori_loop(0, 16, block, 0)
    lax.fori_loop(0, 16, end, 0)


def widen(*parts):
    shape = jax.ShapeDtypeStruct
    return pl.pallas_call(
        widen_kernel,
        out_shape=[shape((4096, 512), F32)] * 2,
        in_specs=[HBM] * 6,
        out_specs=[HBM] * 2,
        scratch_shapes=[pltpu.VMEM((2, 4, 4, 4, n, 16, 128), BF16) for n in SIZES]
        + [
            pltpu.VMEM((4096, 512), F32),
            pltpu.VMEM((4096, 512), F32),
            pltpu.SemaphoreType.DMA((6, 16)),
            pltpu.SemaphoreType.DMA((2, 16)),
        ],
        compiler_params=pltpu.CompilerParams(vmem_limit_bytes=60 * 2**20),
    )(*parts)


def local(hidden, q, k, v, ao, do, lse, pos):
    qg, dog, kg, vg, sg, pq, pk = gather_all(q, do, k, v, ao, lse.T, pos[None, :])
    dqp, dkp, dvp = attend(pq, pk, qg, dog, kg, vg, sg)
    dq, *parts = reduce_all(hidden, dqp, dkp, dvp)
    wk, wv = widen(*parts)
    return dq, wk, wv


def solution(mesh):
    rows = P(("inner", "outer"), None)
    return jax.shard_map(
        local,
        mesh=mesh,
        in_specs=(rows,) * 7 + (P(("inner", "outer")),),
        out_specs=(rows, P(), P()),
        check_vma=False,
    )
```

```python
import functools
import math

import jax
import jax.numpy as jnp
from jax import lax
from jax.experimental import pallas as pl
from jax.experimental.pallas import tpu as pltpu
from jax.sharding import PartitionSpec as P

HEAD = 128
GROUPS = 2
SHARE = 4
RUN = 64
KEYS = 4096
KEY_RUNS = KEYS // RUN
QUERY_ROWS = 1024
QUERY_RUNS = QUERY_ROWS // RUN
UNIT = 2
CHUNK = 512
SCALE = HEAD**-0.5
LOG2E = math.log2(math.e)
F32 = jnp.float32
BF16 = jnp.bfloat16
MESH = pl.DeviceIdType.MESH
NT = (((1,), (1,)), ((), ()))
NN = (((1,), (0,)), ((), ()))
VMEM = pl.BlockSpec(memory_space=pltpu.VMEM)
SMEM = pl.BlockSpec(memory_space=pltpu.SMEM)
HBM = pl.BlockSpec(memory_space=pltpu.HBM)
ORDERS = ("zyx", "xzy", "yxz")
PARTS = (
    (((0, 0), (0, 1), (3, 0)), ((1, 0), (1, 1)), ((2, 0), (2, 1), (3, 1))),
    (((0, 0), (0, 1)), ((1, 0), (1, 1), (3, 0)), ((2, 0), (2, 1), (3, 1))),
)
AXES = ((("y", "M"), ("M", "y")), (("M", "y"), ("M", "y")))
SIZES = [len(tiles) for batch in PARTS for tiles in batch]


def dot(a, b, dims):
    return lax.dot_general(a, b, dims, preferred_element_type=F32)


def wrap(value):
    return lax.rem(value + 4, 4)


class Place:
    def __init__(self):
        inner, outer = lax.axis_index("inner"), lax.axis_index("outer")
        c = lax.rem(inner, 2)
        x = lax.div(inner, 8) * 2 + lax.div(outer, 4)
        y = lax.rem(lax.div(inner, 2), 4)
        z = lax.rem(outer, 4)
        self.c = c
        self.at = {"x": x, "y": y, "z": z, "L": z + c * (x - z), "M": x + c * (z - x)}
        self.step = {"x": (1, 0, 0), "y": (0, 1, 0), "z": (0, 0, 1), "L": (c, 0, 1 - c), "M": (1 - c, 0, c)}

    def device(self, axis=None, by=0, other=False):
        step = (0, 0, 0) if axis is None else self.step[axis]
        x, y, z = (wrap(self.at[name] + by * d) for name, d in zip("xyz", step))
        c = 1 - self.c if other else self.c
        return ((lax.div(x, 2) * 4 + y) * 2 + c, lax.rem(x, 2) * 4 + z)

    def beside(self):
        near = [self.device(axis, by) for axis in "xyz" for by in (1, -1, 2)]
        return near + [self.device(other=True)]


class Net:
    def __init__(self, place, send_sems, recv_sems):
        self.place, self.send_sems, self.recv_sems = place, send_sems, recv_sems
        self.sent = []

    def greet(self):
        barrier = pltpu.get_barrier_semaphore()
        near = self.place.beside()
        for device in near:
            pl.semaphore_signal(barrier, inc=1, device_id=device, device_id_type=MESH)
        pl.semaphore_wait(barrier, len(near))

    def send(self, src, dst, device):
        k = len(self.sent)
        assert k < self.send_sems.shape[0]
        copy = pltpu.make_async_remote_copy(
            src_ref=src,
            dst_ref=dst,
            send_sem=self.send_sems.at[k],
            recv_sem=self.recv_sems.at[k],
            device_id=device,
            device_id_type=MESH,
        )
        copy.start()
        self.sent.append(copy)
        return copy

    def finish(self):
        for copy in self.sent:
            copy.wait_send()

    def pair(self, axis, src, dst):
        return [self.send(src, dst, self.place.device(axis, by)) for by in (1, -1)]

    def relay(self, axis, pair, ref, n):
        s = self.place.at[axis]
        low, high = pl.ds(0, n // 2), pl.ds(n // 2, n - n // 2)
        pair[0].wait_recv()
        block = ref(wrap(s - 1), low)
        up = self.send(block, block, self.place.device(axis, 1))
        pair[1].wait_recv()
        block = ref(wrap(s + 1), high)
        return [up, self.send(block, block, self.place.device(axis, -1))]

    def cast(self, axis, block):
        return [self.send(block, block, self.place.device(axis, by)) for by in (1, -1, 2)]

    def scatter(self, axis, hbm, buf, at, n, relay, from_behind, from_ahead, out):
        s = self.place.at[axis]
        ahead, behind = self.place.device(axis, 1), self.place.device(axis, -1)
        h = n // 2
        low, high, whole = pl.ds(0, h), pl.ds(h, n - h), pl.ds(0, n)
        far, left, right = wrap(s + 2), wrap(s - 1), wrap(s + 1)
        relay_up = self.send(hbm.at[at(far, low)], relay.at[low], ahead)
        relay_down = self.send(hbm.at[at(far, high)], relay.at[high], behind)
        up_high = self.send(hbm.at[at(right, high)], from_behind.at[high], ahead)
        down_low = self.send(hbm.at[at(left, low)], from_ahead.at[low], behind)
        yield
        relay_up.wait_recv()
        spot = at(right, low)
        buf[spot] = (buf[spot].astype(F32) + relay[low].astype(F32)).astype(BF16)
        up_low = self.send(buf.at[spot], from_behind.at[low], ahead)
        relay_down.wait_recv()
        spot = at(left, high)
        buf[spot] = (buf[spot].astype(F32) + relay[high].astype(F32)).astype(BF16)
        down_high = self.send(buf.at[spot], from_ahead.at[high], behind)
        yield
        for copy in (up_high, down_low, up_low, down_high):
            copy.wait_recv()
        out[...] = (
            buf[at(s, whole)].astype(F32) + from_behind[...].astype(F32) + from_ahead[...].astype(F32)
        ).astype(out.dtype)

    def scatter_direct(self, axis, buf, inbox, out):
        s = self.place.at[axis]
        copies = [
            self.send(buf.at[wrap(s + by)], inbox.at[i], self.place.device(axis, by))
            for i, by in enumerate((1, -1, 2))
        ]
        yield
        for copy in copies:
            copy.wait_recv()
        out[...] = (
            buf[s].astype(F32)
            + inbox[0].astype(F32)
            + inbox[1].astype(F32)
            + inbox[2].astype(F32)
        ).astype(out.dtype)


def late(rounds, chain):
    for _ in range(rounds):
        yield
    yield from chain


def together(*chains):
    chains = list(chains)
    while chains:
        for chain in list(chains):
            try:
                next(chain)
            except StopIteration:
                chains.remove(chain)


def gather_kernel(
    q, do, k, v, ao, lse, pos, qg, dog, kg, vg, sg, pq, pk, do_v, ao_v, stats, mine, send_sems, recv_sems, own_sems
):
    place = Place()
    net = Net(place, send_sems, recv_sems)
    y, c, l, m = place.at["y"], place.c, place.at["L"], place.at["M"]
    twin = place.device(other=True)
    loads = [
        pltpu.make_async_copy(src, dst, own_sems.at[7 + n]) for n, (src, dst) in enumerate(((do, do_v), (ao, ao_v)))
    ]
    for copy in loads:
        copy.start()
    net.greet()
    first, second = (pl.multiple_of(i * 128, 128) for i in (c, 1 - c))

    def cut(columns):
        return [pl.ds(pl.multiple_of(i * columns, columns), columns) for i in (c, 1 - c)]

    wide, thin = cut(1024), cut(256)
    owns = []

    def keep(src, dst):
        copy = pltpu.make_async_copy(src, dst, own_sems.at[len(owns)])
        copy.start()
        owns.append(copy)
        return copy

    def queries_chain(src, buf):
        def block(start):
            return lambda slot, rows: buf.at[slot, pl.ds(start + rows.start, rows.size)]

        whole = pl.ds(0, 128)
        mine_at, twin_at = block(first), block(second)
        from_twin = net.send(src.at[:, wide[1]], buf.at[m, pl.ds(first, 128)], twin)
        pair = net.pair("L", src.at[:, wide[0]], mine_at(l, whole))
        own = keep(src.at[:, wide[0]], mine_at(l, whole))
        yield
        from_twin.wait_recv()
        pair2 = net.pair("L", twin_at(l, whole), twin_at(l, whole))
        yield
        relays = net.relay("L", pair, mine_at, 128)
        yield
        relays += net.relay("L", pair2, twin_at, 128)
        yield
        for copy in relays:
            copy.wait_recv()
        own.wait()

    def keys_chain(src, buf, a, b):
        i, j = place.at[a], place.at[b]
        whole = pl.ds(0, 128)

        def block(start):
            return lambda slot, rows: buf.at[j, slot, pl.ds(start + rows.start, rows.size)]

        def chip(slot):
            return lambda other, rows: buf.at[other, slot, rows]

        def pair_b(slot):
            return (slot, net.pair(b, buf.at[j, slot], buf.at[j, slot]))

        mine_at, twin_at = block(first), block(second)
        there = buf.at[y, l] if a == "M" else buf.at[l, y]
        from_twin = net.send(src.at[:, thin[1]], there.at[pl.ds(first, 128)], twin)
        pair = net.pair(a, src.at[:, thin[0]], mine_at(i, whole))
        own = keep(src.at[:, thin[0]], mine_at(i, whole))
        yield
        from_twin.wait_recv()
        pair2 = net.pair(a, twin_at(i, whole), twin_at(i, whole))
        own.wait()
        pairs = [pair_b(i)]
        yield
        relays = net.relay(a, pair, mine_at, 128)
        yield
        relays += net.relay(a, pair2, twin_at, 128)
        pairs += [pair_b(wrap(i - 1)), pair_b(wrap(i + 1))]
        yield
        for copy in relays:
            copy.wait_recv()
        pairs.append(pair_b(wrap(i + 2)))
        yield
        relays = []
        for slot, both in pairs:
            relays += net.relay(b, both, chip(slot), 256)
        yield
        for copy in relays:
            copy.wait_recv()

    def stats_chain():
        kept = [keep(pos, pk.at[y, m, c]), keep(pos, pq.at[l, c])]
        from_twin = [net.send(pos, pk.at[y, l, c], twin), net.send(pos, pq.at[m, c], twin)]
        for copy in loads:
            copy.wait()
        for h in range(16):
            columns = slice(h * HEAD, (h + 1) * HEAD)
            product = do_v[:, columns].astype(F32) * ao_v[:, columns].astype(F32)
            stats[:, h : h + 1] = jnp.sum(product, axis=1, keepdims=True)
        turned = stats[...].T
        for i in range(2):
            mine[i, 0:8, :] = lse[i * 8 : i * 8 + 8] * LOG2E
            mine[i, 8:16, :] = turned[i * 8 : i * 8 + 8]
        from_twin.append(net.send(mine.at[1 - c], sg.at[m, c], twin))
        kept.append(keep(mine.at[c], sg.at[l, c]))
        yield
        for copy in kept:
            copy.wait()
        for copy in from_twin:
            copy.wait_recv()
        places = net.cast("M", pk.at[y, m])
        rest = net.cast("L", sg.at[l]) + net.cast("L", pq.at[l])
        yield
        for copy in places:
            copy.wait_recv()
        rest += net.cast("y", pk.at[y])
        yield
        yield
        for copy in rest:
            copy.wait_recv()

    together(
        keys_chain(k, kg, "M", "y"),
        keys_chain(v, vg, "y", "M"),
        queries_chain(q, qg),
        late(2, queries_chain(do, dog)),
        stats_chain(),
    )
    net.finish()


def gather_all(q, do, k, v, ao, lse, pos):
    shape = jax.ShapeDtypeStruct
    return pl.pallas_call(
        gather_kernel,
        out_shape=[
            shape((4, 256, 1024), BF16),
            shape((4, 256, 1024), BF16),
            shape((4, 4, 256, 256), BF16),
            shape((4, 4, 256, 256), BF16),
            shape((4, 2, 16, 128), F32),
            shape((4, 2, 1, 128), jnp.int32),
            shape((4, 4, 2, 1, 128), jnp.int32),
        ],
        in_specs=[HBM] * 5 + [VMEM] * 2,
        out_specs=[HBM] * 7,
        scratch_shapes=[
            pltpu.VMEM((128, 2048), BF16),
            pltpu.VMEM((128, 2048), BF16),
            pltpu.VMEM((128, 128), F32),
            pltpu.VMEM((2, 16, 128), F32),
            pltpu.SemaphoreType.DMA((83,)),
            pltpu.SemaphoreType.DMA((83,)),
            pltpu.SemaphoreType.DMA((9,)),
        ],
        compiler_params=pltpu.CompilerParams(
            collective_id=0, has_side_effects=True, vmem_limit_bytes=60 * 2**20
        ),
    )(q, do, k, v, ao, lse, pos)


def attend_kernel(
    pq, pk, qg, dog, kg, vg, sg, dqp, dkp, dvp, order, reach, qplace, rank, origin, kplace, found, found_s,
    q_all, do_all, k_all, v_all, columns, dq_all, dk_all, dv_all,
    qs, dos, qt, dot_, lse_s, delta_s, dq_sum, dk_sum, dv_sum, in_sems, out_sems,
):
    rows = UNIT * SHARE * RUN

    def at_run(ref, j, first):
        a, b, r = lax.div(j, 16), lax.rem(lax.div(j, 4), 4), lax.rem(j, 4)
        part = pl.ds(pl.multiple_of(r * RUN, RUN), RUN)
        return ref.at[a, b, part] if first else ref.at[b, a, part]

    def key_copies(j):
        spot = pl.ds(pl.multiple_of(rank[j] * RUN, RUN), RUN)
        return (
            pltpu.make_async_copy(at_run(kg, j, True), k_all.at[spot], in_sems.at[0]),
            pltpu.make_async_copy(at_run(vg, j, False), v_all.at[spot], in_sems.at[1]),
        )

    def query_copies(r):
        i = order[r]
        part = pl.ds(pl.multiple_of(lax.rem(i, 4) * RUN, RUN), RUN)
        spot = pl.ds(pl.multiple_of(r * RUN, RUN), RUN)
        return (
            pltpu.make_async_copy(qg.at[lax.div(i, 4), part], q_all.at[spot], in_sems.at[2]),
            pltpu.make_async_copy(dog.at[lax.div(i, 4), part], do_all.at[spot], in_sems.at[3]),
        )

    def start(make):
        def body(i, _):
            for copy in make(i):
                copy.start()
            return 0

        return body

    def query_place(i):
        return pq[lax.div(i, 4), lax.rem(lax.div(i, 2), 2), 0, lax.rem(i, 2) * RUN]

    def key_place(j):
        c = lax.rem(lax.div(j, 2), 2)
        return pk[lax.div(j, 16), lax.rem(lax.div(j, 4), 4), c, 0, lax.rem(j, 2) * RUN]

    lane = lax.broadcasted_iota(jnp.int32, (1, 128), 1)
    blank = jnp.zeros((1, 128), jnp.int32)
    query_row = lax.fori_loop(
        0, QUERY_RUNS, lambda i, row: jnp.where(lane == i, query_place(i), row), blank, unroll=True
    )
    key_row = lax.fori_loop(
        0, KEY_RUNS, lambda j, row: jnp.where(lane == j, key_place(j), row), blank, unroll=True
    )

    def count_queries(i, total):
        return total + jnp.where(query_place(i) < query_row, 1, 0)

    def count_keys(j, totals):
        place = key_place(j)
        return (
            totals[0] + jnp.where(place < key_row, 1, 0),
            totals[1] + jnp.where(place <= query_row, 1, 0),
        )

    found[0:1, :] = lax.fori_loop(0, QUERY_RUNS, count_queries, blank, unroll=True)
    key_rank, query_reach = lax.fori_loop(0, KEY_RUNS, count_keys, (blank, blank), unroll=True)
    found[1:2, :] = query_reach
    found[2:3, :] = key_rank
    copy = pltpu.make_async_copy(found, found_s, in_sems.at[4])
    copy.start()
    for z in range(4):
        for c in range(2):
            spot = (z * 2 + c) * 128
            columns[spot : spot + 128, 0:16] = sg[z, c].T
    copy.wait()

    def place_query(i, _):
        r = found_s[0, i]
        order[r] = i
        reach[r] = found_s[1, i]
        qplace[r] = query_place(i)
        return 0

    def place_key(j, _):
        rank[j] = found_s[2, j]
        origin[found_s[2, j]] = j
        kplace[found_s[2, j]] = key_place(j)
        return 0

    lax.fori_loop(0, QUERY_RUNS, place_query, 0)
    lax.fori_loop(0, QUERY_RUNS, start(query_copies), 0)
    lax.fori_loop(0, KEY_RUNS, place_key, 0)
    lax.fori_loop(0, KEY_RUNS, start(key_copies), 0)
    dk_sum[...] = jnp.zeros_like(dk_sum)
    dv_sum[...] = jnp.zeros_like(dv_sum)
    pltpu.make_async_copy(q_all, q_all, in_sems.at[2]).wait()
    pltpu.make_async_copy(do_all, do_all, in_sems.at[3]).wait()
    pltpu.make_async_copy(k_all, k_all, in_sems.at[0]).wait()
    pltpu.make_async_copy(v_all, v_all, in_sems.at[1]).wait()

    per = CHUNK // RUN

    def query_back(r):
        i = order[r]
        part = pl.ds(pl.multiple_of(lax.rem(i, 4) * RUN, RUN), RUN)
        spot = pl.ds(pl.multiple_of(r * RUN, RUN), RUN)
        return (pltpu.make_async_copy(dq_all.at[spot], dqp.at[lax.div(i, 4), part], out_sems.at[0]),)

    def key_back(r):
        j = origin[r]
        spot = pl.ds(pl.multiple_of(r * RUN, RUN), RUN)
        return (
            pltpu.make_async_copy(dk_all.at[spot], at_run(dkp, j, True), out_sems.at[1]),
            pltpu.make_async_copy(dv_all.at[spot], at_run(dvp, j, False), out_sems.at[2]),
        )

    def unit(i, _):
        for u in range(UNIT):
            r = i * UNIT + u
            r0 = pl.multiple_of(r * RUN, RUN)
            s0 = pl.multiple_of(order[r] * RUN, RUN)
            for g in range(GROUPS):
                for h in range(SHARE):
                    head = g * SHARE + h
                    o = (u * SHARE + h) * RUN
                    spot = pl.ds(o, RUN)
                    qs[g, spot, :] = q_all[pl.ds(r0, RUN), head * HEAD : (head + 1) * HEAD]
                    dos[g, spot, :] = do_all[pl.ds(r0, RUN), head * HEAD : (head + 1) * HEAD]
                    lse_s[g, spot, :] = columns[pl.ds(s0, RUN), head : head + 1]
                    delta_s[g, spot, :] = columns[pl.ds(s0, RUN), 8 + head : 9 + head]
        for g in range(GROUPS):
            qt[g] = qs[g].T
            dot_[g] = dos[g].T
        dq_sum[...] = jnp.zeros_like(dq_sum)
        first, last = reach[i * UNIT], reach[i * UNIT + UNIT - 1]
        whole = lax.div(first - 1, per)
        rest = lax.rem(last, per)
        chunks = lax.div(last, per) + jnp.where(rest > per // 2, 1, 0)
        halves = jnp.where((rest > 0) & (rest <= per // 2), 1, 0)

        def step(masked, size, base, chunk, _):
            r0 = base + chunk * (size // RUN)
            keys = pl.ds(pl.multiple_of(r0 * RUN, size), size)
            if masked:
                row = lax.broadcasted_iota(jnp.int32, (rows, 1), 0)
                qpos = lax.rem(row, RUN)
                for u in range(UNIT):
                    inside = lax.div(row, SHARE * RUN) == u
                    qpos = qpos + jnp.where(inside, qplace[i * UNIT + u], 0)
                column = lax.broadcasted_iota(jnp.int32, (1, size), 1)
                kpos = lax.rem(column, RUN)
                for u in range(size // RUN):
                    kpos = kpos + jnp.where(lax.div(column, RUN) == u, kplace[r0 + u], 0)
                allowed = kpos <= qpos
            for g in range(GROUPS):
                kk = k_all[keys, g * HEAD : (g + 1) * HEAD]
                vv = v_all[keys, g * HEAD : (g + 1) * HEAD]
                probs = jnp.exp2(dot(qs[g], kk, NT) * (SCALE * LOG2E) - lse_s[g])
                if masked:
                    probs = jnp.where(allowed, probs, 0.0)
                dprobs = dot(dos[g], vv, NT)
                dscores = (probs * (dprobs - delta_s[g])).astype(BF16)
                dq_sum[g] += dot(dscores, kk, NN)
                dv_sum[g, :, keys] += dot(dot_[g], probs.astype(BF16), NN)
                dk_sum[g, :, keys] += dot(qt[g], dscores, NN)
            return 0

        lax.fori_loop(0, whole, functools.partial(step, False, CHUNK, 0), 0)
        lax.fori_loop(whole, chunks, functools.partial(step, True, CHUNK, 0), 0)
        lax.fori_loop(0, halves, functools.partial(step, True, CHUNK // 2, chunks * per), 0)
        for u in range(UNIT):
            r0 = pl.multiple_of((i * UNIT + u) * RUN, RUN)
            for g in range(GROUPS):
                for h in range(SHARE):
                    head = g * SHARE + h
                    o = (u * SHARE + h) * RUN
                    dq_all[pl.ds(r0, RUN), head * HEAD : (head + 1) * HEAD] = (
                        dq_sum[g, o : o + RUN, :] * SCALE
                    ).astype(BF16)
            for copy in query_back(i * UNIT + u):
                copy.start()
        return 0

    lax.fori_loop(0, QUERY_RUNS // UNIT, unit, 0)

    def turn(chunk, _):
        keys = pl.ds(pl.multiple_of(chunk * CHUNK, CHUNK), CHUNK)
        for g in range(GROUPS):
            columns_g = slice(g * HEAD, (g + 1) * HEAD)
            dk_all[keys, columns_g] = (dk_sum[g, :, keys] * SCALE).astype(BF16).T
            dv_all[keys, columns_g] = dv_sum[g, :, keys].astype(BF16).T
        for u in range(per):
            for copy in key_back(chunk * per + u):
                copy.start()
        return 0

    lax.fori_loop(0, KEYS // CHUNK, turn, 0)
    pltpu.make_async_copy(dq_all, dq_all, out_sems.at[0]).wait()
    pltpu.make_async_copy(dk_all, dk_all, out_sems.at[1]).wait()
    pltpu.make_async_copy(dv_all, dv_all, out_sems.at[2]).wait()


def attend(pq, pk, qg, dog, kg, vg, sg):
    shape = jax.ShapeDtypeStruct
    rows = UNIT * SHARE * RUN
    return pl.pallas_call(
        attend_kernel,
        out_shape=[
            shape((4, 256, 1024), BF16),
            shape((4, 4, 256, 256), BF16),
            shape((4, 4, 256, 256), BF16),
        ],
        in_specs=[SMEM] * 2 + [HBM] * 4 + [VMEM],
        out_specs=[HBM] * 3,
        scratch_shapes=[
            pltpu.SMEM((QUERY_RUNS,), jnp.int32),
            pltpu.SMEM((QUERY_RUNS,), jnp.int32),
            pltpu.SMEM((QUERY_RUNS,), jnp.int32),
            pltpu.SMEM((KEY_RUNS,), jnp.int32),
            pltpu.SMEM((KEY_RUNS,), jnp.int32),
            pltpu.SMEM((KEY_RUNS,), jnp.int32),
            pltpu.VMEM((8, 128), jnp.int32),
            pltpu.SMEM((8, 128), jnp.int32),
            pltpu.VMEM((QUERY_ROWS, 1024), BF16),
            pltpu.VMEM((QUERY_ROWS, 1024), BF16),
            pltpu.VMEM((KEYS, 256), BF16),
            pltpu.VMEM((KEYS, 256), BF16),
            pltpu.VMEM((QUERY_ROWS, 16), F32),
            pltpu.VMEM((QUERY_ROWS, 1024), BF16),
            pltpu.VMEM((KEYS, 256), BF16),
            pltpu.VMEM((KEYS, 256), BF16),
            pltpu.VMEM((GROUPS, rows, HEAD), BF16),
            pltpu.VMEM((GROUPS, rows, HEAD), BF16),
            pltpu.VMEM((GROUPS, HEAD, rows), BF16),
            pltpu.VMEM((GROUPS, HEAD, rows), BF16),
            pltpu.VMEM((GROUPS, rows, 1), F32),
            pltpu.VMEM((GROUPS, rows, 1), F32),
            pltpu.VMEM((GROUPS, rows, HEAD), F32),
            pltpu.VMEM((GROUPS, HEAD, KEYS), F32),
            pltpu.VMEM((GROUPS, HEAD, KEYS), F32),
            pltpu.SemaphoreType.DMA((5,)),
            pltpu.SemaphoreType.DMA((3,)),
        ],
        compiler_params=pltpu.CompilerParams(vmem_limit_bytes=60 * 2**20),
    )(pq, pk, qg, dog, kg, vg, sg)


def reduce_kernel(hidden, dqp, dkp, dvp, dq, *rest):
    rest = list(rest)

    def take(n):
        taken, rest[:n] = rest[:n], []
        return taken

    wg = take(6)
    h_own, h_twin, ht, dkv, dq_sums, dk_sums, dv_sums = take(7)
    dq_bufs, dq_own = take(3), take(1)[0]
    term_bufs = [take(5) for _ in range(4)]
    part_bufs = [take(8) for _ in range(6)]
    held = take(6)
    send_sems, recv_sems, own_sems = rest
    place = Place()
    net = Net(place, send_sems, recv_sems)
    c = place.c
    twin = place.device(other=True)
    loads = []
    for src, dst in ((dkp, dk_sums), (dvp, dv_sums), (dqp, dq_sums), (hidden, h_own)):
        loads.append(pltpu.make_async_copy(src, dst, own_sems.at[len(loads)]))
        loads[-1].start()
    net.greet()
    rows = pl.ds(pl.multiple_of(c * 128, 128), 128)
    theirs = pl.ds(pl.multiple_of((1 - c) * 128, 128), 128)
    done = set()

    def loaded(i):
        if i not in done:
            loads[i].wait()
            done.add(i)

    def queries_chain():
        first = net.scatter("L", dqp, dq_sums, lambda slot, part: (slot, part), 256, *dq_bufs, dq_own)
        next(first)
        yield
        loaded(2)
        yield from first
        columns = pl.ds(pl.multiple_of(c * 1024, 1024), 1024)
        copy = net.send(dq_own.at[theirs], dq.at[:, columns], twin)
        own = pltpu.make_async_copy(dq_own.at[rows], dq.at[:, columns], own_sems.at[16])
        own.start()
        yield
        own.wait()
        copy.wait_recv()

    def terms_chain(batch, g):
        hbm, sums = ((dkp, dk_sums), (dvp, dv_sums))[batch]
        relay, up, down, mid, inbox = term_bufs[batch * 2 + g]
        axes = AXES[batch][g]
        columns = pl.ds(g * HEAD, HEAD)

        def at(slot, part):
            outer = axes[0] == ("y", "M")[batch]
            return ((slot, part) if outer else (part, slot)) + (slice(None), columns)

        first = net.scatter(axes[0], hbm, sums, at, 4, relay, up, down, mid)
        next(first)
        yield
        loaded(batch)
        yield from first
        out = dkv.at[:, pl.ds(batch * 256 + g * HEAD, HEAD)]
        yield from net.scatter_direct(axes[1], mid, inbox, out)
        done.add(("terms", batch, g))

    def hidden_chain():
        copy = net.send(hidden, h_twin, twin)
        yield
        loaded(3)
        copy.wait_recv()
        ht[:, 0:128] = jnp.where(c == 0, h_own[...], h_twin[...]).T
        ht[:, 128:256] = jnp.where(c == 0, h_twin[...], h_own[...]).T
        done.add("hidden")

    def project_chain(batch):
        while not {("terms", batch, 0), ("terms", batch, 1), "hidden"} <= done:
            yield

        def project(i, _):
            xi, yi = lax.div(i, 4), lax.rem(i, 4)
            block = pl.ds(pl.multiple_of(i * 256, 256), 256)
            term = dot(ht[block, :], dkv[:, batch * 256 : batch * 256 + 256], NN).astype(BF16)
            for zi in range(4):
                at = {"x": xi, "y": yi, "z": zi}
                for p, tiles in enumerate(PARTS[batch]):
                    o = [at[axis] for axis in ORDERS[p]]
                    for u, (row, column) in enumerate(tiles):
                        r0, c0 = zi * 64 + row * 16, column * 128
                        part_bufs[batch * 3 + p][0][o[0], o[1], o[2], u] = term[r0 : r0 + 16, c0 : c0 + 128]
            return 0

        lax.fori_loop(0, 16, project, 0)
        done.add(("project", batch))

    def part_chain(batch, p):
        while ("project", batch) not in done:
            yield
        n = batch * 3 + p
        order, whole, out = ORDERS[p], held[n], wg[n]
        terms, relay, up, down, mid, inbox, mid2, inbox2 = part_bufs[n]
        at = [place.at[axis] for axis in order]
        mine = whole.at[c]
        yield from net.scatter(
            order[0], terms, terms, lambda slot, part: (slot, part), 4, relay, up, down, mid
        )
        yield from net.scatter_direct(order[1], mid, inbox, mid2)
        yield from net.scatter_direct(order[2], mid2, inbox2, mine.at[at[0], at[1], at[2]])
        copies = net.cast(order[2], mine.at[at[0], at[1], at[2]])
        yield
        for copy in copies:
            copy.wait_recv()
        copies = net.cast(order[1], mine.at[at[0], at[1]])
        yield
        for copy in copies:
            copy.wait_recv()

        def ref(slot, part):
            return mine.at[slot, part]

        def keep(core, which, slot):
            pltpu.make_async_copy(whole.at[core, slot], out.at[core, slot], own_sems.at[4 + 2 * n + which]).start()

        def share(slot):
            keep(c, 0, slot)
            return slot, net.send(mine.at[slot], mine.at[slot], twin)

        pair = net.pair(order[0], mine.at[at[0]], mine.at[at[0]])
        shares = [share(at[0])]
        yield
        relays = net.relay(order[0], pair, ref, 4)
        shares += [share(wrap(at[0] - 1)), share(wrap(at[0] + 1))]
        yield
        for copy in relays:
            copy.wait_recv()
        shares.append(share(wrap(at[0] + 2)))
        yield
        for slot, copy in shares:
            copy.wait_recv()
            keep(1 - c, 1, slot)
        yield
        for which, core in enumerate((c, 1 - c)):
            pltpu.make_async_copy(whole.at[core], out.at[core], own_sems.at[4 + 2 * n + which]).wait()

    chains = []
    for batch in range(2):
        chains += [terms_chain(batch, g) for g in range(GROUPS)]
        chains += [hidden_chain()] if batch == 0 else []
        chains += [project_chain(batch)] + [part_chain(batch, p) for p in range(3)]
    together(*chains, late(1, queries_chain()))
    net.finish()


def reduce_all(hidden, dqp, dkp, dvp):
    shape = jax.ShapeDtypeStruct

    def buf(*dims, dtype=BF16):
        return pltpu.VMEM(dims, dtype)

    scratch = [buf(128, 4096), buf(128, 4096), buf(4096, 256), buf(256, 512)]
    scratch += [buf(4, 256, 1024), buf(4, 4, 256, 256), buf(4, 4, 256, 256)]
    scratch += [buf(256, 1024)] * 4
    for _ in range(4):
        scratch += [buf(4, 256, HEAD)] * 4 + [buf(3, 256, HEAD)]
    for n in SIZES:
        scratch += [buf(4, 4, 4, n, 16, 128)]
        scratch += [buf(4, 4, n, 16, 128)] * 4 + [buf(3, 4, n, 16, 128)]
        scratch += [buf(4, n, 16, 128, dtype=F32), buf(3, n, 16, 128, dtype=F32)]
    scratch += [buf(2, 4, 4, 4, n, 16, 128) for n in SIZES]
    return pl.pallas_call(
        reduce_kernel,
        out_shape=[shape((128, 2048), BF16)]
        + [shape((2, 4, 4, 4, n, 16, 128), BF16) for n in SIZES],
        in_specs=[HBM] * 4,
        out_specs=[HBM] * 7,
        scratch_shapes=scratch
        + [
            pltpu.SemaphoreType.DMA((200,)),
            pltpu.SemaphoreType.DMA((200,)),
            pltpu.SemaphoreType.DMA((17,)),
        ],
        compiler_params=pltpu.CompilerParams(
            collective_id=1, has_side_effects=True, vmem_limit_bytes=60 * 2**20
        ),
    )(hidden, dqp, dkp, dvp)


def widen_kernel(*refs):
    parts, (wk, wv), held, (wk_v, wv_v), (in_sems, out_sems) = (
        refs[0:6], refs[6:8], refs[8:14], refs[14:16], refs[16:18]
    )

    def at(p, x, y, z):
        places = {"x": x, "y": y, "z": z}
        return tuple(places[axis] for axis in ORDERS[p % 3])

    def loads(i):
        x, y = lax.div(i, 4), lax.rem(i, 4)
        spots = [(slice(None),) + at(p, x, y, slice(None)) for p in range(6)]
        return [
            pltpu.make_async_copy(parts[p].at[spot], held[p].at[spot], in_sems.at[p, i])
            for p, spot in enumerate(spots)
        ]

    def stores(i):
        rows = pl.ds(pl.multiple_of(i * 256, 256), 256)
        return [
            pltpu.make_async_copy(src.at[rows], dst.at[rows], out_sems.at[n, i])
            for n, (src, dst) in enumerate(((wk_v, wk), (wv_v, wv)))
        ]

    def begin(i, _):
        for copy in loads(i):
            copy.start()
        return 0

    def block(i, _):
        x, y = lax.div(i, 4), lax.rem(i, 4)
        for copy in loads(i):
            copy.wait()
        for z in range(4):
            r0 = pl.multiple_of(i * 256 + z * 64, 64)
            for core in range(2):
                for p in range(6):
                    out = wk_v if p < 3 else wv_v
                    for u, (row, column) in enumerate(PARTS[p // 3][p % 3]):
                        value = held[p][(core,) + at(p, x, y, z) + (u,)]
                        c0 = core * 256 + column * 128
                        out[pl.ds(r0 + row * 16, 16), c0 : c0 + 128] = value.astype(F32)
        for copy in stores(i):
            copy.start()
        return 0

    def end(i, _):
        for copy in stores(i):
            copy.wait()
        return 0

    lax.fori_loop(0, 16, begin, 0)
    lax.fori_loop(0, 16, block, 0)
    lax.fori_loop(0, 16, end, 0)


def widen(*parts):
    shape = jax.ShapeDtypeStruct
    return pl.pallas_call(
        widen_kernel,
        out_shape=[shape((4096, 512), F32)] * 2,
        in_specs=[HBM] * 6,
        out_specs=[HBM] * 2,
        scratch_shapes=[pltpu.VMEM((2, 4, 4, 4, n, 16, 128), BF16) for n in SIZES]
        + [
            pltpu.VMEM((4096, 512), F32),
            pltpu.VMEM((4096, 512), F32),
            pltpu.SemaphoreType.DMA((6, 16)),
            pltpu.SemaphoreType.DMA((2, 16)),
        ],
        compiler_params=pltpu.CompilerParams(vmem_limit_bytes=60 * 2**20),
    )(*parts)


def local(hidden, q, k, v, ao, do, lse, pos):
    qg, dog, kg, vg, sg, pq, pk = gather_all(q, do, k, v, ao, lse.T, pos[None, :])
    dqp, dkp, dvp = attend(pq, pk, qg, dog, kg, vg, sg)
    dq, *parts = reduce_all(hidden, dqp, dkp, dvp)
    wk, wv = widen(*parts)
    return dq, wk, wv


def solution(mesh):
    rows = P(("inner", "outer"), None)
    return jax.shard_map(
        local,
        mesh=mesh,
        in_specs=(rows,) * 7 + (P(("inner", "outer")),),
        out_specs=(rows, P(), P()),
        check_vma=False,
    )
```

```python
import functools
import math

import jax
import jax.numpy as jnp
from jax import lax
from jax.experimental import pallas as pl
from jax.experimental.pallas import tpu as pltpu
from jax.sharding import PartitionSpec as P

HEAD = 128
GROUPS = 2
SHARE = 4
RUN = 64
KEYS = 4096
KEY_RUNS = KEYS // RUN
QUERY_ROWS = 1024
QUERY_RUNS = QUERY_ROWS // RUN
UNIT = 2
CHUNK = 512
SCALE = HEAD**-0.5
LOG2E = math.log2(math.e)
F32 = jnp.float32
BF16 = jnp.bfloat16
MESH = pl.DeviceIdType.MESH
NT = (((1,), (1,)), ((), ()))
NN = (((1,), (0,)), ((), ()))
VMEM = pl.BlockSpec(memory_space=pltpu.VMEM)
SMEM = pl.BlockSpec(memory_space=pltpu.SMEM)
HBM = pl.BlockSpec(memory_space=pltpu.HBM)
ORDERS = ("zyx", "xzy", "yxz")
PARTS = (
    (((0, 0), (0, 1), (3, 0)), ((1, 0), (1, 1)), ((2, 0), (2, 1), (3, 1))),
    (((0, 0), (0, 1)), ((1, 0), (1, 1), (3, 0)), ((2, 0), (2, 1), (3, 1))),
)
AXES = ((("y", "M"), ("M", "y")), (("M", "y"), ("M", "y")))
SIZES = [len(tiles) for batch in PARTS for tiles in batch]


def dot(a, b, dims):
    return lax.dot_general(a, b, dims, preferred_element_type=F32)


def wrap(value):
    return lax.rem(value + 4, 4)


class Place:
    def __init__(self):
        inner, outer = lax.axis_index("inner"), lax.axis_index("outer")
        c = lax.rem(inner, 2)
        x = lax.div(inner, 8) * 2 + lax.div(outer, 4)
        y = lax.rem(lax.div(inner, 2), 4)
        z = lax.rem(outer, 4)
        self.c = c
        self.at = {"x": x, "y": y, "z": z, "L": z + c * (x - z), "M": x + c * (z - x)}
        self.step = {"x": (1, 0, 0), "y": (0, 1, 0), "z": (0, 0, 1), "L": (c, 0, 1 - c), "M": (1 - c, 0, c)}

    def device(self, axis=None, by=0, other=False):
        step = (0, 0, 0) if axis is None else self.step[axis]
        x, y, z = (wrap(self.at[name] + by * d) for name, d in zip("xyz", step))
        c = 1 - self.c if other else self.c
        return ((lax.div(x, 2) * 4 + y) * 2 + c, lax.rem(x, 2) * 4 + z)

    def beside(self):
        near = [self.device(axis, by) for axis in "xyz" for by in (1, -1, 2)]
        return near + [self.device(other=True)]


class Net:
    def __init__(self, place, send_sems, recv_sems):
        self.place, self.send_sems, self.recv_sems = place, send_sems, recv_sems
        self.sent = []

    def greet(self):
        barrier = pltpu.get_barrier_semaphore()
        near = self.place.beside()
        for device in near:
            pl.semaphore_signal(barrier, inc=1, device_id=device, device_id_type=MESH)
        pl.semaphore_wait(barrier, len(near))

    def send(self, src, dst, device):
        k = len(self.sent)
        assert k < self.send_sems.shape[0]
        copy = pltpu.make_async_remote_copy(
            src_ref=src,
            dst_ref=dst,
            send_sem=self.send_sems.at[k],
            recv_sem=self.recv_sems.at[k],
            device_id=device,
            device_id_type=MESH,
        )
        copy.start()
        self.sent.append(copy)
        return copy

    def finish(self):
        for copy in self.sent:
            copy.wait_send()

    def pair(self, axis, src, dst):
        return [self.send(src, dst, self.place.device(axis, by)) for by in (1, -1)]

    def relay(self, axis, pair, ref, n):
        s = self.place.at[axis]
        low, high = pl.ds(0, n // 2), pl.ds(n // 2, n - n // 2)
        pair[0].wait_recv()
        block = ref(wrap(s - 1), low)
        up = self.send(block, block, self.place.device(axis, 1))
        pair[1].wait_recv()
        block = ref(wrap(s + 1), high)
        return [up, self.send(block, block, self.place.device(axis, -1))]

    def cast(self, axis, block):
        return [self.send(block, block, self.place.device(axis, by)) for by in (1, -1, 2)]

    def scatter(self, axis, hbm, buf, at, n, relay, from_behind, from_ahead, out):
        s = self.place.at[axis]
        ahead, behind = self.place.device(axis, 1), self.place.device(axis, -1)
        h = n // 2
        low, high, whole = pl.ds(0, h), pl.ds(h, n - h), pl.ds(0, n)
        far, left, right = wrap(s + 2), wrap(s - 1), wrap(s + 1)
        relay_up = self.send(hbm.at[at(far, low)], relay.at[low], ahead)
        relay_down = self.send(hbm.at[at(far, high)], relay.at[high], behind)
        up_high = self.send(hbm.at[at(right, high)], from_behind.at[high], ahead)
        down_low = self.send(hbm.at[at(left, low)], from_ahead.at[low], behind)
        yield
        relay_up.wait_recv()
        spot = at(right, low)
        buf[spot] = (buf[spot].astype(F32) + relay[low].astype(F32)).astype(BF16)
        up_low = self.send(buf.at[spot], from_behind.at[low], ahead)
        relay_down.wait_recv()
        spot = at(left, high)
        buf[spot] = (buf[spot].astype(F32) + relay[high].astype(F32)).astype(BF16)
        down_high = self.send(buf.at[spot], from_ahead.at[high], behind)
        yield
        for copy in (up_high, down_low, up_low, down_high):
            copy.wait_recv()
        out[...] = (
            buf[at(s, whole)].astype(F32) + from_behind[...].astype(F32) + from_ahead[...].astype(F32)
        ).astype(out.dtype)

    def scatter_direct(self, axis, buf, inbox, out):
        s = self.place.at[axis]
        copies = [
            self.send(buf.at[wrap(s + by)], inbox.at[i], self.place.device(axis, by))
            for i, by in enumerate((1, -1, 2))
        ]
        yield
        for copy in copies:
            copy.wait_recv()
        out[...] = (
            buf[s].astype(F32)
            + inbox[0].astype(F32)
            + inbox[1].astype(F32)
            + inbox[2].astype(F32)
        ).astype(out.dtype)


def late(rounds, chain):
    for _ in range(rounds):
        yield
    yield from chain


def together(*chains):
    chains = list(chains)
    while chains:
        for chain in list(chains):
            try:
                next(chain)
            except StopIteration:
                chains.remove(chain)


def gather_kernel(
    q, do, k, v, ao, lse, pos, qg, dog, kg, vg, sg, pq, pk, do_v, ao_v, stats, mine, send_sems, recv_sems, own_sems
):
    place = Place()
    net = Net(place, send_sems, recv_sems)
    y, c, l, m = place.at["y"], place.c, place.at["L"], place.at["M"]
    twin = place.device(other=True)
    loads = [
        pltpu.make_async_copy(src, dst, own_sems.at[7 + n]) for n, (src, dst) in enumerate(((do, do_v), (ao, ao_v)))
    ]
    for copy in loads:
        copy.start()
    net.greet()
    first, second = (pl.multiple_of(i * 128, 128) for i in (c, 1 - c))

    def cut(columns):
        return [pl.ds(pl.multiple_of(i * columns, columns), columns) for i in (c, 1 - c)]

    wide, thin = cut(1024), cut(256)
    owns = []

    def keep(src, dst):
        copy = pltpu.make_async_copy(src, dst, own_sems.at[len(owns)])
        copy.start()
        owns.append(copy)
        return copy

    def queries_chain(src, buf):
        def block(start):
            return lambda slot, rows: buf.at[slot, pl.ds(start + rows.start, rows.size)]

        whole = pl.ds(0, 128)
        mine_at, twin_at = block(first), block(second)
        from_twin = net.send(src.at[:, wide[1]], buf.at[m, pl.ds(first, 128)], twin)
        pair = net.pair("L", src.at[:, wide[0]], mine_at(l, whole))
        own = keep(src.at[:, wide[0]], mine_at(l, whole))
        yield
        from_twin.wait_recv()
        pair2 = net.pair("L", twin_at(l, whole), twin_at(l, whole))
        yield
        relays = net.relay("L", pair, mine_at, 128)
        yield
        relays += net.relay("L", pair2, twin_at, 128)
        yield
        for copy in relays:
            copy.wait_recv()
        own.wait()

    def keys_chain(src, buf, a, b):
        i, j = place.at[a], place.at[b]
        whole = pl.ds(0, 128)

        def block(start):
            return lambda slot, rows: buf.at[j, slot, pl.ds(start + rows.start, rows.size)]

        def chip(slot):
            return lambda other, rows: buf.at[other, slot, rows]

        def pair_b(slot):
            return (slot, net.pair(b, buf.at[j, slot], buf.at[j, slot]))

        mine_at, twin_at = block(first), block(second)
        there = buf.at[y, l] if a == "M" else buf.at[l, y]
        from_twin = net.send(src.at[:, thin[1]], there.at[pl.ds(first, 128)], twin)
        pair = net.pair(a, src.at[:, thin[0]], mine_at(i, whole))
        own = keep(src.at[:, thin[0]], mine_at(i, whole))
        yield
        from_twin.wait_recv()
        pair2 = net.pair(a, twin_at(i, whole), twin_at(i, whole))
        own.wait()
        pairs = [pair_b(i)]
        yield
        relays = net.relay(a, pair, mine_at, 128)
        yield
        relays += net.relay(a, pair2, twin_at, 128)
        pairs += [pair_b(wrap(i - 1)), pair_b(wrap(i + 1))]
        yield
        for copy in relays:
            copy.wait_recv()
        pairs.append(pair_b(wrap(i + 2)))
        yield
        relays = []
        for slot, both in pairs:
            relays += net.relay(b, both, chip(slot), 256)
        yield
        for copy in relays:
            copy.wait_recv()

    def stats_chain():
        kept = [keep(pos, pk.at[y, m, c]), keep(pos, pq.at[l, c])]
        from_twin = [net.send(pos, pk.at[y, l, c], twin), net.send(pos, pq.at[m, c], twin)]
        for copy in loads:
            copy.wait()
        for h in range(16):
            columns = slice(h * HEAD, (h + 1) * HEAD)
            product = do_v[:, columns].astype(F32) * ao_v[:, columns].astype(F32)
            stats[:, h : h + 1] = jnp.sum(product, axis=1, keepdims=True)
        turned = stats[...].T
        for i in range(2):
            mine[i, 0:8, :] = lse[i * 8 : i * 8 + 8] * LOG2E
            mine[i, 8:16, :] = turned[i * 8 : i * 8 + 8]
        from_twin.append(net.send(mine.at[1 - c], sg.at[m, c], twin))
        kept.append(keep(mine.at[c], sg.at[l, c]))
        yield
        for copy in kept:
            copy.wait()
        for copy in from_twin:
            copy.wait_recv()
        places = net.cast("M", pk.at[y, m])
        rest = net.cast("L", sg.at[l]) + net.cast("L", pq.at[l])
        yield
        for copy in places:
            copy.wait_recv()
        rest += net.cast("y", pk.at[y])
        yield
        yield
        for copy in rest:
            copy.wait_recv()

    together(
        keys_chain(k, kg, "M", "y"),
        keys_chain(v, vg, "y", "M"),
        queries_chain(q, qg),
        late(2, queries_chain(do, dog)),
        stats_chain(),
    )
    net.finish()


def gather_all(q, do, k, v, ao, lse, pos):
    shape = jax.ShapeDtypeStruct
    return pl.pallas_call(
        gather_kernel,
        out_shape=[
            shape((4, 256, 1024), BF16),
            shape((4, 256, 1024), BF16),
            shape((4, 4, 256, 256), BF16),
            shape((4, 4, 256, 256), BF16),
            shape((4, 2, 16, 128), F32),
            shape((4, 2, 1, 128), jnp.int32),
            shape((4, 4, 2, 1, 128), jnp.int32),
        ],
        in_specs=[HBM] * 5 + [VMEM] * 2,
        out_specs=[HBM] * 7,
        scratch_shapes=[
            pltpu.VMEM((128, 2048), BF16),
            pltpu.VMEM((128, 2048), BF16),
            pltpu.VMEM((128, 128), F32),
            pltpu.VMEM((2, 16, 128), F32),
            pltpu.SemaphoreType.DMA((83,)),
            pltpu.SemaphoreType.DMA((83,)),
            pltpu.SemaphoreType.DMA((9,)),
        ],
        compiler_params=pltpu.CompilerParams(
            collective_id=0, has_side_effects=True, vmem_limit_bytes=60 * 2**20
        ),
    )(q, do, k, v, ao, lse, pos)


def attend_kernel(
    pq, pk, qg, dog, kg, vg, sg, dqp, dkp, dvp, order, reach, qplace, rank, origin, kplace, found, found_s,
    q_all, do_all, k_all, v_all, columns, dq_all, dk_all, dv_all,
    qs, dos, qt, dot_, lse_s, delta_s, dq_sum, dk_sum, dv_sum, in_sems, out_sems,
):
    rows = UNIT * SHARE * RUN

    def at_run(ref, j, first):
        a, b, r = lax.div(j, 16), lax.rem(lax.div(j, 4), 4), lax.rem(j, 4)
        part = pl.ds(pl.multiple_of(r * RUN, RUN), RUN)
        return ref.at[a, b, part] if first else ref.at[b, a, part]

    def key_copies(j):
        spot = pl.ds(pl.multiple_of(rank[j] * RUN, RUN), RUN)
        return (
            pltpu.make_async_copy(at_run(kg, j, True), k_all.at[spot], in_sems.at[0]),
            pltpu.make_async_copy(at_run(vg, j, False), v_all.at[spot], in_sems.at[1]),
        )

    def query_copies(r):
        i = order[r]
        part = pl.ds(pl.multiple_of(lax.rem(i, 4) * RUN, RUN), RUN)
        spot = pl.ds(pl.multiple_of(r * RUN, RUN), RUN)
        return (
            pltpu.make_async_copy(qg.at[lax.div(i, 4), part], q_all.at[spot], in_sems.at[2]),
            pltpu.make_async_copy(dog.at[lax.div(i, 4), part], do_all.at[spot], in_sems.at[3]),
        )

    def start(make):
        def body(i, _):
            for copy in make(i):
                copy.start()
            return 0

        return body

    def query_place(i):
        return pq[lax.div(i, 4), lax.rem(lax.div(i, 2), 2), 0, lax.rem(i, 2) * RUN]

    def key_place(j):
        c = lax.rem(lax.div(j, 2), 2)
        return pk[lax.div(j, 16), lax.rem(lax.div(j, 4), 4), c, 0, lax.rem(j, 2) * RUN]

    lane = lax.broadcasted_iota(jnp.int32, (1, 128), 1)
    blank = jnp.zeros((1, 128), jnp.int32)
    query_row = lax.fori_loop(
        0, QUERY_RUNS, lambda i, row: jnp.where(lane == i, query_place(i), row), blank, unroll=True
    )
    key_row = lax.fori_loop(
        0, KEY_RUNS, lambda j, row: jnp.where(lane == j, key_place(j), row), blank, unroll=True
    )

    def count_queries(i, total):
        return total + jnp.where(query_place(i) < query_row, 1, 0)

    def count_keys(j, totals):
        place = key_place(j)
        return (
            totals[0] + jnp.where(place < key_row, 1, 0),
            totals[1] + jnp.where(place <= query_row, 1, 0),
        )

    found[0:1, :] = lax.fori_loop(0, QUERY_RUNS, count_queries, blank, unroll=True)
    key_rank, query_reach = lax.fori_loop(0, KEY_RUNS, count_keys, (blank, blank), unroll=True)
    found[1:2, :] = query_reach
    found[2:3, :] = key_rank
    copy = pltpu.make_async_copy(found, found_s, in_sems.at[4])
    copy.start()
    for z in range(4):
        for c in range(2):
            spot = (z * 2 + c) * 128
            columns[spot : spot + 128, 0:16] = sg[z, c].T
    copy.wait()

    def place_query(i, _):
        r = found_s[0, i]
        order[r] = i
        reach[r] = found_s[1, i]
        qplace[r] = query_place(i)
        return 0

    def place_key(j, _):
        rank[j] = found_s[2, j]
        origin[found_s[2, j]] = j
        kplace[found_s[2, j]] = key_place(j)
        return 0

    lax.fori_loop(0, QUERY_RUNS, place_query, 0)
    lax.fori_loop(0, QUERY_RUNS, start(query_copies), 0)
    lax.fori_loop(0, KEY_RUNS, place_key, 0)
    lax.fori_loop(0, KEY_RUNS, start(key_copies), 0)
    dk_sum[...] = jnp.zeros_like(dk_sum)
    dv_sum[...] = jnp.zeros_like(dv_sum)
    pltpu.make_async_copy(q_all, q_all, in_sems.at[2]).wait()
    pltpu.make_async_copy(do_all, do_all, in_sems.at[3]).wait()
    pltpu.make_async_copy(k_all, k_all, in_sems.at[0]).wait()
    pltpu.make_async_copy(v_all, v_all, in_sems.at[1]).wait()

    per = CHUNK // RUN

    def query_back(r):
        i = order[r]
        part = pl.ds(pl.multiple_of(lax.rem(i, 4) * RUN, RUN), RUN)
        spot = pl.ds(pl.multiple_of(r * RUN, RUN), RUN)
        return (pltpu.make_async_copy(dq_all.at[spot], dqp.at[lax.div(i, 4), part], out_sems.at[0]),)

    def key_back(r):
        j = origin[r]
        spot = pl.ds(pl.multiple_of(r * RUN, RUN), RUN)
        return (
            pltpu.make_async_copy(dk_all.at[spot], at_run(dkp, j, True), out_sems.at[1]),
            pltpu.make_async_copy(dv_all.at[spot], at_run(dvp, j, False), out_sems.at[2]),
        )

    def unit(i, _):
        for u in range(UNIT):
            r = i * UNIT + u
            r0 = pl.multiple_of(r * RUN, RUN)
            s0 = pl.multiple_of(order[r] * RUN, RUN)
            for g in range(GROUPS):
                for h in range(SHARE):
                    head = g * SHARE + h
                    o = (u * SHARE + h) * RUN
                    spot = pl.ds(o, RUN)
                    qs[g, spot, :] = q_all[pl.ds(r0, RUN), head * HEAD : (head + 1) * HEAD]
                    dos[g, spot, :] = do_all[pl.ds(r0, RUN), head * HEAD : (head + 1) * HEAD]
                    lse_s[g, spot, :] = columns[pl.ds(s0, RUN), head : head + 1]
                    delta_s[g, spot, :] = columns[pl.ds(s0, RUN), 8 + head : 9 + head]
        for g in range(GROUPS):
            qt[g] = qs[g].T
            dot_[g] = dos[g].T
        dq_sum[...] = jnp.zeros_like(dq_sum)
        first, last = reach[i * UNIT], reach[i * UNIT + UNIT - 1]
        whole = lax.div(first - 1, per)
        rest = lax.rem(last, per)
        chunks = lax.div(last, per) + jnp.where(rest > per // 2, 1, 0)
        halves = jnp.where((rest > per // 4) & (rest <= per // 2), 1, 0)
        quarters = jnp.where((rest > 0) & (rest <= per // 4), 1, 0)

        def step(masked, size, base, chunk, _):
            r0 = base + chunk * (size // RUN)
            keys = pl.ds(pl.multiple_of(r0 * RUN, size), size)
            if masked:
                row = lax.broadcasted_iota(jnp.int32, (rows, 1), 0)
                qpos = lax.rem(row, RUN)
                for u in range(UNIT):
                    inside = lax.div(row, SHARE * RUN) == u
                    qpos = qpos + jnp.where(inside, qplace[i * UNIT + u], 0)
                column = lax.broadcasted_iota(jnp.int32, (1, size), 1)
                kpos = lax.rem(column, RUN)
                for u in range(size // RUN):
                    kpos = kpos + jnp.where(lax.div(column, RUN) == u, kplace[r0 + u], 0)
                allowed = kpos <= qpos
            for g in range(GROUPS):
                kk = k_all[keys, g * HEAD : (g + 1) * HEAD]
                vv = v_all[keys, g * HEAD : (g + 1) * HEAD]
                probs = jnp.exp2(dot(qs[g], kk, NT) * (SCALE * LOG2E) - lse_s[g])
                if masked:
                    probs = jnp.where(allowed, probs, 0.0)
                dprobs = dot(dos[g], vv, NT)
                dscores = (probs * (dprobs - delta_s[g])).astype(BF16)
                dq_sum[g] += dot(dscores, kk, NN)
                dv_sum[g, :, keys] += dot(dot_[g], probs.astype(BF16), NN)
                dk_sum[g, :, keys] += dot(qt[g], dscores, NN)
            return 0

        lax.fori_loop(0, whole, functools.partial(step, False, CHUNK, 0), 0)
        lax.fori_loop(whole, chunks, functools.partial(step, True, CHUNK, 0), 0)
        lax.fori_loop(0, halves, functools.partial(step, True, CHUNK // 2, chunks * per), 0)
        lax.fori_loop(0, quarters, functools.partial(step, True, CHUNK // 4, chunks * per), 0)
        for u in range(UNIT):
            r0 = pl.multiple_of((i * UNIT + u) * RUN, RUN)
            for g in range(GROUPS):
                for h in range(SHARE):
                    head = g * SHARE + h
                    o = (u * SHARE + h) * RUN
                    dq_all[pl.ds(r0, RUN), head * HEAD : (head + 1) * HEAD] = (
                        dq_sum[g, o : o + RUN, :] * SCALE
                    ).astype(BF16)
            for copy in query_back(i * UNIT + u):
                copy.start()
        return 0

    lax.fori_loop(0, QUERY_RUNS // UNIT, unit, 0)

    def turn(chunk, _):
        keys = pl.ds(pl.multiple_of(chunk * CHUNK, CHUNK), CHUNK)
        for g in range(GROUPS):
            columns_g = slice(g * HEAD, (g + 1) * HEAD)
            dk_all[keys, columns_g] = (dk_sum[g, :, keys] * SCALE).astype(BF16).T
            dv_all[keys, columns_g] = dv_sum[g, :, keys].astype(BF16).T
        for u in range(per):
            for copy in key_back(chunk * per + u):
                copy.start()
        return 0

    lax.fori_loop(0, KEYS // CHUNK, turn, 0)
    pltpu.make_async_copy(dq_all, dq_all, out_sems.at[0]).wait()
    pltpu.make_async_copy(dk_all, dk_all, out_sems.at[1]).wait()
    pltpu.make_async_copy(dv_all, dv_all, out_sems.at[2]).wait()


def attend(pq, pk, qg, dog, kg, vg, sg):
    shape = jax.ShapeDtypeStruct
    rows = UNIT * SHARE * RUN
    return pl.pallas_call(
        attend_kernel,
        out_shape=[
            shape((4, 256, 1024), BF16),
            shape((4, 4, 256, 256), BF16),
            shape((4, 4, 256, 256), BF16),
        ],
        in_specs=[SMEM] * 2 + [HBM] * 4 + [VMEM],
        out_specs=[HBM] * 3,
        scratch_shapes=[
            pltpu.SMEM((QUERY_RUNS,), jnp.int32),
            pltpu.SMEM((QUERY_RUNS,), jnp.int32),
            pltpu.SMEM((QUERY_RUNS,), jnp.int32),
            pltpu.SMEM((KEY_RUNS,), jnp.int32),
            pltpu.SMEM((KEY_RUNS,), jnp.int32),
            pltpu.SMEM((KEY_RUNS,), jnp.int32),
            pltpu.VMEM((8, 128), jnp.int32),
            pltpu.SMEM((8, 128), jnp.int32),
            pltpu.VMEM((QUERY_ROWS, 1024), BF16),
            pltpu.VMEM((QUERY_ROWS, 1024), BF16),
            pltpu.VMEM((KEYS, 256), BF16),
            pltpu.VMEM((KEYS, 256), BF16),
            pltpu.VMEM((QUERY_ROWS, 16), F32),
            pltpu.VMEM((QUERY_ROWS, 1024), BF16),
            pltpu.VMEM((KEYS, 256), BF16),
            pltpu.VMEM((KEYS, 256), BF16),
            pltpu.VMEM((GROUPS, rows, HEAD), BF16),
            pltpu.VMEM((GROUPS, rows, HEAD), BF16),
            pltpu.VMEM((GROUPS, HEAD, rows), BF16),
            pltpu.VMEM((GROUPS, HEAD, rows), BF16),
            pltpu.VMEM((GROUPS, rows, 1), F32),
            pltpu.VMEM((GROUPS, rows, 1), F32),
            pltpu.VMEM((GROUPS, rows, HEAD), F32),
            pltpu.VMEM((GROUPS, HEAD, KEYS), F32),
            pltpu.VMEM((GROUPS, HEAD, KEYS), F32),
            pltpu.SemaphoreType.DMA((5,)),
            pltpu.SemaphoreType.DMA((3,)),
        ],
        compiler_params=pltpu.CompilerParams(vmem_limit_bytes=60 * 2**20),
    )(pq, pk, qg, dog, kg, vg, sg)


def reduce_kernel(hidden, dqp, dkp, dvp, dq, *rest):
    rest = list(rest)

    def take(n):
        taken, rest[:n] = rest[:n], []
        return taken

    wg = take(6)
    h_own, h_twin, ht, dkv, dq_sums, dk_sums, dv_sums = take(7)
    dq_bufs, dq_own = take(3), take(1)[0]
    term_bufs = [take(5) for _ in range(4)]
    part_bufs = [take(8) for _ in range(6)]
    held = take(6)
    send_sems, recv_sems, own_sems = rest
    place = Place()
    net = Net(place, send_sems, recv_sems)
    c = place.c
    twin = place.device(other=True)
    loads = []
    for src, dst in ((dkp, dk_sums), (dvp, dv_sums), (dqp, dq_sums), (hidden, h_own)):
        loads.append(pltpu.make_async_copy(src, dst, own_sems.at[len(loads)]))
        loads[-1].start()
    net.greet()
    rows = pl.ds(pl.multiple_of(c * 128, 128), 128)
    theirs = pl.ds(pl.multiple_of((1 - c) * 128, 128), 128)
    done = set()

    def loaded(i):
        if i not in done:
            loads[i].wait()
            done.add(i)

    def queries_chain():
        first = net.scatter("L", dqp, dq_sums, lambda slot, part: (slot, part), 256, *dq_bufs, dq_own)
        next(first)
        yield
        loaded(2)
        yield from first
        columns = pl.ds(pl.multiple_of(c * 1024, 1024), 1024)
        copy = net.send(dq_own.at[theirs], dq.at[:, columns], twin)
        own = pltpu.make_async_copy(dq_own.at[rows], dq.at[:, columns], own_sems.at[16])
        own.start()
        yield
        own.wait()
        copy.wait_recv()

    def terms_chain(batch, g):
        hbm, sums = ((dkp, dk_sums), (dvp, dv_sums))[batch]
        relay, up, down, mid, inbox = term_bufs[batch * 2 + g]
        axes = AXES[batch][g]
        columns = pl.ds(g * HEAD, HEAD)

        def at(slot, part):
            outer = axes[0] == ("y", "M")[batch]
            return ((slot, part) if outer else (part, slot)) + (slice(None), columns)

        first = net.scatter(axes[0], hbm, sums, at, 4, relay, up, down, mid)
        next(first)
        yield
        loaded(batch)
        yield from first
        out = dkv.at[:, pl.ds(batch * 256 + g * HEAD, HEAD)]
        yield from net.scatter_direct(axes[1], mid, inbox, out)
        done.add(("terms", batch, g))

    def hidden_chain():
        copy = net.send(hidden, h_twin, twin)
        yield
        loaded(3)
        copy.wait_recv()
        ht[:, 0:128] = jnp.where(c == 0, h_own[...], h_twin[...]).T
        ht[:, 128:256] = jnp.where(c == 0, h_twin[...], h_own[...]).T
        done.add("hidden")

    def project_chain(batch):
        while not {("terms", batch, 0), ("terms", batch, 1), "hidden"} <= done:
            yield

        def project(i, _):
            xi, yi = lax.div(i, 4), lax.rem(i, 4)
            block = pl.ds(pl.multiple_of(i * 256, 256), 256)
            term = dot(ht[block, :], dkv[:, batch * 256 : batch * 256 + 256], NN).astype(BF16)
            for zi in range(4):
                at = {"x": xi, "y": yi, "z": zi}
                for p, tiles in enumerate(PARTS[batch]):
                    o = [at[axis] for axis in ORDERS[p]]
                    for u, (row, column) in enumerate(tiles):
                        r0, c0 = zi * 64 + row * 16, column * 128
                        part_bufs[batch * 3 + p][0][o[0], o[1], o[2], u] = term[r0 : r0 + 16, c0 : c0 + 128]
            return 0

        lax.fori_loop(0, 16, project, 0)
        done.add(("project", batch))

    def part_chain(batch, p):
        while ("project", batch) not in done:
            yield
        n = batch * 3 + p
        order, whole, out = ORDERS[p], held[n], wg[n]
        terms, relay, up, down, mid, inbox, mid2, inbox2 = part_bufs[n]
        at = [place.at[axis] for axis in order]
        mine = whole.at[c]
        yield from net.scatter(
            order[0], terms, terms, lambda slot, part: (slot, part), 4, relay, up, down, mid
        )
        yield from net.scatter_direct(order[1], mid, inbox, mid2)
        yield from net.scatter_direct(order[2], mid2, inbox2, mine.at[at[0], at[1], at[2]])
        copies = net.cast(order[2], mine.at[at[0], at[1], at[2]])
        yield
        for copy in copies:
            copy.wait_recv()
        copies = net.cast(order[1], mine.at[at[0], at[1]])
        yield
        for copy in copies:
            copy.wait_recv()

        def ref(slot, part):
            return mine.at[slot, part]

        def keep(core, which, slot):
            pltpu.make_async_copy(whole.at[core, slot], out.at[core, slot], own_sems.at[4 + 2 * n + which]).start()

        def share(slot):
            keep(c, 0, slot)
            return slot, net.send(mine.at[slot], mine.at[slot], twin)

        pair = net.pair(order[0], mine.at[at[0]], mine.at[at[0]])
        shares = [share(at[0])]
        yield
        relays = net.relay(order[0], pair, ref, 4)
        shares += [share(wrap(at[0] - 1)), share(wrap(at[0] + 1))]
        yield
        for copy in relays:
            copy.wait_recv()
        shares.append(share(wrap(at[0] + 2)))
        yield
        for slot, copy in shares:
            copy.wait_recv()
            keep(1 - c, 1, slot)
        yield
        for which, core in enumerate((c, 1 - c)):
            pltpu.make_async_copy(whole.at[core], out.at[core], own_sems.at[4 + 2 * n + which]).wait()

    chains = []
    for batch in range(2):
        chains += [terms_chain(batch, g) for g in range(GROUPS)]
        chains += [hidden_chain()] if batch == 0 else []
        chains += [project_chain(batch)] + [part_chain(batch, p) for p in range(3)]
    together(*chains, late(1, queries_chain()))
    net.finish()


def reduce_all(hidden, dqp, dkp, dvp):
    shape = jax.ShapeDtypeStruct

    def buf(*dims, dtype=BF16):
        return pltpu.VMEM(dims, dtype)

    scratch = [buf(128, 4096), buf(128, 4096), buf(4096, 256), buf(256, 512)]
    scratch += [buf(4, 256, 1024), buf(4, 4, 256, 256), buf(4, 4, 256, 256)]
    scratch += [buf(256, 1024)] * 4
    for _ in range(4):
        scratch += [buf(4, 256, HEAD)] * 4 + [buf(3, 256, HEAD)]
    for n in SIZES:
        scratch += [buf(4, 4, 4, n, 16, 128)]
        scratch += [buf(4, 4, n, 16, 128)] * 4 + [buf(3, 4, n, 16, 128)]
        scratch += [buf(4, n, 16, 128, dtype=F32), buf(3, n, 16, 128, dtype=F32)]
    scratch += [buf(2, 4, 4, 4, n, 16, 128) for n in SIZES]
    return pl.pallas_call(
        reduce_kernel,
        out_shape=[shape((128, 2048), BF16)]
        + [shape((2, 4, 4, 4, n, 16, 128), BF16) for n in SIZES],
        in_specs=[HBM] * 4,
        out_specs=[HBM] * 7,
        scratch_shapes=scratch
        + [
            pltpu.SemaphoreType.DMA((200,)),
            pltpu.SemaphoreType.DMA((200,)),
            pltpu.SemaphoreType.DMA((17,)),
        ],
        compiler_params=pltpu.CompilerParams(
            collective_id=1, has_side_effects=True, vmem_limit_bytes=60 * 2**20
        ),
    )(hidden, dqp, dkp, dvp)


def widen_kernel(*refs):
    parts, (wk, wv), held, (wk_v, wv_v), (in_sems, out_sems) = (
        refs[0:6], refs[6:8], refs[8:14], refs[14:16], refs[16:18]
    )

    def at(p, x, y, z):
        places = {"x": x, "y": y, "z": z}
        return tuple(places[axis] for axis in ORDERS[p % 3])

    def loads(i):
        x, y = lax.div(i, 4), lax.rem(i, 4)
        spots = [(slice(None),) + at(p, x, y, slice(None)) for p in range(6)]
        return [
            pltpu.make_async_copy(parts[p].at[spot], held[p].at[spot], in_sems.at[p, i])
            for p, spot in enumerate(spots)
        ]

    def stores(i):
        rows = pl.ds(pl.multiple_of(i * 256, 256), 256)
        return [
            pltpu.make_async_copy(src.at[rows], dst.at[rows], out_sems.at[n, i])
            for n, (src, dst) in enumerate(((wk_v, wk), (wv_v, wv)))
        ]

    def begin(i, _):
        for copy in loads(i):
            copy.start()
        return 0

    def block(i, _):
        x, y = lax.div(i, 4), lax.rem(i, 4)
        for copy in loads(i):
            copy.wait()
        for z in range(4):
            r0 = pl.multiple_of(i * 256 + z * 64, 64)
            for core in range(2):
                for p in range(6):
                    out = wk_v if p < 3 else wv_v
                    for u, (row, column) in enumerate(PARTS[p // 3][p % 3]):
                        value = held[p][(core,) + at(p, x, y, z) + (u,)]
                        c0 = core * 256 + column * 128
                        out[pl.ds(r0 + row * 16, 16), c0 : c0 + 128] = value.astype(F32)
        for copy in stores(i):
            copy.start()
        return 0

    def end(i, _):
        for copy in stores(i):
            copy.wait()
        return 0

    lax.fori_loop(0, 16, begin, 0)
    lax.fori_loop(0, 16, block, 0)
    lax.fori_loop(0, 16, end, 0)


def widen(*parts):
    shape = jax.ShapeDtypeStruct
    return pl.pallas_call(
        widen_kernel,
        out_shape=[shape((4096, 512), F32)] * 2,
        in_specs=[HBM] * 6,
        out_specs=[HBM] * 2,
        scratch_shapes=[pltpu.VMEM((2, 4, 4, 4, n, 16, 128), BF16) for n in SIZES]
        + [
            pltpu.VMEM((4096, 512), F32),
            pltpu.VMEM((4096, 512), F32),
            pltpu.SemaphoreType.DMA((6, 16)),
            pltpu.SemaphoreType.DMA((2, 16)),
        ],
        compiler_params=pltpu.CompilerParams(vmem_limit_bytes=60 * 2**20),
    )(*parts)


def local(hidden, q, k, v, ao, do, lse, pos):
    qg, dog, kg, vg, sg, pq, pk = gather_all(q, do, k, v, ao, lse.T, pos[None, :])
    dqp, dkp, dvp = attend(pq, pk, qg, dog, kg, vg, sg)
    dq, *parts = reduce_all(hidden, dqp, dkp, dvp)
    wk, wv = widen(*parts)
    return dq, wk, wv


def solution(mesh):
    rows = P(("inner", "outer"), None)
    return jax.shard_map(
        local,
        mesh=mesh,
        in_specs=(rows,) * 7 + (P(("inner", "outer")),),
        out_specs=(rows, P(), P()),
        check_vma=False,
    )
```
